256 devices in a mesh: gx: 8 (over y, x_lo), gy: 16 (over z, core), col: 2 (over x_hi).
Axes of the slice: x: 4 (x_hi: 2, x_lo: 2; x = x_hi * 2 + x_lo), y: 4, z: 8, core: 2. Of those that a mesh axis runs over, the one named last changes fastest.
Arguments:
- start_block: bfloat16 [2, 8, 64, 128, 256], P(None, 'gx', 'gy', None, 'col'), may hold values from -6 to 6
- hamiltonian: bfloat16 [2, 8, 64, 9, 128, 128], P(None, 'gx', 'gy'), as said below
- neighbour_index: int32 [8, 64, 9], P('gx', 'gy'), may hold values from 0 to 8, as said below
- block_count: int32 [8, 64], P('gx', 'gy'), may hold values from 1 to 9, as said below
Outputs:
- ritz_block: bfloat16 [2, 8, 64, 128, 256], P(None, 'gx', 'gy', None, 'col')
- projected: float32 [2, 256, 256], P(None, None, 'col')
The draws below stay inside these ranges and needn't reach their ends.
Inputs may be any that keep to these rules, and one draw needn't show every extreme that they name: `neighbour_index`: slot 0 of every tile holds code 4 (the tile itself); a tile's 9 codes are distinct; the live codes of a tile stand in its first block_count slots; a bond is live on both of its sides or on neither. `block_count`: some tile has all 9 slots live. `hamiltonian`: the block of a tile toward code c equals the transpose of the block of that neighbour tile toward code 8 - c; the block toward code 4 is symmetric.
All inputs are finite; a program needn't handle non-finite values.
Results may differ from the reference program's by a relative error of at most 0.0067.
Values may be sent and summed in bfloat16 or wider, within the bound.
No kernel may reach another device: no remote copies, remote signals or barrier semaphores. Data moves between devices by JAX's collectives and lax.ppermute only.
A program may use at most 64 MiB of HBM per device.

```python
import jax
import jax.numpy as jnp
from jax import lax

TILE = 128
NB = 9
K = 256
TXG = 8
TYG = 64
ROWS = 65536


def bond_layout(key):
    key_live, key_px, key_py, key_order = jax.random.split(key, 4)
    grid_x = jnp.arange(TXG, dtype=jnp.int32)[:, None]
    grid_y = jnp.arange(TYG, dtype=jnp.int32)[None, :]
    pick_x = jax.random.randint(key_px, (), 0, TXG)
    pick_y = jax.random.randint(key_py, (), 0, TYG)
    coins = jax.random.randint(key_live, (TXG, TYG, 4), 0, 10) < 7
    halves = []
    for code in range(4):
        shift_x = code // 3 - 1
        shift_y = code % 3 - 1
        chosen = (grid_x == pick_x) & (grid_y == pick_y)
        partner = ((grid_x + shift_x) % TXG == pick_x) & ((grid_y + shift_y) % TYG == pick_y)
        halves.append(coins[:, :, code] | chosen | partner)
    columns = list(halves)
    columns.append(jnp.ones((TXG, TYG), dtype=bool))
    for code in range(5, 9):
        shift_x = code // 3 - 1
        shift_y = code % 3 - 1
        columns.append(jnp.roll(halves[8 - code], (-shift_x, -shift_y), axis=(0, 1)))
    live = jnp.stack(columns, axis=-1)
    codes = jnp.arange(9, dtype=jnp.int32)
    noise = jax.random.randint(key_order, (TXG, TYG, 9), 0, 1 << 20)
    scores = noise * 16 + codes + jnp.where(live, 0, 1 << 25).astype(jnp.int32)
    scores = jnp.where(codes == 4, -1, scores)
    order = jnp.argsort(scores, axis=-1).astype(jnp.int32)
    count = jnp.sum(live.astype(jnp.int32), axis=-1).astype(jnp.int32)
    return (order, count)


def draw_neighbour_index(key, part):
    order, count = bond_layout(key)
    return order


def draw_block_count(key, part):
    order, count = bond_layout(key)
    return count


def draw_hamiltonian(key, part):
    order, count = bond_layout(key)
    key = jax.random.fold_in(key, 13)
    scale = (TILE * NB) ** (-0.5)
    raw = jax.random.normal(key, (2, TXG, TYG, 5, TILE, TILE), jnp.float32) * scale
    blocks = [raw[:, :, :, code].astype(jnp.bfloat16) for code in range(4)]
    selfish = raw[:, :, :, 4]
    blocks.append(((selfish + jnp.swapaxes(selfish, -1, -2)) * 0.7071067811865476).astype(jnp.bfloat16))
    for code in range(5, 9):
        shift_x = code // 3 - 1
        shift_y = code % 3 - 1
        mirror = jnp.swapaxes(raw[:, :, :, 8 - code], -1, -2).astype(jnp.bfloat16)
        blocks.append(jnp.roll(mirror, (-shift_x, -shift_y), axis=(1, 2)))
    stacked = jnp.stack(blocks, axis=3)
    return jnp.take_along_axis(stacked, order[None, :, :, :, None, None], axis=3)


def steps_of(own_key, shape, cuts, smallest, top_value):
    factor_of, own = 1.0, jax.random.fold_in(own_key, 6)
    for axis_at, parts in cuts:
        heights = jnp.exp(jax.random.uniform(jax.random.fold_in(own, axis_at), (parts,), jnp.float32, smallest / len(cuts), top_value / len(cuts)))
        factor_of = factor_of * jnp.repeat(heights, shape[axis_at] // parts).reshape([-1 if axis == axis_at else 1 for axis in range(len(shape))])
    return factor_of


def scatter_about(key, extent, width, reach, pieces=(), kind=jnp.bfloat16):
    drawn = width * jax.random.normal(key, extent, jnp.float32)
    if pieces:
        drawn = drawn * steps_of(key, extent, pieces, -0.22, 0.18)
    return jnp.clip(drawn, -reach, reach).astype(kind)


def setup_inputs(seed: int = 0) -> dict:
    arg_keys = jax.random.split(jax.random.key(seed), 5)
    start_block = scatter_about(arg_keys[0], (2, TXG, TYG, TILE, K), 1.0, 6.0, ((1, 8), (2, 16), (4, 2)))
    hamiltonian = draw_hamiltonian(jax.random.fold_in(arg_keys[4], 71), 0)
    neighbour_index = draw_neighbour_index(jax.random.fold_in(arg_keys[4], 71), 0)
    block_count = draw_block_count(jax.random.fold_in(arg_keys[4], 71), 0)
    return {"start_block": start_block, "hamiltonian": hamiltonian, "neighbour_index": neighbour_index, "block_count": block_count}


def apply_ham(hamiltonian, vectors, neighbour_index, block_count):
    total = jnp.zeros(vectors.shape, jnp.float32)
    base_x = jnp.arange(TXG, dtype=jnp.int32)[:, None]
    base_y = jnp.arange(TYG, dtype=jnp.int32)[None, :]
    for slot_index in range(NB):
        offset_code = neighbour_index[:, :, slot_index]
        index_x = (base_x + offset_code // 3 - 1) % TXG
        index_y = (base_y + offset_code % 3 - 1) % TYG
        beside = vectors[:, index_x, index_y]
        live = (slot_index < block_count)[None, :, :, None, None]
        beside = jnp.where(live, beside, jnp.zeros_like(beside))
        total = total + jnp.einsum('sxyij,sxyjk->sxyik', hamiltonian[:, :, :, slot_index].astype(jnp.float32), beside.astype(jnp.float32))
    return total

def reference(start_block, hamiltonian, neighbour_index, block_count):
    first = (0.5 * apply_ham(hamiltonian, start_block, neighbour_index, block_count)).astype(jnp.bfloat16)
    second = (apply_ham(hamiltonian, first, neighbour_index, block_count) - start_block.astype(jnp.float32)).astype(jnp.bfloat16)
    image = apply_ham(hamiltonian, second, neighbour_index, block_count).astype(jnp.bfloat16)
    second_f = second.astype(jnp.float32)
    correlation = jnp.einsum('sxytp,sxytq->spq', second_f, second_f) / ROWS
    coupling = jnp.einsum('sxytp,sxytq->spq', second_f, image.astype(jnp.float32)) / ROWS
    lower = jnp.linalg.cholesky(correlation)
    eye = jnp.broadcast_to(jnp.eye(K, dtype=jnp.float32), lower.shape)
    inverse = lax.linalg.triangular_solve(lower, eye, left_side=True, lower=True)
    rotation = jnp.swapaxes(inverse, 1, 2).astype(jnp.bfloat16)
    ritz_block = jnp.einsum('sxytp,spq->sxytq', second_f, rotation.astype(jnp.float32)).astype(jnp.bfloat16)
    half = jnp.einsum('sij,sjk->sik', inverse, coupling, precision=lax.Precision.HIGHEST)
    projected = jnp.einsum('sij,skj->sik', half, inverse, precision=lax.Precision.HIGHEST)
    return (ritz_block, projected)
```

```python
import jax
import jax.numpy as jnp
from jax import lax
from jax.sharding import PartitionSpec as P

NB = 9


def extended_2(block, sides, width):
    for axis, dim in sides:
        count = lax.axis_size(axis)
        forward = [(i, i + 1) for i in range(count - 1)]
        forward.append((count - 1, 0))
        backward = [(target, source) for source, target in forward]
        low = lax.ppermute(
            lax.slice_in_dim(block, block.shape[dim] - width, None, axis=dim), axis, forward
        )
        high = lax.ppermute(lax.slice_in_dim(block, 0, width, axis=dim), axis, backward)
        block = jnp.concatenate([low, block, high], axis=dim)
    return block


def offset_blocks(hamiltonian, neighbour_index, block_count):
    codes = jnp.arange(9, dtype=jnp.int32)
    slots = jnp.arange(NB, dtype=jnp.int32)
    selector = (neighbour_index[:, :, :, None] == codes) & (
        slots[None, None, :, None] < block_count[:, :, None, None]
    )
    return jnp.einsum(
        "xyjc,sxyjab->sxycab",
        selector.astype(jnp.bfloat16),
        hamiltonian,
        preferred_element_type=jnp.float32,
    ).astype(jnp.bfloat16)


def apply_ham(ordered, vectors):
    extended = extended_2(vectors, (("gx", 1), ("gy", 2)), 1)
    tiles_x = vectors.shape[1]
    tiles_y = vectors.shape[2]
    total = jnp.zeros(vectors.shape, jnp.float32)
    for code in range(9):
        beside = extended[:, code // 3 : code // 3 + tiles_x, code % 3 : code % 3 + tiles_y]
        total = total + jnp.einsum(
            "sxyij,sxyjk->sxyik", ordered[:, :, :, code], beside, preferred_element_type=jnp.float32
        )
    return total


def factor_parts(correlation, coupling):
    lower = jnp.linalg.cholesky(correlation)
    eye = jnp.broadcast_to(jnp.eye(correlation.shape[1], dtype=jnp.float32), lower.shape)
    inverse = lax.linalg.triangular_solve(lower, eye, left_side=True, lower=True)
    rotation = jnp.swapaxes(inverse, 1, 2).astype(jnp.bfloat16)
    half = jnp.einsum("sij,sjk->sik", inverse, coupling, precision=lax.Precision.HIGHEST)
    projected_full = jnp.einsum("sij,skj->sik", half, inverse, precision=lax.Precision.HIGHEST)
    return (rotation, projected_full)


def per_device(start_block, hamiltonian, neighbour_index, block_count):
    ordered = offset_blocks(hamiltonian, neighbour_index, block_count)
    first = (0.5 * apply_ham(ordered, start_block)).astype(jnp.bfloat16)
    second = (apply_ham(ordered, first) - start_block.astype(jnp.float32)).astype(jnp.bfloat16)
    image = apply_ham(ordered, second).astype(jnp.bfloat16)
    width_local = second.shape[4]
    owners = lax.axis_size("col")
    width_all = width_local * owners
    total_rows = (
        second.shape[1]
        * second.shape[2]
        * second.shape[3]
        * lax.axis_size("gx")
        * lax.axis_size("gy")
    )
    column_owner = lax.axis_index("col")
    every_column = lax.all_gather(second, "col", axis=4, tiled=True)
    paired = jnp.concatenate([second, image], axis=4)
    partial_gram = jnp.einsum(
        "sxytp,sxytq->spq", every_column, paired, preferred_element_type=jnp.float32
    )
    group = ("gx", "gy")
    members = lax.axis_size("gx") * lax.axis_size("gy")
    pieces = partial_gram.reshape(members, -1)
    mine = lax.all_to_all(pieces, group, 0, 0, tiled=True).sum(axis=0) / total_rows
    spread = jnp.broadcast_to(mine[None], pieces.shape)
    summed = lax.all_to_all(spread, group, 0, 0, tiled=True).reshape(partial_gram.shape)
    gathered = lax.all_gather(summed, "col", axis=2, tiled=True)
    gathered = gathered.reshape(2, width_all, owners, 2, width_local)
    correlation = gathered[:, :, :, 0, :].reshape(2, width_all, width_all)
    coupling = gathered[:, :, :, 1, :].reshape(2, width_all, width_all)
    rotation, projected_full = factor_parts(correlation, coupling)
    rotation_mine = lax.dynamic_slice_in_dim(rotation, column_owner * width_local, width_local, 2)
    ritz_block = jnp.einsum(
        "sxytp,spq->sxytq", every_column, rotation_mine, preferred_element_type=jnp.float32
    ).astype(jnp.bfloat16)
    projected = lax.dynamic_slice_in_dim(projected_full, column_owner * width_local, width_local, 2)
    return (ritz_block, projected)


def solution(mesh):
    return jax.shard_map(
        per_device,
        mesh=mesh,
        in_specs=(
            P(None, "gx", "gy", None, "col"),
            P(None, "gx", "gy", None, None, None),
            P("gx", "gy", None),
            P("gx", "gy"),
        ),
        out_specs=(P(None, "gx", "gy", None, "col"), P(None, None, "col")),
        check_vma=False,
    )
```

```python
import functools

import jax
import jax.numpy as jnp
from jax import lax
from jax.experimental import pallas as pl
from jax.experimental.pallas import tpu as pltpu
from jax.sharding import PartitionSpec as P

NB = 9
T = 128
AXES = ("gx", "gy", "col")
BF = jnp.bfloat16
F32 = jnp.float32
SPIN, COL, PAR_Y, PAR_X = 36, 37, 38, 39


def col_of(gx, spin):
    return spin ^ ((gx >> 1) & 1)


def device(sizes, gx, gy, col):
    return ((gx % sizes[0]) * sizes[1] + gy % sizes[1]) * sizes[2] + col


def pairs(sizes, target):
    out = []
    for gx in range(sizes[0]):
        for gy in range(sizes[1]):
            for spin in range(2):
                there = target(gx, gy)
                there_gx = there[0] % sizes[0]
                out.append(
                    (
                        device(sizes, gx, gy, col_of(gx, spin)),
                        device(sizes, there_gx, there[1], col_of(there_gx, spin)),
                    )
                )
    return out


def partner(index, kind):
    if kind == 0:
        return index
    return index + 1 if (index % 2 == 0) == (kind == 1) else index - 1


def swap(sizes, block, kind_x, kind_y):
    perm = pairs(sizes, lambda gx, gy: (partner(gx, kind_x), partner(gy, kind_y)))
    return lax.ppermute(block, AXES, perm)


def shift(sizes, block, dx, dy):
    return lax.ppermute(block, AXES, pairs(sizes, lambda gx, gy: (gx + dx, gy + dy)))


def swap_col(sizes, block):
    perm = [(d, d ^ 1) for d in range(sizes[0] * sizes[1] * 2)]
    return lax.ppermute(block, AXES, perm)


def exchange(sizes, pieces):
    groups = [
        [device(sizes, gx, gy, col_of(gx, spin)) for gx in range(sizes[0]) for gy in range(sizes[1])]
        for spin in range(2)
    ]
    return lax.all_to_all(pieces, AXES, 0, 0, axis_index_groups=groups, tiled=True)


def dot(a, b, dims=((1,), (0,))):
    return lax.dot_general(a, b, (dims, ((), ())), preferred_element_type=F32)


def split(a):
    high = a.astype(BF)
    return high, (a - high.astype(F32)).astype(BF)


def dot3(a, b, dims=((1,), (0,))):
    (ah, al), (bh, bl) = split(a), split(b)
    return dot(ah, bh, dims) + (dot(ah, bl, dims) + dot(al, bh, dims))


def h_block(m, h, tile, side, dy):
    slot = m[(tile * 3 + side) * 3 + dy]
    block = h[0, 0, tile, jnp.maximum(slot, 0)]
    return jnp.where(slot >= 0, block, jnp.zeros_like(block))


def h_row(m, h, tile, side, dys):
    return jnp.concatenate([h_block(m, h, tile, side, dy) for dy in dys], axis=1)


def fill(m, ext, middle, p, q):
    par = m[PAR_Y]
    ext[1:5] = middle
    ext[pl.ds(jnp.where(par == 0, 5, 0), 1)] = p
    ext[pl.ds(jnp.where(par == 0, 0, 5), 1)] = q


def store_sides(m, ref, p_ref, q_ref):
    par = m[PAR_Y]
    p_ref[...] = ref[pl.ds(jnp.where(par == 0, 3, 0), 1)]
    q_ref[...] = ref[pl.ds(jnp.where(par == 0, 0, 3), 1)]


def join_kernel(m, start, other, v, p, q):
    own = start[pl.ds(m[SPIN], 1)][0, 0]
    first_col = m[COL] == 0
    v[:, :, :T] = jnp.where(first_col, own, other[...])
    v[:, :, T:] = jnp.where(first_col, other[...], own)
    store_sides(m, v, p, q)


def own_kernel(m, h, v, p, q, acc, ext):
    fill(m, ext, v[...], p[...], q[...])
    for tile in range(4):
        row = h_row(m, h, tile, 0, range(3))
        acc[tile] = dot(row, ext[tile : tile + 3].reshape(3 * T, 2 * T))


def side_kernel(m, h, a, b, ca, cb, acc, *rest, last):
    if last:
        v, out, low, high, ext_a, ext_b = rest
    else:
        out, p, q, ext_a, ext_b = rest
    fill(m, ext_a, a[...], ca[0:1], ca[1:2])
    fill(m, ext_b, b[...], cb[0:1], cb[1:2])
    for tile in range(4):
        total = acc[tile]
        for side, ext in ((1, ext_a), (2, ext_b)):
            row = h_row(m, h, tile, side, range(3))
            total += dot(row, ext[tile : tile + 3].reshape(3 * T, 2 * T))
        if last:
            out[tile] = (total - v[tile].astype(F32)).astype(BF)
        else:
            out[tile] = (0.5 * total).astype(BF)
    if last:
        low[...] = out[0:1]
        high[...] = out[3:4]
    else:
        store_sides(m, out, p, q)


def inner_kernel(m, h, s, corr, acc):
    flat = s[...].reshape(4 * T, 2 * T)
    corr[...] = dot(flat, flat, ((0,), (0,)))
    for tile in range(4):
        total = 0.5 * dot(h_block(m, h, tile, 0, 1), s[tile])
        if tile < 3:
            total += dot(h_block(m, h, tile, 0, 2), s[tile + 1])
        acc[tile] = total


def places():
    shape = (2 * T, 2 * T)
    return lax.broadcasted_iota(jnp.int32, shape, 0), lax.broadcasted_iota(jnp.int32, shape, 1)


def gram_kernel(m, h, s, above, right, right_low, right_high, acc, corr, out, ext):
    ext[0:1] = right_low[...]
    ext[1:5] = right[...]
    ext[5:6] = right_high[...]
    side = 1 + m[PAR_X]
    half = jnp.zeros((2 * T, 2 * T), F32)
    for tile in range(4):
        total = acc[tile]
        if tile == 3:
            total += dot(h_block(m, h, tile, 0, 2), above[0])
        row = h_row(m, h, tile, side, range(3))
        total += dot(row, ext[tile : tile + 3].reshape(3 * T, 2 * T))
        high, low = split(total)
        half += dot(s[tile], high, ((0,), (0,))) + dot(s[tile], low, ((0,), (0,)))
    coupling = half + half.T
    rows, cols = places()
    both = jnp.where(rows >= cols, corr[...], coupling)
    diagonal = jnp.sum(jnp.where(rows == cols, coupling, 0.0), axis=1, keepdims=True)
    lane = lax.broadcasted_iota(jnp.int32, (T, T), 1)
    extra = jnp.where(lane == 0, diagonal[:T], jnp.where(lane == 1, diagonal[T:], 0.0))
    out[:, 0, :] = jnp.concatenate([both[:T], both[T:], extra], axis=1)


def lower_part(e, rows, cols):
    return jnp.where(rows > cols, e, jnp.where(rows == cols, 0.5 * e, 0.0))


def final_kernel(m, packed, s, keep, send, p_keep, p_send, x_ref, a_ref):
    rows, cols = places()
    table = packed[:, 0, :]
    both = jnp.concatenate([table[:, : 2 * T], table[:, 2 * T : 4 * T]], axis=0)
    diagonal = jnp.concatenate([table[:, 4 * T : 4 * T + 1], table[:, 4 * T + 1 : 4 * T + 2]], axis=0)
    turned = both.T
    corr = jnp.where(rows >= cols, both, turned)
    coupling = jnp.where(rows < cols, both, jnp.where(rows == cols, diagonal, turned))
    on_diagonal = jnp.where(rows == cols, corr, 0.0)
    scale_row = 1.0 / jnp.sqrt(jnp.sum(on_diagonal, axis=0, keepdims=True))
    scale_col = 1.0 / jnp.sqrt(jnp.sum(on_diagonal, axis=1, keepdims=True))
    scaled = corr * scale_row * scale_col
    unit = (rows == cols).astype(F32)

    a_ref[...] = scaled
    x_ref[...] = unit - lower_part(scaled - unit, rows, cols)

    def step(state):
        count, _ = state
        x = x_ref[...]
        e = dot3(dot3(x, a_ref[...]), x, ((1,), (1,))) - unit
        x_ref[...] = x - dot3(lower_part(e, rows, cols), x)
        return count + 1, jnp.sum(e * e)

    def more(state):
        count, size = state
        return (count < 12) & (size >= 4e-6) & (size < 1e4)

    _, size = lax.while_loop(more, step, (0, F32(1.0)))

    @pl.when(jnp.logical_not(size < 4e-6))
    def _():
        a_ref[...] = scaled
        x_ref[...] = unit

        def eliminate(j, carry):
            row = a_ref[pl.ds(j, 1), :]
            pivot = jnp.sum(jnp.where(cols[:1] == j, row, 0.0), axis=1, keepdims=True)
            a = a_ref[...]
            column = jnp.sum(jnp.where(cols == j, a, 0.0), axis=1, keepdims=True)
            factor = jnp.where(rows[:, :1] > j, column / pivot, 0.0)
            x = x_ref[...]
            x_row = x_ref[pl.ds(j, 1), :]
            a_ref[...] = a - factor * row
            x_ref[...] = x - factor * x_row
            return carry

        lax.fori_loop(0, 2 * T, eliminate, 0)
        pivots = jnp.sum(jnp.where(rows == cols, a_ref[...], 0.0), axis=1, keepdims=True)
        x_ref[...] = x_ref[...] / jnp.sqrt(pivots)

    x = x_ref[...] * scale_row
    rotation = x.astype(BF)
    ritz = dot(s[...].reshape(4 * T, 2 * T), rotation, ((1,), (1,))).astype(BF)
    ritz = ritz.reshape(4, T, 2 * T)
    projected = dot3(dot3(x, coupling), x, ((1,), (1,)))
    first_col = m[COL] == 0
    keep[...] = jnp.where(first_col, ritz[:, :, :T], ritz[:, :, T:])
    send[...] = jnp.where(first_col, ritz[:, :, T:], ritz[:, :, :T])
    p_keep[...] = jnp.where(first_col, projected[:, :T], projected[:, T:])
    p_send[...] = jnp.where(first_col, projected[:, T:], projected[:, :T])


def whole(shape):
    return pl.BlockSpec(shape, lambda i, m, n=len(shape): (0,) * n)


def call(kernel, m, arrays, outs, scratch=(), with_h=None, flops=0, name=None):
    specs = [whole(a.shape) for a in arrays]
    if with_h is not None:
        shape = (1,) + with_h.shape[1:]
        specs.insert(0, pl.BlockSpec(shape, lambda i, m: (m[SPIN], 0, 0, 0, 0, 0)))
        arrays = [with_h, *arrays]
    moved = sum(a.size * a.dtype.itemsize for a in arrays) + sum(o.size * o.dtype.itemsize for o in outs)
    return pl.pallas_call(
        kernel,
        out_shape=outs,
        grid_spec=pltpu.PrefetchScalarGridSpec(
            num_scalar_prefetch=1,
            grid=(1,),
            in_specs=specs,
            out_specs=[whole(o.shape) for o in outs],
            scratch_shapes=list(scratch),
        ),
        compiler_params=pltpu.CompilerParams(vmem_limit_bytes=32 * 1024 * 1024),
        cost_estimate=pl.CostEstimate(flops=flops, bytes_accessed=moved, transcendentals=0),
        name=name,
    )(m, *arrays)


def table(neighbour_index, block_count):
    gx, gy, col = (lax.axis_index(a) for a in AXES)
    spin = col ^ ((gx >> 1) & 1)
    toward = jnp.where(gx % 2 == 0, 1, -1)
    dx = jnp.stack([jnp.zeros_like(toward), toward, -toward])
    codes = (dx[:, None] + 1) * 3 + jnp.arange(3, dtype=jnp.int32)[None, :]
    slots = jnp.arange(NB, dtype=jnp.int32)
    index, count = neighbour_index[0], block_count[0]
    match = (index[:, None, None, :] == codes[None, :, :, None]) & (
        slots < count[:, None, None, None]
    )
    found = jnp.sum(jnp.where(match, slots + 1, 0), axis=-1) - 1
    scalars = jnp.stack([spin, col, gy % 2, gx % 2])
    return spin, col, jnp.concatenate([found.reshape(-1), scalars]).astype(jnp.int32)


def shaped(shape, dtype):
    return jax.ShapeDtypeStruct(shape, dtype)


def per_device(start_block, hamiltonian, neighbour_index, block_count):
    sizes = tuple(lax.axis_size(a) for a in AXES)
    members = sizes[0] * sizes[1]
    block, tile, full = (4, T, 2 * T), (1, T, 2 * T), (2 * T, 2 * T)
    ext = pltpu.VMEM((6, T, 2 * T), BF)
    spin, col, m = table(neighbour_index, block_count)

    other = swap_col(sizes, lax.dynamic_index_in_dim(start_block, 1 - spin, 0, keepdims=False)[0])
    v, p, q = call(
        join_kernel, m, [start_block, other],
        [shaped(block, BF), shaped(tile, BF), shaped(tile, BF)], name="join",
    )

    def apply_ham(x, p, q, before):
        p, q = swap(sizes, p, 0, 1), swap(sizes, q, 0, 2)
        a, b = swap(sizes, x, 1, 0), swap(sizes, x, 2, 0)
        ends = jnp.concatenate([p, q], axis=0)
        ca, cb = swap(sizes, ends, 1, 0), swap(sizes, ends, 2, 0)
        (acc,) = call(
            own_kernel, m, [x, p, q], [shaped(block, F32)], [ext], hamiltonian,
            2 * 12 * T * T * 2 * T, "own",
        )
        last = before is not None
        arrays = [a, b, ca, cb, acc] + ([before] if last else [])
        return call(
            functools.partial(side_kernel, last=last), m, arrays,
            [shaped(block, BF), shaped(tile, BF), shaped(tile, BF)], [ext, ext], hamiltonian,
            2 * 24 * T * T * 2 * T, "sides",
        )

    first, p, q = apply_ham(v, p, q, None)
    second, low, high = apply_ham(first, p, q, v)

    above = shift(sizes, low, 0, -1)
    right_high = shift(sizes, low, -1, -1)
    right_low = shift(sizes, high, -1, 1)
    right = shift(sizes, second, -1, 0)
    corr, acc = call(
        inner_kernel, m, [second], [shaped(full, F32), shaped(block, F32)], (), hamiltonian,
        2 * 15 * T * T * 2 * T, "inner",
    )
    (packed,) = call(
        gram_kernel, m, [second, above, right, right_low, right_high, acc, corr],
        [shaped((members, 1, 5 * T), F32)], [ext], hamiltonian, 2 * 21 * T * T * 2 * T, "gram",
    )

    rows = members * second.shape[0] * second.shape[1]
    mine = exchange(sizes, packed).sum(axis=0, keepdims=True) / rows
    spread = jnp.broadcast_to(mine, packed.shape)
    gathered = exchange(sizes, spread)

    half = (4, T, T)
    keep, send, p_keep, p_send = call(
        final_kernel, m, [gathered, second],
        [shaped(half, BF), shaped(half, BF), shaped((2 * T, T), F32), shaped((2 * T, T), F32)],
        [pltpu.VMEM(full, F32), pltpu.VMEM(full, F32)], None, 0, "final",
    )
    got, p_got = swap_col(sizes, send), swap_col(sizes, p_send)
    ritz = jnp.where(spin == 0, jnp.stack([keep, got]), jnp.stack([got, keep]))
    projected = jnp.where(spin == 0, jnp.stack([p_keep, p_got]), jnp.stack([p_got, p_keep]))
    return ritz[:, None], projected


def solution(mesh):
    return jax.shard_map(
        per_device,
        mesh=mesh,
        in_specs=(
            P(None, "gx", "gy", None, "col"),
            P(None, "gx", "gy", None, None, None),
            P("gx", "gy", None),
            P("gx", "gy"),
        ),
        out_specs=(P(None, "gx", "gy", None, "col"), P(None, None, "col")),
        check_vma=False,
    )
```

```python
import functools

import jax
import jax.numpy as jnp
from jax import lax
from jax.experimental import pallas as pl
from jax.experimental.pallas import tpu as pltpu
from jax.sharding import PartitionSpec as P

NB = 9
T = 128
AXES = ("gx", "gy", "col")
BF = jnp.bfloat16
F32 = jnp.float32
SPIN, COL, PAR_Y, PAR_X = 36, 37, 38, 39


def col_of(gx, spin):
    return spin ^ ((gx >> 1) & 1)


def device(sizes, gx, gy, col):
    return ((gx % sizes[0]) * sizes[1] + gy % sizes[1]) * sizes[2] + col


def pairs(sizes, target):
    out = []
    for gx in range(sizes[0]):
        for gy in range(sizes[1]):
            for spin in range(2):
                there = target(gx, gy)
                there_gx = there[0] % sizes[0]
                out.append(
                    (
                        device(sizes, gx, gy, col_of(gx, spin)),
                        device(sizes, there_gx, there[1], col_of(there_gx, spin)),
                    )
                )
    return out


def partner(index, kind):
    if kind == 0:
        return index
    return index + 1 if (index % 2 == 0) == (kind == 1) else index - 1


def swap(sizes, block, kind_x, kind_y):
    perm = pairs(sizes, lambda gx, gy: (partner(gx, kind_x), partner(gy, kind_y)))
    return lax.ppermute(block, AXES, perm)


def shift(sizes, block, dx, dy):
    return lax.ppermute(block, AXES, pairs(sizes, lambda gx, gy: (gx + dx, gy + dy)))


def swap_col(sizes, block):
    perm = [(d, d ^ 1) for d in range(sizes[0] * sizes[1] * 2)]
    return lax.ppermute(block, AXES, perm)


def exchange(sizes, pieces):
    groups = [
        [
            device(sizes, gx, gy, col_of(gx, spin))
            for gx in range(sizes[0])
            for gy in range(core, sizes[1], 2)
        ]
        for spin in range(2)
        for core in range(2)
    ]
    return lax.all_to_all(pieces, AXES, 0, 0, axis_index_groups=groups, tiled=True)


def dot(a, b, dims=((1,), (0,))):
    return lax.dot_general(a, b, (dims, ((), ())), preferred_element_type=F32)


def split(a):
    high = a.astype(BF)
    return high, (a - high.astype(F32)).astype(BF)


def dot3(a, b, dims=((1,), (0,))):
    (ah, al), (bh, bl) = split(a), split(b)
    return dot(ah, bh, dims) + (dot(ah, bl, dims) + dot(al, bh, dims))


def h_block(m, h, tile, side, dy):
    slot = m[(tile * 3 + side) * 3 + dy]
    block = h[0, 0, tile, jnp.maximum(slot, 0)]
    return jnp.where(slot >= 0, block, jnp.zeros_like(block))


def h_row(m, h, tile, side, dys):
    return jnp.concatenate([h_block(m, h, tile, side, dy) for dy in dys], axis=1)


def fill(m, ext, middle, p, q):
    par = m[PAR_Y]
    ext[1:5] = middle
    ext[pl.ds(jnp.where(par == 0, 5, 0), 1)] = p
    ext[pl.ds(jnp.where(par == 0, 0, 5), 1)] = q


def store_sides(m, ref, p_ref, q_ref):
    par = m[PAR_Y]
    p_ref[...] = ref[pl.ds(jnp.where(par == 0, 3, 0), 1)]
    q_ref[...] = ref[pl.ds(jnp.where(par == 0, 0, 3), 1)]


def join_kernel(m, own, other, v, p, q):
    first_col = m[COL] == 0
    v[:, :, :T] = jnp.where(first_col, own[...], other[...])
    v[:, :, T:] = jnp.where(first_col, other[...], own[...])
    store_sides(m, v, p, q)


def own_kernel(m, h, v, p, q, acc, ext):
    fill(m, ext, v[...], p[...], q[...])
    for tile in range(4):
        row = h_row(m, h, tile, 0, range(3))
        acc[tile] = dot(row, ext[tile : tile + 3].reshape(3 * T, 2 * T))


def side_kernel(m, h, a, b, ca, cb, acc, *rest, last):
    if last:
        v, out, low, high, ext_a, ext_b = rest
    else:
        out, p, q, ext_a, ext_b = rest
    fill(m, ext_a, a[...], ca[0:1], ca[1:2])
    fill(m, ext_b, b[...], cb[0:1], cb[1:2])
    for tile in range(4):
        total = acc[tile]
        for side, ext in ((1, ext_a), (2, ext_b)):
            row = h_row(m, h, tile, side, range(3))
            total += dot(row, ext[tile : tile + 3].reshape(3 * T, 2 * T))
        if last:
            out[tile] = (total - v[tile].astype(F32)).astype(BF)
        else:
            out[tile] = (0.5 * total).astype(BF)
    if last:
        low[...] = out[0:1]
        high[...] = out[3:4]
    else:
        store_sides(m, out, p, q)


def inner_kernel(m, h, s, corr, acc):
    flat = s[...].reshape(4 * T, 2 * T)
    corr[...] = dot(flat, flat, ((0,), (0,)))
    for tile in range(4):
        total = 0.5 * dot(h_block(m, h, tile, 0, 1), s[tile])
        if tile < 3:
            total += dot(h_block(m, h, tile, 0, 2), s[tile + 1])
        acc[tile] = total


def places():
    shape = (2 * T, 2 * T)
    return lax.broadcasted_iota(jnp.int32, shape, 0), lax.broadcasted_iota(jnp.int32, shape, 1)


def gram_kernel(m, h, s, above, right, right_low, right_high, acc, corr, mine, theirs, ext):
    ext[0:1] = right_low[...]
    ext[1:5] = right[...]
    ext[5:6] = right_high[...]
    side = 1 + m[PAR_X]
    half = jnp.zeros((2 * T, 2 * T), F32)
    for tile in range(4):
        total = acc[tile]
        if tile == 3:
            total += dot(h_block(m, h, tile, 0, 2), above[0])
        row = h_row(m, h, tile, side, range(3))
        total += dot(row, ext[tile : tile + 3].reshape(3 * T, 2 * T))
        high, low = split(total)
        half += dot(s[tile], high, ((0,), (0,))) + dot(s[tile], low, ((0,), (0,)))
    coupling = half + half.T
    rows, cols = places()
    both = jnp.where(rows >= cols, corr[...], coupling)
    diagonal = jnp.sum(jnp.where(rows == cols, coupling, 0.0), axis=1, keepdims=True)
    first, second = pack(both[:T], diagonal[:T]), pack(both[T:], diagonal[T:])
    even = m[PAR_Y] == 0
    mine[:, 0, :] = jnp.where(even, first, second)
    theirs[:, 0, :] = jnp.where(even, second, first)


def pack(square, diagonal):
    lane = lax.broadcasted_iota(jnp.int32, (T // 2, T), 1)
    extra = jnp.where(lane == 0, diagonal[: T // 2], jnp.where(lane == 1, diagonal[T // 2 :], 0.0))
    return jnp.concatenate([square[: T // 2], square[T // 2 :], extra], axis=1)


def unpack(table):
    square = jnp.concatenate([table[:, : 2 * T], table[:, 2 * T : 4 * T]], axis=0)
    return square, jnp.concatenate([table[:, 4 * T : 4 * T + 1], table[:, 4 * T + 1 : 4 * T + 2]], axis=0)


def lower_part(e, rows, cols):
    return jnp.where(rows > cols, e, jnp.where(rows == cols, 0.5 * e, 0.0))


def final_kernel(m, mine, theirs, s, keep, send, p_keep, p_send, x_ref, a_ref):
    rows, cols = places()
    even = m[PAR_Y] == 0
    first, second = mine[:, 0, :], theirs[:, 0, :]
    top = unpack(jnp.where(even, first, second))
    bottom = unpack(jnp.where(even, second, first))
    both = jnp.concatenate([top[0], bottom[0]], axis=0)
    diagonal = jnp.concatenate([top[1], bottom[1]], axis=0)
    turned = both.T
    corr = jnp.where(rows >= cols, both, turned)
    coupling = jnp.where(rows < cols, both, jnp.where(rows == cols, diagonal, turned))
    on_diagonal = jnp.where(rows == cols, corr, 0.0)
    scale_row = 1.0 / jnp.sqrt(jnp.sum(on_diagonal, axis=0, keepdims=True))
    scale_col = 1.0 / jnp.sqrt(jnp.sum(on_diagonal, axis=1, keepdims=True))
    scaled = corr * scale_row * scale_col
    unit = (rows == cols).astype(F32)

    a_ref[...] = scaled
    x_ref[...] = unit - lower_part(scaled - unit, rows, cols)

    def step(state):
        count, _ = state
        x = x_ref[...]
        e = dot3(dot3(x, a_ref[...]), x, ((1,), (1,))) - unit
        x_ref[...] = x - dot3(lower_part(e, rows, cols), x)
        return count + 1, jnp.sum(e * e)

    def more(state):
        count, size = state
        return (count < 12) & (size >= 4e-6) & (size < 1e4)

    _, size = lax.while_loop(more, step, (0, F32(1.0)))

    @pl.when(jnp.logical_not(size < 4e-6))
    def _():
        a_ref[...] = scaled
        x_ref[...] = unit

        def eliminate(j, carry):
            row = a_ref[pl.ds(j, 1), :]
            pivot = jnp.sum(jnp.where(cols[:1] == j, row, 0.0), axis=1, keepdims=True)
            a = a_ref[...]
            column = jnp.sum(jnp.where(cols == j, a, 0.0), axis=1, keepdims=True)
            factor = jnp.where(rows[:, :1] > j, column / pivot, 0.0)
            x = x_ref[...]
            x_row = x_ref[pl.ds(j, 1), :]
            a_ref[...] = a - factor * row
            x_ref[...] = x - factor * x_row
            return carry

        lax.fori_loop(0, 2 * T, eliminate, 0)
        pivots = jnp.sum(jnp.where(rows == cols, a_ref[...], 0.0), axis=1, keepdims=True)
        x_ref[...] = x_ref[...] / jnp.sqrt(pivots)

    x = x_ref[...] * scale_row
    rotation = x.astype(BF)
    ritz = dot(s[...].reshape(4 * T, 2 * T), rotation, ((1,), (1,))).astype(BF)
    ritz = ritz.reshape(4, T, 2 * T)
    projected = dot3(dot3(x, coupling), x, ((1,), (1,)))
    first_col = m[COL] == 0
    keep[...] = jnp.where(first_col, ritz[:, :, :T], ritz[:, :, T:])
    send[...] = jnp.where(first_col, ritz[:, :, T:], ritz[:, :, :T])
    p_keep[...] = jnp.where(first_col, projected[:, :T], projected[:, T:])
    p_send[...] = jnp.where(first_col, projected[:, T:], projected[:, :T])


def whole(shape):
    return pl.BlockSpec(shape, lambda i, m, n=len(shape): (0,) * n)


def call(kernel, m, arrays, outs, scratch=(), with_h=None, flops=0, name=None):
    specs = [whole(a.shape) for a in arrays]
    if with_h is not None:
        shape = (1,) + with_h.shape[1:]
        specs.insert(0, pl.BlockSpec(shape, lambda i, m: (m[SPIN], 0, 0, 0, 0, 0)))
        arrays = [with_h, *arrays]
    moved = sum(a.size * a.dtype.itemsize for a in arrays) + sum(o.size * o.dtype.itemsize for o in outs)
    return pl.pallas_call(
        kernel,
        out_shape=outs,
        grid_spec=pltpu.PrefetchScalarGridSpec(
            num_scalar_prefetch=1,
            grid=(1,),
            in_specs=specs,
            out_specs=[whole(o.shape) for o in outs],
            scratch_shapes=list(scratch),
        ),
        compiler_params=pltpu.CompilerParams(vmem_limit_bytes=32 * 1024 * 1024),
        cost_estimate=pl.CostEstimate(flops=flops, bytes_accessed=moved, transcendentals=0),
        name=name,
    )(m, *arrays)


def table(neighbour_index, block_count):
    gx, gy, col = (lax.axis_index(a) for a in AXES)
    spin = col ^ ((gx >> 1) & 1)
    toward = jnp.where(gx % 2 == 0, 1, -1)
    dx = jnp.stack([jnp.zeros_like(toward), toward, -toward])
    codes = (dx[:, None] + 1) * 3 + jnp.arange(3, dtype=jnp.int32)[None, :]
    slots = jnp.arange(NB, dtype=jnp.int32)
    index, count = neighbour_index[0], block_count[0]
    match = (index[:, None, None, :] == codes[None, :, :, None]) & (
        slots < count[:, None, None, None]
    )
    found = jnp.sum(jnp.where(match, slots + 1, 0), axis=-1) - 1
    scalars = jnp.stack([spin, col, gy % 2, gx % 2])
    return spin, col, jnp.concatenate([found.reshape(-1), scalars]).astype(jnp.int32)


def shaped(shape, dtype):
    return jax.ShapeDtypeStruct(shape, dtype)


def per_device(start_block, hamiltonian, neighbour_index, block_count):
    sizes = tuple(lax.axis_size(a) for a in AXES)
    members = sizes[0] * sizes[1]
    block, tile, full = (4, T, 2 * T), (1, T, 2 * T), (2 * T, 2 * T)
    ext = pltpu.VMEM((6, T, 2 * T), BF)
    spin, col, m = table(neighbour_index, block_count)

    other = swap_col(sizes, lax.dynamic_index_in_dim(start_block, 1 - spin, 0, keepdims=False)[0])
    own = lax.dynamic_index_in_dim(start_block, spin, 0, keepdims=False)[0]
    v, p, q = call(
        join_kernel, m, [own, other],
        [shaped(block, BF), shaped(tile, BF), shaped(tile, BF)], name="join",
    )

    def apply_ham(x, p, q, before):
        p, q = swap(sizes, p, 0, 1), swap(sizes, q, 0, 2)
        a, b = swap(sizes, x, 1, 0), swap(sizes, x, 2, 0)
        ends = jnp.concatenate([p, q], axis=0)
        ca, cb = swap(sizes, ends, 1, 0), swap(sizes, ends, 2, 0)
        (acc,) = call(
            own_kernel, m, [x, p, q], [shaped(block, F32)], [ext], hamiltonian,
            2 * 12 * T * T * 2 * T, "own",
        )
        last = before is not None
        arrays = [a, b, ca, cb, acc] + ([before] if last else [])
        return call(
            functools.partial(side_kernel, last=last), m, arrays,
            [shaped(block, BF), shaped(tile, BF), shaped(tile, BF)], [ext, ext], hamiltonian,
            2 * 24 * T * T * 2 * T, "sides",
        )

    first, p, q = apply_ham(v, p, q, None)
    second, low, high = apply_ham(first, p, q, v)

    above = shift(sizes, low, 0, -1)
    right_high = shift(sizes, low, -1, -1)
    right_low = shift(sizes, high, -1, 1)
    right = shift(sizes, second, -1, 0)
    corr, acc = call(
        inner_kernel, m, [second], [shaped(full, F32), shaped(block, F32)], (), hamiltonian,
        2 * 15 * T * T * 2 * T, "inner",
    )
    piece = shaped((members // 2, 1, 5 * T), F32)
    mine, theirs = call(
        gram_kernel, m, [second, above, right, right_low, right_high, acc, corr],
        [piece, piece], [ext], hamiltonian, 2 * 21 * T * T * 2 * T, "gram",
    )

    rows = members * second.shape[0] * second.shape[1]
    partial = mine + swap(sizes, theirs, 0, 1)
    total = exchange(sizes, partial).sum(axis=0, keepdims=True) / rows
    mine = exchange(sizes, jnp.broadcast_to(total, partial.shape))
    theirs = swap(sizes, mine, 0, 1)

    half = (4, T, T)
    keep, send, p_keep, p_send = call(
        final_kernel, m, [mine, theirs, second],
        [shaped(half, BF), shaped(half, BF), shaped((2 * T, T), F32), shaped((2 * T, T), F32)],
        [pltpu.VMEM(full, F32), pltpu.VMEM(full, F32)], None, 0, "final",
    )
    got, p_got = swap_col(sizes, send), swap_col(sizes, p_send)
    ritz = jnp.where(spin == 0, jnp.stack([keep, got]), jnp.stack([got, keep]))
    projected = jnp.where(spin == 0, jnp.stack([p_keep, p_got]), jnp.stack([p_got, p_keep]))
    return ritz[:, None], projected


def solution(mesh):
    return jax.shard_map(
        per_device,
        mesh=mesh,
        in_specs=(
            P(None, "gx", "gy", None, "col"),
            P(None, "gx", "gy", None, None, None),
            P("gx", "gy", None),
            P("gx", "gy"),
        ),
        out_specs=(P(None, "gx", "gy", None, "col"), P(None, None, "col")),
        check_vma=False,
    )
```

```python
import functools

import jax
import jax.numpy as jnp
from jax import lax
from jax.experimental import pallas as pl
from jax.experimental.pallas import tpu as pltpu
from jax.sharding import PartitionSpec as P

NB = 9
T = 128
AXES = ("gx", "gy", "col")
BF = jnp.bfloat16
F32 = jnp.float32
SPIN, COL, PAR_Y, PAR_X = 36, 37, 38, 39


def col_of(gx, spin):
    return spin ^ ((gx >> 1) & 1)


def device(sizes, gx, gy, col):
    return ((gx % sizes[0]) * sizes[1] + gy % sizes[1]) * sizes[2] + col


def pairs(sizes, target):
    out = []
    for gx in range(sizes[0]):
        for gy in range(sizes[1]):
            for spin in range(2):
                there = target(gx, gy)
                there_gx = there[0] % sizes[0]
                out.append(
                    (
                        device(sizes, gx, gy, col_of(gx, spin)),
                        device(sizes, there_gx, there[1], col_of(there_gx, spin)),
                    )
                )
    return out


def partner(index, kind):
    if kind == 0:
        return index
    return index + 1 if (index % 2 == 0) == (kind == 1) else index - 1


def swap(sizes, block, kind_x, kind_y):
    perm = pairs(sizes, lambda gx, gy: (partner(gx, kind_x), partner(gy, kind_y)))
    return lax.ppermute(block, AXES, perm)


def shift(sizes, block, dx, dy):
    return lax.ppermute(block, AXES, pairs(sizes, lambda gx, gy: (gx + dx, gy + dy)))


def swap_col(sizes, block):
    perm = [(d, d ^ 1) for d in range(sizes[0] * sizes[1] * 2)]
    return lax.ppermute(block, AXES, perm)


def exchange(sizes, pieces):
    groups = [
        [
            device(sizes, gx, gy, col_of(gx, spin))
            for gx in range(sizes[0])
            for gy in range(core, sizes[1], 2)
        ]
        for spin in range(2)
        for core in range(2)
    ]
    return lax.all_to_all(pieces, AXES, 0, 0, axis_index_groups=groups, tiled=True)


def dot(a, b, dims=((1,), (0,))):
    return lax.dot_general(a, b, (dims, ((), ())), preferred_element_type=F32)


def split(a):
    high = a.astype(BF)
    return high, (a - high.astype(F32)).astype(BF)


def dot3(a, b, dims=((1,), (0,))):
    (ah, al), (bh, bl) = split(a), split(b)
    return dot(ah, bh, dims) + (dot(ah, bl, dims) + dot(al, bh, dims))


def h_block(m, h, tile, side, dy):
    slot = m[(tile * 3 + side) * 3 + dy]
    block = h[0, 0, tile, jnp.maximum(slot, 0)]
    return jnp.where(slot >= 0, block, jnp.zeros_like(block))


def h_row(m, h, tile, side, dys):
    return jnp.concatenate([h_block(m, h, tile, side, dy) for dy in dys], axis=1)


def fill(m, ext, mid, ends):
    even = m[PAR_Y] == 0
    ext[1:2] = ends[1:2]
    ext[2:5] = mid[...]
    ext[pl.ds(jnp.where(even, 5, 0), 1)] = ends[0:1]
    ext[pl.ds(jnp.where(even, 0, 5), 1)] = ends[2:3]


def store_sides(m, ref, mid, p_ref, q_ref):
    even = m[PAR_Y] == 0
    p_ref[...] = ref[pl.ds(jnp.where(even, 3, 0), 1)]
    q_ref[...] = ref[pl.ds(jnp.where(even, 0, 3), 1)]
    mid[...] = ref[1:4]


def join_kernel(m, own, other, v, mid, p, q):
    first_col = m[COL] == 0
    v[:, :, :T] = jnp.where(first_col, own[...], other[...])
    v[:, :, T:] = jnp.where(first_col, other[...], own[...])
    store_sides(m, v, mid, p, q)


def own_kernel(m, h, mid, ends, acc, ext):
    fill(m, ext, mid, ends)
    for tile in range(4):
        row = h_row(m, h, tile, 0, range(3))
        acc[tile] = dot(row, ext[tile : tile + 3].reshape(3 * T, 2 * T))


def side_kernel(m, h, a, a_ends, b, b_ends, acc, *rest, last):
    if last:
        v, out, mid, p, q, ext_a, ext_b = rest
    else:
        out, mid, p, q, ext_a, ext_b = rest
    fill(m, ext_a, a, a_ends)
    fill(m, ext_b, b, b_ends)
    for tile in range(4):
        total = acc[tile]
        for side, ext in ((1, ext_a), (2, ext_b)):
            row = h_row(m, h, tile, side, range(3))
            total += dot(row, ext[tile : tile + 3].reshape(3 * T, 2 * T))
        if last:
            out[tile] = (total - v[tile].astype(F32)).astype(BF)
        else:
            out[tile] = (0.5 * total).astype(BF)
    store_sides(m, out, mid, p, q)


def inner_kernel(m, h, s, corr, acc):
    flat = s[...].reshape(4 * T, 2 * T)
    corr[...] = dot(flat, flat, ((0,), (0,)))
    for tile in range(4):
        total = 0.5 * dot(h_block(m, h, tile, 0, 1), s[tile])
        if tile < 3:
            total += dot(h_block(m, h, tile, 0, 2), s[tile + 1])
        acc[tile] = total


def places():
    shape = (2 * T, 2 * T)
    return lax.broadcasted_iota(jnp.int32, shape, 0), lax.broadcasted_iota(jnp.int32, shape, 1)


def gram_kernel(m, h, s, ends, right, right_ends, acc, corr, mine, theirs, ext):
    fill(m, ext, right, right_ends)
    above = jnp.where(m[PAR_Y] == 0, ends[0], ends[2])
    side = 1 + m[PAR_X]
    half = jnp.zeros((2 * T, 2 * T), F32)
    for tile in range(4):
        total = acc[tile]
        if tile == 3:
            total += dot(h_block(m, h, tile, 0, 2), above)
        row = h_row(m, h, tile, side, range(3))
        total += dot(row, ext[tile : tile + 3].reshape(3 * T, 2 * T))
        high, low = split(total)
        half += dot(s[tile], high, ((0,), (0,))) + dot(s[tile], low, ((0,), (0,)))
    coupling = half + half.T
    rows, cols = places()
    both = jnp.where(rows >= cols, corr[...], coupling)
    diagonal = jnp.sum(jnp.where(rows == cols, coupling, 0.0), axis=1, keepdims=True)
    first, second = pack(both[:T], diagonal[:T]), pack(both[T:], diagonal[T:])
    even = m[PAR_Y] == 0
    mine[:, 0, :] = jnp.where(even, first, second)
    theirs[:, 0, :] = jnp.where(even, second, first)


def pack(square, diagonal):
    lane = lax.broadcasted_iota(jnp.int32, (T // 2, T), 1)
    extra = jnp.where(lane == 0, diagonal[: T // 2], jnp.where(lane == 1, diagonal[T // 2 :], 0.0))
    return jnp.concatenate([square[: T // 2], square[T // 2 :], extra], axis=1)


def unpack(table):
    square = jnp.concatenate([table[:, : 2 * T], table[:, 2 * T : 4 * T]], axis=0)
    return square, jnp.concatenate([table[:, 4 * T : 4 * T + 1], table[:, 4 * T + 1 : 4 * T + 2]], axis=0)


def lower_part(e, rows, cols):
    return jnp.where(rows > cols, e, jnp.where(rows == cols, 0.5 * e, 0.0))


def final_kernel(m, mine, theirs, s, keep, send, p_keep, p_send, x_ref, a_ref):
    rows, cols = places()
    even = m[PAR_Y] == 0
    first, second = mine[:, 0, :], theirs[:, 0, :]
    top = unpack(jnp.where(even, first, second))
    bottom = unpack(jnp.where(even, second, first))
    both = jnp.concatenate([top[0], bottom[0]], axis=0)
    diagonal = jnp.concatenate([top[1], bottom[1]], axis=0)
    turned = both.T
    corr = jnp.where(rows >= cols, both, turned)
    coupling = jnp.where(rows < cols, both, jnp.where(rows == cols, diagonal, turned))
    on_diagonal = jnp.where(rows == cols, corr, 0.0)
    scale_row = 1.0 / jnp.sqrt(jnp.sum(on_diagonal, axis=0, keepdims=True))
    scale_col = 1.0 / jnp.sqrt(jnp.sum(on_diagonal, axis=1, keepdims=True))
    scaled = corr * scale_row * scale_col
    unit = (rows == cols).astype(F32)

    a_ref[...] = scaled
    x_ref[...] = unit - lower_part(scaled - unit, rows, cols)

    def step(state):
        count, _ = state
        x = x_ref[...]
        e = dot3(dot3(x, a_ref[...]), x, ((1,), (1,))) - unit
        x_ref[...] = x - dot3(lower_part(e, rows, cols), x)
        return count + 1, jnp.sum(e * e)

    def more(state):
        count, size = state
        return (count < 12) & (size >= 4e-6) & (size < 1e4)

    _, size = lax.while_loop(more, step, (0, F32(1.0)))

    @pl.when(jnp.logical_not(size < 4e-6))
    def _():
        a_ref[...] = scaled
        x_ref[...] = unit

        def eliminate(j, carry):
            row = a_ref[pl.ds(j, 1), :]
            pivot = jnp.sum(jnp.where(cols[:1] == j, row, 0.0), axis=1, keepdims=True)
            a = a_ref[...]
            column = jnp.sum(jnp.where(cols == j, a, 0.0), axis=1, keepdims=True)
            factor = jnp.where(rows[:, :1] > j, column / pivot, 0.0)
            x = x_ref[...]
            x_row = x_ref[pl.ds(j, 1), :]
            a_ref[...] = a - factor * row
            x_ref[...] = x - factor * x_row
            return carry

        lax.fori_loop(0, 2 * T, eliminate, 0)
        pivots = jnp.sum(jnp.where(rows == cols, a_ref[...], 0.0), axis=1, keepdims=True)
        x_ref[...] = x_ref[...] / jnp.sqrt(pivots)

    x = x_ref[...] * scale_row
    rotation = x.astype(BF)
    ritz = dot(s[...].reshape(4 * T, 2 * T), rotation, ((1,), (1,))).astype(BF)
    ritz = ritz.reshape(4, T, 2 * T)
    projected = dot3(dot3(x, coupling), x, ((1,), (1,)))
    first_col = m[COL] == 0
    keep[...] = jnp.where(first_col, ritz[:, :, :T], ritz[:, :, T:])
    send[...] = jnp.where(first_col, ritz[:, :, T:], ritz[:, :, :T])
    p_keep[...] = jnp.where(first_col, projected[:, :T], projected[:, T:])
    p_send[...] = jnp.where(first_col, projected[:, T:], projected[:, :T])


def whole(shape):
    return pl.BlockSpec(shape, lambda i, m, n=len(shape): (0,) * n)


def call(kernel, m, arrays, outs, scratch=(), with_h=None, flops=0, name=None):
    specs = [whole(a.shape) for a in arrays]
    if with_h is not None:
        shape = (1,) + with_h.shape[1:]
        specs.insert(0, pl.BlockSpec(shape, lambda i, m: (m[SPIN], 0, 0, 0, 0, 0)))
        arrays = [with_h, *arrays]
    moved = sum(a.size * a.dtype.itemsize for a in arrays) + sum(o.size * o.dtype.itemsize for o in outs)
    return pl.pallas_call(
        kernel,
        out_shape=outs,
        grid_spec=pltpu.PrefetchScalarGridSpec(
            num_scalar_prefetch=1,
            grid=(1,),
            in_specs=specs,
            out_specs=[whole(o.shape) for o in outs],
            scratch_shapes=list(scratch),
        ),
        compiler_params=pltpu.CompilerParams(vmem_limit_bytes=32 * 1024 * 1024),
        cost_estimate=pl.CostEstimate(flops=flops, bytes_accessed=moved, transcendentals=0),
        name=name,
    )(m, *arrays)


def table(neighbour_index, block_count):
    gx, gy, col = (lax.axis_index(a) for a in AXES)
    spin = col ^ ((gx >> 1) & 1)
    toward = jnp.where(gx % 2 == 0, 1, -1)
    dx = jnp.stack([jnp.zeros_like(toward), toward, -toward])
    codes = (dx[:, None] + 1) * 3 + jnp.arange(3, dtype=jnp.int32)[None, :]
    slots = jnp.arange(NB, dtype=jnp.int32)
    index, count = neighbour_index[0], block_count[0]
    match = (index[:, None, None, :] == codes[None, :, :, None]) & (
        slots < count[:, None, None, None]
    )
    found = jnp.sum(jnp.where(match, slots + 1, 0), axis=-1) - 1
    scalars = jnp.stack([spin, col, gy % 2, gx % 2])
    return spin, col, jnp.concatenate([found.reshape(-1), scalars]).astype(jnp.int32)


def shaped(shape, dtype):
    return jax.ShapeDtypeStruct(shape, dtype)


def per_device(start_block, hamiltonian, neighbour_index, block_count):
    sizes = tuple(lax.axis_size(a) for a in AXES)
    members = sizes[0] * sizes[1]
    block, middle, tile, full = (4, T, 2 * T), (3, T, 2 * T), (1, T, 2 * T), (2 * T, 2 * T)
    ext = pltpu.VMEM((6, T, 2 * T), BF)
    spin, col, m = table(neighbour_index, block_count)

    other = swap_col(sizes, lax.dynamic_index_in_dim(start_block, 1 - spin, 0, keepdims=False)[0])
    own = lax.dynamic_index_in_dim(start_block, spin, 0, keepdims=False)[0]
    parts = [shaped(block, BF), shaped(middle, BF), shaped(tile, BF), shaped(tile, BF)]
    v, mid, p, q = call(join_kernel, m, [own, other], parts, name="join")

    def along_y(x, p, q):
        p, q = swap(sizes, p, 0, 1), swap(sizes, q, 0, 2)
        return jnp.concatenate([p, x[:1], q], axis=0)

    def apply_ham(x, mid, p, q, before):
        ends = along_y(x, p, q)
        a, b = swap(sizes, mid, 1, 0), swap(sizes, mid, 2, 0)
        a_ends, b_ends = swap(sizes, ends, 1, 0), swap(sizes, ends, 2, 0)
        (acc,) = call(
            own_kernel, m, [mid, ends], [shaped(block, F32)], [ext], hamiltonian,
            2 * 12 * T * T * 2 * T, "own",
        )
        last = before is not None
        arrays = [a, a_ends, b, b_ends, acc] + ([before] if last else [])
        return call(
            functools.partial(side_kernel, last=last), m, arrays, parts, [ext, ext], hamiltonian,
            2 * 24 * T * T * 2 * T, "sides",
        )

    first, mid, p, q = apply_ham(v, mid, p, q, None)
    second, mid, p, q = apply_ham(first, mid, p, q, v)

    ends = along_y(second, p, q)
    right = shift(sizes, mid, -1, 0)
    right_ends = shift(sizes, ends, -1, 0)
    corr, acc = call(
        inner_kernel, m, [second], [shaped(full, F32), shaped(block, F32)], (), hamiltonian,
        2 * 15 * T * T * 2 * T, "inner",
    )
    piece = shaped((members // 2, 1, 5 * T), F32)
    mine, theirs = call(
        gram_kernel, m, [second, ends, right, right_ends, acc, corr],
        [piece, piece], [ext], hamiltonian, 2 * 21 * T * T * 2 * T, "gram",
    )

    rows = members * second.shape[0] * second.shape[1]
    partial = mine + swap(sizes, theirs, 0, 1)
    total = exchange(sizes, partial).sum(axis=0, keepdims=True) / rows
    mine = exchange(sizes, jnp.broadcast_to(total, partial.shape))
    theirs = swap(sizes, mine, 0, 1)

    half = (4, T, T)
    keep, send, p_keep, p_send = call(
        final_kernel, m, [mine, theirs, second],
        [shaped(half, BF), shaped(half, BF), shaped((2 * T, T), F32), shaped((2 * T, T), F32)],
        [pltpu.VMEM(full, F32), pltpu.VMEM(full, F32)], None, 0, "final",
    )
    got, p_got = swap_col(sizes, send), swap_col(sizes, p_send)
    ritz = jnp.where(spin == 0, jnp.stack([keep, got]), jnp.stack([got, keep]))
    projected = jnp.where(spin == 0, jnp.stack([p_keep, p_got]), jnp.stack([p_got, p_keep]))
    return ritz[:, None], projected


def solution(mesh):
    return jax.shard_map(
        per_device,
        mesh=mesh,
        in_specs=(
            P(None, "gx", "gy", None, "col"),
            P(None, "gx", "gy", None, None, None),
            P("gx", "gy", None),
            P("gx", "gy"),
        ),
        out_specs=(P(None, "gx", "gy", None, "col"), P(None, None, "col")),
        check_vma=False,
    )
```

```python
import functools

import jax
import jax.numpy as jnp
from jax import lax
from jax.experimental import pallas as pl
from jax.experimental.pallas import tpu as pltpu
from jax.sharding import PartitionSpec as P

NB = 9
T = 128
AXES = ("gx", "gy", "col")
BF = jnp.bfloat16
F32 = jnp.float32
SPIN, COL, PAR_Y, PAR_X = 36, 37, 38, 39


def col_of(gx, spin):
    return spin ^ ((gx >> 1) & 1)


def device(sizes, gx, gy, col):
    return ((gx % sizes[0]) * sizes[1] + gy % sizes[1]) * sizes[2] + col


def pairs(sizes, target):
    out = []
    for gx in range(sizes[0]):
        for gy in range(sizes[1]):
            for spin in range(2):
                there = target(gx, gy)
                there_gx = there[0] % sizes[0]
                out.append(
                    (
                        device(sizes, gx, gy, col_of(gx, spin)),
                        device(sizes, there_gx, there[1], col_of(there_gx, spin)),
                    )
                )
    return out


def partner(index, kind):
    if kind == 0:
        return index
    return index + 1 if (index % 2 == 0) == (kind == 1) else index - 1


def swap(sizes, block, kind_x, kind_y):
    perm = pairs(sizes, lambda gx, gy: (partner(gx, kind_x), partner(gy, kind_y)))
    return lax.ppermute(block, AXES, perm)


def shift(sizes, block, dx, dy):
    return lax.ppermute(block, AXES, pairs(sizes, lambda gx, gy: (gx + dx, gy + dy)))


def swap_col(sizes, block):
    perm = [(d, d ^ 1) for d in range(sizes[0] * sizes[1] * 2)]
    return lax.ppermute(block, AXES, perm)


def exchange(sizes, pieces):
    groups = [
        [
            device(sizes, gx, gy, col_of(gx, spin))
            for gx in range(sizes[0])
            for gy in range(core, sizes[1], 2)
        ]
        for spin in range(2)
        for core in range(2)
    ]
    return lax.all_to_all(pieces, AXES, 0, 0, axis_index_groups=groups, tiled=True)


def dot(a, b, dims=((1,), (0,))):
    return lax.dot_general(a, b, (dims, ((), ())), preferred_element_type=F32)


def split(a):
    high = a.astype(BF)
    return high, (a - high.astype(F32)).astype(BF)


def dot3(a, b, dims=((1,), (0,))):
    (ah, al), (bh, bl) = split(a), split(b)
    return dot(ah, bh, dims) + (dot(ah, bl, dims) + dot(al, bh, dims))


def order_kernel(m, h, o):
    for tile in range(4):
        for at in range(9):
            slot = m[tile * 9 + at]
            block = h[0, 0, tile, jnp.maximum(slot, 0)]
            o[tile, :, at * T : (at + 1) * T] = jnp.where(slot >= 0, block, jnp.zeros_like(block))


def blocks(o, tile, sides, dys):
    out = []
    for side in sides:
        at = (side * 3 + dys[0]) * T
        if not isinstance(side, int):
            at = pl.multiple_of(at, T)
        out.append(o[tile, :, pl.ds(at, len(dys) * T)])
    return out[0] if len(out) == 1 else jnp.concatenate(out, axis=1)


def join_kernel(m, own, other, v):
    first_col = m[COL] == 0
    v[:, :, :T] = jnp.where(first_col, own[...], other[...])
    v[:, :, T:] = jnp.where(first_col, other[...], own[...])


def edges_kernel(m, *refs):
    *sources, p, q = refs
    even = m[PAR_Y] == 0
    for at, x in enumerate(sources):
        p[at : at + 1] = x[pl.ds(jnp.where(even, 3, 0), 1)]
        q[at : at + 1] = x[pl.ds(jnp.where(even, 0, 3), 1)]


def inside(o, tile, sides, sources):
    dys = [dy for dy in range(3) if 0 <= tile + dy - 1 < 4]
    at = tile + dys[0] - 1
    rhs = [x[at : at + len(dys)].reshape(len(dys) * T, 2 * T) for x in sources]
    return dot(blocks(o, tile, sides, dys), rhs[0] if len(rhs) == 1 else jnp.concatenate(rhs, axis=0))


def ends(m, p, q):
    even = m[PAR_Y] == 0
    return jnp.where(even, q[...], p[...]), jnp.where(even, p[...], q[...])


def outside(o, tile, sides, dy, tiles):
    return dot(blocks(o, tile, sides, (dy,)), tiles.reshape(len(sides) * T, 2 * T))


def core_kernel(m, o, x, a, b, acc):
    for tile in range(4):
        acc[tile] = inside(o, tile, range(3), (x, a, b))


def rim_kernel(m, o, p, q, acc, *rest):
    *before, out = rest
    low, high = ends(m, p, q)
    for tile in range(4):
        total = acc[tile]
        if tile == 0:
            total += outside(o, tile, range(3), 0, low)
        if tile == 3:
            total += outside(o, tile, range(3), 2, high)
        if before:
            out[tile] = (total - before[0][tile].astype(F32)).astype(BF)
        else:
            out[tile] = (0.5 * total).astype(BF)


def corr_kernel(m, o, s, corr, acc):
    flat = s[...].reshape(4 * T, 2 * T)
    corr[...] = dot(flat, flat, ((0,), (0,)))
    for tile in range(4):
        total = 0.5 * dot(blocks(o, tile, (0,), (1,)), s[tile])
        if tile < 3:
            total += dot(blocks(o, tile, (0,), (2,)), s[tile + 1])
        acc[tile] = total


def coupled(s_tile, total):
    high, low = split(total)
    return dot(s_tile, high, ((0,), (0,))) + dot(s_tile, low, ((0,), (0,)))


def right_kernel(m, o, s, right, acc, out, half):
    side = 1 + m[PAR_X]
    total = jnp.zeros((2 * T, 2 * T), F32)
    for tile in range(4):
        part = acc[tile] + inside(o, tile, (side,), (right,))
        if tile in (1, 2):
            total += coupled(s[tile], part)
        else:
            out[tile // 3] = part
    half[...] = total


def places():
    shape = (2 * T, 2 * T)
    return lax.broadcasted_iota(jnp.int32, shape, 0), lax.broadcasted_iota(jnp.int32, shape, 1)


def gram_kernel(m, o, s, p, q, acc, partial, corr, mine, theirs):
    side = 1 + m[PAR_X]
    low, high = ends(m, p, q)
    half = partial[...]
    half += coupled(s[0], acc[0] + outside(o, 0, (side,), 0, low[1:2]))
    half += coupled(s[3], acc[1] + outside(o, 3, (0, side), 2, high))
    coupling = half + half.T
    rows, cols = places()
    both = jnp.where(rows >= cols, corr[...], coupling)
    diagonal = jnp.sum(jnp.where(rows == cols, coupling, 0.0), axis=1, keepdims=True)
    first, second = pack(both[:T], diagonal[:T]), pack(both[T:], diagonal[T:])
    even = m[PAR_Y] == 0
    mine[:, 0, :] = jnp.where(even, first, second)
    theirs[:, 0, :] = jnp.where(even, second, first)


def pack(square, diagonal):
    lane = lax.broadcasted_iota(jnp.int32, (T // 2, T), 1)
    extra = jnp.where(lane == 0, diagonal[: T // 2], jnp.where(lane == 1, diagonal[T // 2 :], 0.0))
    return jnp.concatenate([square[: T // 2], square[T // 2 :], extra], axis=1)


def unpack(table):
    square = jnp.concatenate([table[:, : 2 * T], table[:, 2 * T : 4 * T]], axis=0)
    return square, jnp.concatenate([table[:, 4 * T : 4 * T + 1], table[:, 4 * T + 1 : 4 * T + 2]], axis=0)


def lower_part(e, rows, cols):
    return jnp.where(rows > cols, e, jnp.where(rows == cols, 0.5 * e, 0.0))


def final_kernel(m, mine, theirs, s, keep, send, p_keep, p_send, x_ref, a_ref):
    rows, cols = places()
    even = m[PAR_Y] == 0
    first, second = mine[:, 0, :], theirs[:, 0, :]
    top = unpack(jnp.where(even, first, second))
    bottom = unpack(jnp.where(even, second, first))
    both = jnp.concatenate([top[0], bottom[0]], axis=0)
    diagonal = jnp.concatenate([top[1], bottom[1]], axis=0)
    turned = both.T
    corr = jnp.where(rows >= cols, both, turned)
    coupling = jnp.where(rows < cols, both, jnp.where(rows == cols, diagonal, turned))
    on_diagonal = jnp.where(rows == cols, corr, 0.0)
    scale_row = 1.0 / jnp.sqrt(jnp.sum(on_diagonal, axis=0, keepdims=True))
    scale_col = 1.0 / jnp.sqrt(jnp.sum(on_diagonal, axis=1, keepdims=True))
    scaled = corr * scale_row * scale_col
    unit = (rows == cols).astype(F32)

    a_ref[...] = scaled
    x_ref[...] = unit - lower_part(scaled - unit, rows, cols)

    def step(state):
        count, _ = state
        x = x_ref[...]
        e = dot3(dot3(x, a_ref[...]), x, ((1,), (1,))) - unit
        x_ref[...] = x - dot3(lower_part(e, rows, cols), x)
        return count + 1, jnp.sum(e * e)

    def more(state):
        count, size = state
        return (count < 12) & (size >= 4e-6) & (size < 1e4)

    _, size = lax.while_loop(more, step, (0, F32(1.0)))

    @pl.when(jnp.logical_not(size < 4e-6))
    def _():
        a_ref[...] = scaled
        x_ref[...] = unit

        def eliminate(j, carry):
            row = a_ref[pl.ds(j, 1), :]
            pivot = jnp.sum(jnp.where(cols[:1] == j, row, 0.0), axis=1, keepdims=True)
            a = a_ref[...]
            column = jnp.sum(jnp.where(cols == j, a, 0.0), axis=1, keepdims=True)
            factor = jnp.where(rows[:, :1] > j, column / pivot, 0.0)
            x = x_ref[...]
            x_row = x_ref[pl.ds(j, 1), :]
            a_ref[...] = a - factor * row
            x_ref[...] = x - factor * x_row
            return carry

        lax.fori_loop(0, 2 * T, eliminate, 0)
        pivots = jnp.sum(jnp.where(rows == cols, a_ref[...], 0.0), axis=1, keepdims=True)
        x_ref[...] = x_ref[...] / jnp.sqrt(pivots)

    x = x_ref[...] * scale_row
    rotation = x.astype(BF)
    ritz = dot(s[...].reshape(4 * T, 2 * T), rotation, ((1,), (1,))).astype(BF)
    ritz = ritz.reshape(4, T, 2 * T)
    projected = dot3(dot3(x, coupling), x, ((1,), (1,)))
    first_col = m[COL] == 0
    keep[...] = jnp.where(first_col, ritz[:, :, :T], ritz[:, :, T:])
    send[...] = jnp.where(first_col, ritz[:, :, T:], ritz[:, :, :T])
    p_keep[...] = jnp.where(first_col, projected[:, :T], projected[:, T:])
    p_send[...] = jnp.where(first_col, projected[:, T:], projected[:, :T])


def whole(shape):
    return pl.BlockSpec(shape, lambda i, m, n=len(shape): (0,) * n)


def call(kernel, m, arrays, outs, name, flops=0, specs=None, scratch=()):
    arrays = list(arrays)
    moved = sum(a.size * a.dtype.itemsize for a in [*arrays, *outs])
    return pl.pallas_call(
        kernel,
        out_shape=outs,
        grid_spec=pltpu.PrefetchScalarGridSpec(
            num_scalar_prefetch=1,
            grid=(1,),
            in_specs=specs or [whole(a.shape) for a in arrays],
            out_specs=[whole(o.shape) for o in outs],
            scratch_shapes=list(scratch),
        ),
        compiler_params=pltpu.CompilerParams(vmem_limit_bytes=32 * 1024 * 1024),
        cost_estimate=pl.CostEstimate(flops=2 * T * T * 2 * T * flops, bytes_accessed=moved, transcendentals=0),
        name=name,
    )(m, *arrays)


def table(neighbour_index, block_count):
    gx, gy, col = (lax.axis_index(a) for a in AXES)
    spin = col ^ ((gx >> 1) & 1)
    toward = jnp.where(gx % 2 == 0, 1, -1)
    dx = jnp.stack([jnp.zeros_like(toward), toward, -toward])
    codes = (dx[:, None] + 1) * 3 + jnp.arange(3, dtype=jnp.int32)[None, :]
    slots = jnp.arange(NB, dtype=jnp.int32)
    index, count = neighbour_index[0], block_count[0]
    match = (index[:, None, None, :] == codes[None, :, :, None]) & (
        slots < count[:, None, None, None]
    )
    found = jnp.sum(jnp.where(match, slots + 1, 0), axis=-1) - 1
    scalars = jnp.stack([spin, col, gy % 2, gx % 2])
    return spin, col, jnp.concatenate([found.reshape(-1), scalars]).astype(jnp.int32)


def shaped(shape, dtype):
    return jax.ShapeDtypeStruct(shape, dtype)


def per_device(start_block, hamiltonian, neighbour_index, block_count):
    sizes = tuple(lax.axis_size(a) for a in AXES)
    members = sizes[0] * sizes[1]
    block, full = (4, T, 2 * T), (2 * T, 2 * T)
    spin, col, m = table(neighbour_index, block_count)

    other = swap_col(sizes, lax.dynamic_index_in_dim(start_block, 1 - spin, 0, keepdims=False)[0])
    own = lax.dynamic_index_in_dim(start_block, spin, 0, keepdims=False)[0]
    spin_block = pl.BlockSpec((1,) + hamiltonian.shape[1:], lambda i, m: (m[SPIN], 0, 0, 0, 0, 0))
    (o,) = call(order_kernel, m, [hamiltonian], [shaped((4, T, NB * T), BF)], "order", specs=[spin_block])
    (v,) = call(join_kernel, m, [own, other], [shaped(block, BF)], "join")

    def along_y(*sources):
        edge = shaped((len(sources), T, 2 * T), BF)
        p, q = call(edges_kernel, m, sources, [edge, edge], "edges")
        return swap(sizes, p, 0, 1), swap(sizes, q, 0, 2)

    def apply_ham(o, x, before):
        a, b = swap(sizes, x, 1, 0), swap(sizes, x, 2, 0)
        o, a, b = lax.optimization_barrier((o, a, b))
        p, q = along_y(x, a, b)
        (acc,) = call(core_kernel, m, [o, x, a, b], [shaped(block, F32)], "core", 30)
        (out,) = call(rim_kernel, m, [o, p, q, acc, *before], [shaped(block, BF)], "rim", 6)
        return o, out

    o, first = apply_ham(o, v, [])
    o, second = apply_ham(o, first, [v])

    right = shift(sizes, second, -1, 0)
    corr, acc = call(corr_kernel, m, [o, second], [shaped(full, F32), shaped(block, F32)], "corr", 15)
    p, q = along_y(second, right)
    acc, half = call(
        right_kernel, m, [o, second, right, acc], [shaped((2, T, 2 * T), F32), shaped(full, F32)], "right", 18
    )
    piece = shaped((members // 2, 1, 5 * T), F32)
    mine, theirs = call(gram_kernel, m, [o, second, p, q, acc, half, corr], [piece, piece], "gram", 11)

    rows = members * second.shape[0] * second.shape[1]
    partial = mine + swap(sizes, theirs, 0, 1)
    total = exchange(sizes, partial).sum(axis=0, keepdims=True) / rows
    mine = exchange(sizes, jnp.broadcast_to(total, partial.shape))
    theirs = swap(sizes, mine, 0, 1)

    half = (4, T, T)
    keep, send, p_keep, p_send = call(
        final_kernel, m, [mine, theirs, second],
        [shaped(half, BF), shaped(half, BF), shaped((2 * T, T), F32), shaped((2 * T, T), F32)], "final", 80,
        scratch=[pltpu.VMEM(full, F32), pltpu.VMEM(full, F32)],
    )
    got, p_got = swap_col(sizes, send), swap_col(sizes, p_send)
    ritz = jnp.where(spin == 0, jnp.stack([keep, got]), jnp.stack([got, keep]))
    projected = jnp.where(spin == 0, jnp.stack([p_keep, p_got]), jnp.stack([p_got, p_keep]))
    return ritz[:, None], projected


def solution(mesh):
    return jax.shard_map(
        per_device,
        mesh=mesh,
        in_specs=(
            P(None, "gx", "gy", None, "col"),
            P(None, "gx", "gy", None, None, None),
            P("gx", "gy", None),
            P("gx", "gy"),
        ),
        out_specs=(P(None, "gx", "gy", None, "col"), P(None, None, "col")),
        check_vma=False,
    )
```

```python
import functools

import jax
import jax.numpy as jnp
from jax import lax
from jax.experimental import pallas as pl
from jax.experimental.pallas import tpu as pltpu
from jax.sharding import PartitionSpec as P

NB = 9
T = 128
AXES = ("gx", "gy", "col")
BF = jnp.bfloat16
F32 = jnp.float32
SPIN, COL, PAR_Y, PAR_X = 36, 37, 38, 39


def col_of(gx, spin):
    return spin ^ ((gx >> 1) & 1)


def device(sizes, gx, gy, col):
    return ((gx % sizes[0]) * sizes[1] + gy % sizes[1]) * sizes[2] + col


def pairs(sizes, target):
    out = []
    for gx in range(sizes[0]):
        for gy in range(sizes[1]):
            for spin in range(2):
                there = target(gx, gy)
                there_gx = there[0] % sizes[0]
                out.append(
                    (
                        device(sizes, gx, gy, col_of(gx, spin)),
                        device(sizes, there_gx, there[1], col_of(there_gx, spin)),
                    )
                )
    return out


def partner(index, kind):
    if kind == 0:
        return index
    return index + 1 if (index % 2 == 0) == (kind == 1) else index - 1


def swap(sizes, block, kind_x, kind_y):
    perm = pairs(sizes, lambda gx, gy: (partner(gx, kind_x), partner(gy, kind_y)))
    return lax.ppermute(block, AXES, perm)


def shift(sizes, block, dx, dy):
    return lax.ppermute(block, AXES, pairs(sizes, lambda gx, gy: (gx + dx, gy + dy)))


def swap_col(sizes, block):
    perm = [(d, d ^ 1) for d in range(sizes[0] * sizes[1] * 2)]
    return lax.ppermute(block, AXES, perm)


def exchange(sizes, pieces):
    groups = [
        [
            device(sizes, gx, gy, col_of(gx, spin))
            for gx in range(sizes[0])
            for gy in range(core, sizes[1], 2)
        ]
        for spin in range(2)
        for core in range(2)
    ]
    return lax.all_to_all(pieces, AXES, 0, 0, axis_index_groups=groups, tiled=True)


def dot(a, b, dims=((1,), (0,))):
    return lax.dot_general(a, b, (dims, ((), ())), preferred_element_type=F32)


def split(a):
    high = a.astype(BF)
    return high, (a - high.astype(F32)).astype(BF)


def dot3(a, b, dims=((1,), (0,))):
    (ah, al), (bh, bl) = split(a), split(b)
    return dot(ah, bh, dims) + (dot(ah, bl, dims) + dot(al, bh, dims))


def order_kernel(m, h, o):
    for tile in range(4):
        for at in range(9):
            slot = m[tile * 9 + at]
            block = h[0, 0, tile, jnp.maximum(slot, 0)]
            o[tile, :, at * T : (at + 1) * T] = jnp.where(slot >= 0, block, jnp.zeros_like(block))


def blocks(o, tile, sides, dys):
    out = []
    for side in sides:
        at = (side * 3 + dys[0]) * T
        if not isinstance(side, int):
            at = pl.multiple_of(at, T)
        out.append(o[tile, :, pl.ds(at, len(dys) * T)])
    return out[0] if len(out) == 1 else jnp.concatenate(out, axis=1)


def store_parts(m, ref, mid, p, q):
    even = m[PAR_Y] == 0
    p[...] = ref[pl.ds(jnp.where(even, 3, 0), 1)]
    q[...] = ref[pl.ds(jnp.where(even, 0, 3), 1)]
    mid[...] = ref[1:4]


def join_kernel(m, own, other, v, mid, p, q):
    first_col = m[COL] == 0
    v[:, :, :T] = jnp.where(first_col, own[...], other[...])
    v[:, :, T:] = jnp.where(first_col, other[...], own[...])
    store_parts(m, v, mid, p, q)


def fill(m, ext, mid, ends):
    even = m[PAR_Y] == 0
    ext[1:2] = ends[1:2]
    ext[2:5] = mid[...]
    ext[pl.ds(jnp.where(even, 5, 0), 1)] = ends[0:1]
    ext[pl.ds(jnp.where(even, 0, 5), 1)] = ends[2:3]


def product(o, tile, sides, at, sources):
    row = blocks(o, tile, sides, [place - tile for place in at])
    return dot(row, jnp.concatenate([x.reshape(len(at) * T, 2 * T) for x in sources], axis=0))


def core_kernel(m, o, mid, ends, a, b, acc, ext):
    fill(m, ext, mid, ends)
    for tile in range(4):
        total = product(o, tile, (0,), range(tile, tile + 3), [ext[tile : tile + 3]])
        at = [place for place in range(tile, tile + 3) if 2 <= place <= 4]
        sources = [x[at[0] - 2 : at[-1] - 1] for x in (a, b)]
        acc[tile] = total + product(o, tile, (1, 2), at, sources)


def rim_kernel(m, o, a_ends, b_ends, acc, *rest, last):
    if last:
        before, out, first_out, last_out = rest
    else:
        out, mid, p, q = rest
    even = m[PAR_Y] == 0
    low = [jnp.where(even, x[2:3], x[0:1]) for x in (a_ends, b_ends)]
    first = [x[1:2] for x in (a_ends, b_ends)]
    high = [jnp.where(even, x[0:1], x[2:3]) for x in (a_ends, b_ends)]
    for tile in range(4):
        total = acc[tile]
        if tile == 0:
            pair = [jnp.concatenate([x, y], axis=0) for x, y in zip(low, first)]
            total += product(o, tile, (1, 2), (0, 1), pair)
        if tile == 1:
            total += product(o, tile, (1, 2), (1,), first)
        if tile == 3:
            total += product(o, tile, (1, 2), (5,), high)
        if last:
            out[tile] = (total - before[tile].astype(F32)).astype(BF)
        else:
            out[tile] = (0.5 * total).astype(BF)
    if last:
        first_out[...] = out[0:1]
        last_out[...] = out[3:4]
    else:
        store_parts(m, out, mid, p, q)


def corr_kernel(m, o, s, corr, acc):
    flat = s[...].reshape(4 * T, 2 * T)
    corr[...] = dot(flat, flat, ((0,), (0,)))
    for tile in range(4):
        total = 0.5 * dot(blocks(o, tile, (0,), (1,)), s[tile])
        if tile < 3:
            total += dot(blocks(o, tile, (0,), (2,)), s[tile + 1])
        acc[tile] = total


def coupled(s_tile, total):
    high, low = split(total)
    return dot(s_tile, high, ((0,), (0,))) + dot(s_tile, low, ((0,), (0,)))


def places():
    shape = (2 * T, 2 * T)
    return lax.broadcasted_iota(jnp.int32, shape, 0), lax.broadcasted_iota(jnp.int32, shape, 1)


def gram_kernel(m, o, s, above, right_low, right, right_high, acc, corr, mine, theirs, ext):
    ext[0:1] = right_low[...]
    ext[1:5] = right[...]
    ext[5:6] = right_high[...]
    side = 1 + m[PAR_X]
    half = jnp.zeros((2 * T, 2 * T), F32)
    for tile in range(4):
        part = acc[tile] + product(o, tile, (side,), range(tile, tile + 3), [ext[tile : tile + 3]])
        if tile == 3:
            part += product(o, tile, (0,), (5,), [above[...]])
        half += coupled(s[tile], part)
    coupling = half + half.T
    rows, cols = places()
    both = jnp.where(rows >= cols, corr[...], coupling)
    diagonal = jnp.sum(jnp.where(rows == cols, coupling, 0.0), axis=1, keepdims=True)
    first, second = pack(both[:T], diagonal[:T]), pack(both[T:], diagonal[T:])
    even = m[PAR_Y] == 0
    mine[:, 0, :] = jnp.where(even, first, second)
    theirs[:, 0, :] = jnp.where(even, second, first)


def pack(square, diagonal):
    lane = lax.broadcasted_iota(jnp.int32, (T // 2, T), 1)
    extra = jnp.where(lane == 0, diagonal[: T // 2], jnp.where(lane == 1, diagonal[T // 2 :], 0.0))
    return jnp.concatenate([square[: T // 2], square[T // 2 :], extra], axis=1)


def unpack(table):
    square = jnp.concatenate([table[:, : 2 * T], table[:, 2 * T : 4 * T]], axis=0)
    return square, jnp.concatenate([table[:, 4 * T : 4 * T + 1], table[:, 4 * T + 1 : 4 * T + 2]], axis=0)


def lower_part(e, rows, cols):
    return jnp.where(rows > cols, e, jnp.where(rows == cols, 0.5 * e, 0.0))


def final_kernel(m, mine, theirs, s, keep, p_keep, send, x_ref, a_ref):
    rows, cols = places()
    even = m[PAR_Y] == 0
    first, second = mine[:, 0, :], theirs[:, 0, :]
    top = unpack(jnp.where(even, first, second))
    bottom = unpack(jnp.where(even, second, first))
    both = jnp.concatenate([top[0], bottom[0]], axis=0)
    diagonal = jnp.concatenate([top[1], bottom[1]], axis=0)
    turned = both.T
    corr = jnp.where(rows >= cols, both, turned)
    coupling = jnp.where(rows < cols, both, jnp.where(rows == cols, diagonal, turned))
    on_diagonal = jnp.where(rows == cols, corr, 0.0)
    scale_row = 1.0 / jnp.sqrt(jnp.sum(on_diagonal, axis=0, keepdims=True))
    scale_col = 1.0 / jnp.sqrt(jnp.sum(on_diagonal, axis=1, keepdims=True))
    scaled = corr * scale_row * scale_col
    unit = (rows == cols).astype(F32)

    a_ref[...] = scaled
    x_ref[...] = unit - lower_part(scaled - unit, rows, cols)

    def step(state):
        count, _ = state
        x = x_ref[...]
        e = dot3(dot3(x, a_ref[...]), x, ((1,), (1,))) - unit
        x_ref[...] = x - dot3(lower_part(e, rows, cols), x)
        return count + 1, jnp.sum(e * e)

    def more(state):
        count, size = state
        return (count < 12) & (size >= 4e-6) & (size < 1e4)

    _, size = lax.while_loop(more, step, (0, F32(1.0)))

    @pl.when(jnp.logical_not(size < 4e-6))
    def _():
        a_ref[...] = scaled
        x_ref[...] = unit

        def eliminate(j, carry):
            row = a_ref[pl.ds(j, 1), :]
            pivot = jnp.sum(jnp.where(cols[:1] == j, row, 0.0), axis=1, keepdims=True)
            a = a_ref[...]
            column = jnp.sum(jnp.where(cols == j, a, 0.0), axis=1, keepdims=True)
            factor = jnp.where(rows[:, :1] > j, column / pivot, 0.0)
            x = x_ref[...]
            x_row = x_ref[pl.ds(j, 1), :]
            a_ref[...] = a - factor * row
            x_ref[...] = x - factor * x_row
            return carry

        lax.fori_loop(0, 2 * T, eliminate, 0)
        pivots = jnp.sum(jnp.where(rows == cols, a_ref[...], 0.0), axis=1, keepdims=True)
        x_ref[...] = x_ref[...] / jnp.sqrt(pivots)

    x = x_ref[...] * scale_row
    rotation = x.astype(BF)
    ritz = dot(s[...].reshape(4 * T, 2 * T), rotation, ((1,), (1,))).astype(BF)
    ritz = ritz.reshape(4, T, 2 * T)
    projected = dot3(dot3(x, coupling), x, ((1,), (1,)))
    first_col = m[COL] == 0
    keep[...] = jnp.where(first_col, ritz[:, :, :T], ritz[:, :, T:])
    send[0:4] = jnp.where(first_col, ritz[:, :, T:], ritz[:, :, :T])
    p_keep[...] = jnp.where(first_col, projected[:, :T], projected[:, T:])
    high, low = split(jnp.where(first_col, projected[:, T:], projected[:, :T]))
    send[4:6] = high.reshape(2, T, T)
    send[6:8] = low.reshape(2, T, T)


def assemble_kernel(m, keep, p_keep, got, ritz, projected):
    spin = m[SPIN]
    ritz[pl.ds(spin, 1)] = keep[...][None, None]
    ritz[pl.ds(1 - spin, 1)] = got[0:4][None, None]
    projected[pl.ds(spin, 1)] = p_keep[...][None]
    received = got[4:6].astype(F32) + got[6:8].astype(F32)
    projected[pl.ds(1 - spin, 1)] = received.reshape(1, 2 * T, T)


def whole(shape):
    return pl.BlockSpec(shape, lambda i, m, n=len(shape): (0,) * n)


def call(kernel, m, arrays, outs, name, flops=0, specs=None, scratch=()):
    arrays = list(arrays)
    moved = sum(a.size * a.dtype.itemsize for a in [*arrays, *outs])
    return pl.pallas_call(
        kernel,
        out_shape=outs,
        grid_spec=pltpu.PrefetchScalarGridSpec(
            num_scalar_prefetch=1,
            grid=(1,),
            in_specs=specs or [whole(a.shape) for a in arrays],
            out_specs=[whole(o.shape) for o in outs],
            scratch_shapes=list(scratch),
        ),
        compiler_params=pltpu.CompilerParams(vmem_limit_bytes=32 * 1024 * 1024),
        cost_estimate=pl.CostEstimate(flops=2 * T * T * 2 * T * flops, bytes_accessed=moved, transcendentals=0),
        name=name,
    )(m, *arrays)


def table(neighbour_index, block_count):
    gx, gy, col = (lax.axis_index(a) for a in AXES)
    spin = col ^ ((gx >> 1) & 1)
    toward = jnp.where(gx % 2 == 0, 1, -1)
    dx = jnp.stack([jnp.zeros_like(toward), toward, -toward])
    codes = (dx[:, None] + 1) * 3 + jnp.arange(3, dtype=jnp.int32)[None, :]
    slots = jnp.arange(NB, dtype=jnp.int32)
    index, count = neighbour_index[0], block_count[0]
    match = (index[:, None, None, :] == codes[None, :, :, None]) & (
        slots < count[:, None, None, None]
    )
    found = jnp.sum(jnp.where(match, slots + 1, 0), axis=-1) - 1
    scalars = jnp.stack([spin, col, gy % 2, gx % 2])
    return spin, col, jnp.concatenate([found.reshape(-1), scalars]).astype(jnp.int32)


def shaped(shape, dtype):
    return jax.ShapeDtypeStruct(shape, dtype)


def per_device(start_block, hamiltonian, neighbour_index, block_count):
    sizes = tuple(lax.axis_size(a) for a in AXES)
    members = sizes[0] * sizes[1]
    block, full = (4, T, 2 * T), (2 * T, 2 * T)
    spin, col, m = table(neighbour_index, block_count)

    other = swap_col(sizes, lax.dynamic_index_in_dim(start_block, 1 - spin, 0, keepdims=False)[0])
    own = lax.dynamic_index_in_dim(start_block, spin, 0, keepdims=False)[0]
    spin_block = pl.BlockSpec((1,) + hamiltonian.shape[1:], lambda i, m: (m[SPIN], 0, 0, 0, 0, 0))
    (o,) = call(order_kernel, m, [hamiltonian], [shaped((4, T, NB * T), BF)], "order", specs=[spin_block])
    tile, middle = shaped((1, T, 2 * T), BF), shaped((3, T, 2 * T), BF)
    parts = [shaped(block, BF), middle, tile, tile]
    ext = pltpu.VMEM((6, T, 2 * T), BF)
    v, mid, p, q = call(join_kernel, m, [own, other], parts, "join")

    def apply_ham(o, x, mid, p, q, before):
        last = before is not None
        p, q = swap(sizes, p, 0, 1), swap(sizes, q, 0, 2)
        ends = jnp.concatenate([p, x[:1], q], axis=0)
        a, b = swap(sizes, mid, 1, 0), swap(sizes, mid, 2, 0)
        o, a, b = lax.optimization_barrier((o, a, b))
        a_ends, b_ends = swap(sizes, ends, 1, 0), swap(sizes, ends, 2, 0)
        (acc,) = call(core_kernel, m, [o, mid, ends, a, b], [shaped(block, F32)], "core", 28, scratch=[ext])
        arrays = [o, a_ends, b_ends, acc] + ([before] if last else [])
        outs = [shaped(block, BF), tile, tile] if last else parts
        return o, call(functools.partial(rim_kernel, last=last), m, arrays, outs, "rim", 8)

    o, (first, mid, p, q) = apply_ham(o, v, mid, p, q, None)
    o, (second, low, high) = apply_ham(o, first, mid, p, q, v)

    above = shift(sizes, low, 0, -1)
    right_high = shift(sizes, low, -1, -1)
    right_low = shift(sizes, high, -1, 1)
    right = shift(sizes, second, -1, 0)
    corr, acc = call(corr_kernel, m, [o, second], [shaped(full, F32), shaped(block, F32)], "corr", 15)
    piece = shaped((members // 2, 1, 5 * T), F32)
    mine, theirs = call(
        gram_kernel, m, [o, second, above, right_low, right, right_high, acc, corr], [piece, piece], "gram", 29,
        scratch=[ext],
    )

    rows = members * second.shape[0] * second.shape[1]
    partial = mine + swap(sizes, theirs, 0, 1)
    total = exchange(sizes, partial).sum(axis=0, keepdims=True) / rows
    mine = exchange(sizes, jnp.broadcast_to(total, partial.shape))
    theirs = swap(sizes, mine, 0, 1)

    keep, p_keep, send = call(
        final_kernel, m, [mine, theirs, second],
        [shaped((4, T, T), BF), shaped((2 * T, T), F32), shaped((8, T, T), BF)], "final", 80,
        scratch=[pltpu.VMEM(full, F32), pltpu.VMEM(full, F32)],
    )
    got = swap_col(sizes, send)
    ritz = shaped((2, 1, 4, T, T), BF)
    return tuple(
        call(assemble_kernel, m, [keep, p_keep, got], [ritz, shaped((2, 2 * T, T), F32)], "assemble")
    )


def solution(mesh):
    return jax.shard_map(
        per_device,
        mesh=mesh,
        in_specs=(
            P(None, "gx", "gy", None, "col"),
            P(None, "gx", "gy", None, None, None),
            P("gx", "gy", None),
            P("gx", "gy"),
        ),
        out_specs=(P(None, "gx", "gy", None, "col"), P(None, None, "col")),
        check_vma=False,
    )
```

```python
import functools

import jax
import jax.numpy as jnp
from jax import lax
from jax.experimental import pallas as pl
from jax.experimental.pallas import tpu as pltpu
from jax.sharding import PartitionSpec as P

NB = 9
T = 128
AXES = ("gx", "gy", "col")
BF = jnp.bfloat16
F32 = jnp.float32
SPIN, COL, PAR_Y, PAR_X = 36, 37, 38, 39


def col_of(gx, spin):
    return spin ^ ((gx >> 1) & 1)


def device(sizes, gx, gy, col):
    return ((gx % sizes[0]) * sizes[1] + gy % sizes[1]) * sizes[2] + col


def pairs(sizes, target):
    out = []
    for gx in range(sizes[0]):
        for gy in range(sizes[1]):
            for spin in range(2):
                there = target(gx, gy)
                there_gx = there[0] % sizes[0]
                out.append(
                    (
                        device(sizes, gx, gy, col_of(gx, spin)),
                        device(sizes, there_gx, there[1], col_of(there_gx, spin)),
                    )
                )
    return out


def partner(index, kind):
    if kind == 0:
        return index
    return index + 1 if (index % 2 == 0) == (kind == 1) else index - 1


def swap(sizes, block, kind_x, kind_y):
    perm = pairs(sizes, lambda gx, gy: (partner(gx, kind_x), partner(gy, kind_y)))
    return lax.ppermute(block, AXES, perm)


def shift(sizes, block, dx, dy):
    return lax.ppermute(block, AXES, pairs(sizes, lambda gx, gy: (gx + dx, gy + dy)))


def swap_col(sizes, block):
    perm = [(d, d ^ 1) for d in range(sizes[0] * sizes[1] * 2)]
    return lax.ppermute(block, AXES, perm)


def exchange(sizes, pieces):
    groups = [
        [
            device(sizes, gx, gy, col_of(gx, spin))
            for gx in range(sizes[0])
            for gy in range(core, sizes[1], 2)
        ]
        for spin in range(2)
        for core in range(2)
    ]
    return lax.all_to_all(pieces, AXES, 0, 0, axis_index_groups=groups, tiled=True)


def dot(a, b, dims=((1,), (0,))):
    return lax.dot_general(a, b, (dims, ((), ())), preferred_element_type=F32)


def split(a):
    high = a.astype(BF)
    return high, (a - high.astype(F32)).astype(BF)


def dot3(a, b, dims=((1,), (0,))):
    (ah, al), (bh, bl) = split(a), split(b)
    return dot(ah, bh, dims) + (dot(ah, bl, dims) + dot(al, bh, dims))


def order_kernel(m, h, o):
    for tile in range(4):
        for at in range(9):
            slot = m[tile * 9 + at]
            block = h[0, 0, tile, jnp.maximum(slot, 0)]
            o[tile, :, at * T : (at + 1) * T] = jnp.where(slot >= 0, block, jnp.zeros_like(block))


def blocks(o, tile, sides, dys):
    out = []
    for side in sides:
        at = (side * 3 + dys[0]) * T
        if not isinstance(side, int):
            at = pl.multiple_of(at, T)
        out.append(o[tile, :, pl.ds(at, len(dys) * T)])
    return out[0] if len(out) == 1 else jnp.concatenate(out, axis=1)


def store_edges(m, ref, p, q):
    even = m[PAR_Y] == 0
    p[...] = ref[pl.ds(jnp.where(even, 3, 0), 1)]
    q[0:1] = ref[pl.ds(jnp.where(even, 0, 3), 1)]
    q[1:2] = ref[1:2]


def join_kernel(m, own, other, v, p, q):
    first_col = m[COL] == 0
    v[:, :, :T] = jnp.where(first_col, own[...], other[...])
    v[:, :, T:] = jnp.where(first_col, other[...], own[...])
    store_edges(m, v, p, q)


def ends_of(m, ends):
    even = m[PAR_Y] == 0
    return jnp.where(even, ends[1:2], ends[0:1]), jnp.where(even, ends[0:1], ends[1:2])


def product(o, tile, sides, at, sources):
    row = blocks(o, tile, sides, [place - tile for place in at])
    return dot(row, jnp.concatenate([x.reshape(len(at) * T, 2 * T) for x in sources], axis=0))


def core_kernel(m, o, x, ends, a, b, acc, ext):
    low, high = ends_of(m, ends)
    ext[0:1] = low
    ext[1:5] = x[...]
    ext[5:6] = high
    for tile in range(4):
        total = product(o, tile, (0,), range(tile, tile + 3), [ext[tile : tile + 3]])
        at = [place for place in range(tile, tile + 3) if 1 <= place <= 4]
        sources = [y[at[0] - 1 : at[-1]] for y in (a, b)]
        acc[tile] = total + product(o, tile, (1, 2), at, sources)


def rim_kernel(m, o, a_ends, b_ends, acc, *rest, last):
    if last:
        before, out, first_out, last_out = rest
    else:
        out, p, q = rest
    low, high = zip(ends_of(m, a_ends), ends_of(m, b_ends))
    for tile in range(4):
        total = acc[tile]
        if tile == 0:
            total += product(o, tile, (1, 2), (0,), low)
        if tile == 3:
            total += product(o, tile, (1, 2), (5,), high)
        if last:
            out[tile] = (total - before[tile].astype(F32)).astype(BF)
        else:
            out[tile] = (0.5 * total).astype(BF)
    if last:
        first_out[...] = out[0:1]
        last_out[...] = out[3:4]
    else:
        store_edges(m, out, p, q)


def corr_kernel(m, o, s, corr, turned, acc):
    flat = s[...].reshape(4 * T, 2 * T)
    turned[...] = flat.T
    corr[...] = dot(turned[...], flat)
    for tile in range(4):
        total = 0.5 * dot(blocks(o, tile, (0,), (1,)), s[tile])
        if tile < 3:
            total += dot(blocks(o, tile, (0,), (2,)), s[tile + 1])
        acc[tile] = total


def places():
    shape = (2 * T, 2 * T)
    return lax.broadcasted_iota(jnp.int32, shape, 0), lax.broadcasted_iota(jnp.int32, shape, 1)


def gram_kernel(m, o, turned, above, right_low, right, right_high, acc, corr, mine, theirs, ext):
    ext[0:1] = right_low[...]
    ext[1:5] = right[...]
    ext[5:6] = right_high[...]
    side = 1 + m[PAR_X]
    parts = []
    for tile in range(4):
        part = acc[tile] + product(o, tile, (side,), range(tile, tile + 3), [ext[tile : tile + 3]])
        if tile == 3:
            part += product(o, tile, (0,), (5,), [above[...]])
        parts.append(part)
    high, low = split(jnp.concatenate(parts, axis=0))
    half = dot(turned[...], high) + dot(turned[...], low)
    coupling = half + half.T
    rows, cols = places()
    both = jnp.where(rows >= cols, corr[...], coupling)
    diagonal = jnp.sum(jnp.where(rows == cols, coupling, 0.0), axis=1, keepdims=True)
    first, second = pack(both[:T], diagonal[:T]), pack(both[T:], diagonal[T:])
    even = m[PAR_Y] == 0
    mine[:, 0, :] = jnp.where(even, first, second)
    theirs[:, 0, :] = jnp.where(even, second, first)


def pack(square, diagonal):
    lane = lax.broadcasted_iota(jnp.int32, (T // 2, T), 1)
    extra = jnp.where(lane == 0, diagonal[: T // 2], jnp.where(lane == 1, diagonal[T // 2 :], 0.0))
    return jnp.concatenate([square[: T // 2], square[T // 2 :], extra], axis=1)


def unpack(table):
    square = jnp.concatenate([table[:, : 2 * T], table[:, 2 * T : 4 * T]], axis=0)
    return square, jnp.concatenate([table[:, 4 * T : 4 * T + 1], table[:, 4 * T + 1 : 4 * T + 2]], axis=0)


def lower_part(e, rows, cols):
    return jnp.where(rows > cols, e, jnp.where(rows == cols, 0.5 * e, 0.0))


def square_of(m, mine, theirs):
    even = m[PAR_Y] == 0
    first, second = mine[:, 0, :], theirs[:, 0, :]
    top = unpack(jnp.where(even, first, second))
    bottom = unpack(jnp.where(even, second, first))
    return jnp.concatenate([top[0], bottom[0]], axis=0), jnp.concatenate([top[1], bottom[1]], axis=0)


def inverse_kernel(m, mine, theirs, s, keep, send, x_out, x_ref, a_ref):
    rows, cols = places()
    both, _ = square_of(m, mine, theirs)
    turned = both.T
    corr = jnp.where(rows >= cols, both, turned)
    on_diagonal = jnp.where(rows == cols, corr, 0.0)
    scale_row = 1.0 / jnp.sqrt(jnp.sum(on_diagonal, axis=0, keepdims=True))
    scale_col = 1.0 / jnp.sqrt(jnp.sum(on_diagonal, axis=1, keepdims=True))
    scaled = corr * scale_row * scale_col
    unit = (rows == cols).astype(F32)

    a_ref[...] = scaled
    x_ref[...] = unit - lower_part(scaled - unit, rows, cols)

    def step(state):
        count, _ = state
        x = x_ref[...]
        e = dot3(dot3(x, a_ref[...]), x, ((1,), (1,))) - unit
        x_ref[...] = x - dot3(lower_part(e, rows, cols), x)
        return count + 1, jnp.sum(e * e)

    def more(state):
        count, size = state
        return (count < 12) & (size >= 4e-6) & (size < 1e4)

    _, size = lax.while_loop(more, step, (0, F32(1.0)))

    @pl.when(jnp.logical_not(size < 4e-6))
    def _():
        a_ref[...] = scaled
        x_ref[...] = unit

        def eliminate(j, carry):
            row = a_ref[pl.ds(j, 1), :]
            pivot = jnp.sum(jnp.where(cols[:1] == j, row, 0.0), axis=1, keepdims=True)
            a = a_ref[...]
            column = jnp.sum(jnp.where(cols == j, a, 0.0), axis=1, keepdims=True)
            factor = jnp.where(rows[:, :1] > j, column / pivot, 0.0)
            x = x_ref[...]
            x_row = x_ref[pl.ds(j, 1), :]
            a_ref[...] = a - factor * row
            x_ref[...] = x - factor * x_row
            return carry

        lax.fori_loop(0, 2 * T, eliminate, 0)
        pivots = jnp.sum(jnp.where(rows == cols, a_ref[...], 0.0), axis=1, keepdims=True)
        x_ref[...] = x_ref[...] / jnp.sqrt(pivots)

    x = x_ref[...] * scale_row
    x_out[...] = x
    ritz = dot(s[...].reshape(4 * T, 2 * T), x.astype(BF), ((1,), (1,))).astype(BF)
    ritz = ritz.reshape(4, T, 2 * T)
    first_col = m[COL] == 0
    keep[...] = jnp.where(first_col, ritz[:, :, :T], ritz[:, :, T:])
    send[...] = jnp.where(first_col, ritz[:, :, T:], ritz[:, :, :T])


def project_kernel(m, mine, theirs, x_ref, keep, send):
    rows, cols = places()
    both, diagonal = square_of(m, mine, theirs)
    coupling = jnp.where(rows < cols, both, jnp.where(rows == cols, diagonal, both.T))
    x = x_ref[...]
    projected = dot3(dot3(x, coupling), x, ((1,), (1,)))
    first_col = m[COL] == 0
    keep[...] = jnp.where(first_col, projected[:, :T], projected[:, T:])
    send[...] = jnp.where(first_col, projected[:, T:], projected[:, :T]).astype(BF)


def whole(shape):
    return pl.BlockSpec(shape, lambda i, m, n=len(shape): (0,) * n)


def call(kernel, m, arrays, outs, name, flops=0, specs=None, scratch=()):
    arrays = list(arrays)
    moved = sum(a.size * a.dtype.itemsize for a in [*arrays, *outs])
    return pl.pallas_call(
        kernel,
        out_shape=outs,
        grid_spec=pltpu.PrefetchScalarGridSpec(
            num_scalar_prefetch=1,
            grid=(1,),
            in_specs=specs or [whole(a.shape) for a in arrays],
            out_specs=[whole(o.shape) for o in outs],
            scratch_shapes=list(scratch),
        ),
        compiler_params=pltpu.CompilerParams(vmem_limit_bytes=32 * 1024 * 1024),
        cost_estimate=pl.CostEstimate(flops=2 * T * T * 2 * T * flops, bytes_accessed=moved, transcendentals=0),
        name=name,
    )(m, *arrays)


def table(neighbour_index, block_count):
    gx, gy, col = (lax.axis_index(a) for a in AXES)
    spin = col ^ ((gx >> 1) & 1)
    toward = jnp.where(gx % 2 == 0, 1, -1)
    dx = jnp.stack([jnp.zeros_like(toward), toward, -toward])
    codes = (dx[:, None] + 1) * 3 + jnp.arange(3, dtype=jnp.int32)[None, :]
    slots = jnp.arange(NB, dtype=jnp.int32)
    index, count = neighbour_index[0], block_count[0]
    match = (index[:, None, None, :] == codes[None, :, :, None]) & (
        slots < count[:, None, None, None]
    )
    found = jnp.sum(jnp.where(match, slots + 1, 0), axis=-1) - 1
    scalars = jnp.stack([spin, col, gy % 2, gx % 2])
    return spin, col, jnp.concatenate([found.reshape(-1), scalars]).astype(jnp.int32)


def shaped(shape, dtype):
    return jax.ShapeDtypeStruct(shape, dtype)


def per_device(start_block, hamiltonian, neighbour_index, block_count):
    sizes = tuple(lax.axis_size(a) for a in AXES)
    members = sizes[0] * sizes[1]
    block, full = (4, T, 2 * T), (2 * T, 2 * T)
    spin, col, m = table(neighbour_index, block_count)

    other = swap_col(sizes, lax.dynamic_index_in_dim(start_block, 1 - spin, 0, keepdims=False)[0])
    own = lax.dynamic_index_in_dim(start_block, spin, 0, keepdims=False)[0]
    spin_block = pl.BlockSpec((1,) + hamiltonian.shape[1:], lambda i, m: (m[SPIN], 0, 0, 0, 0, 0))
    (o,) = call(order_kernel, m, [hamiltonian], [shaped((4, T, NB * T), BF)], "order", specs=[spin_block])
    tile = shaped((1, T, 2 * T), BF)
    parts = [shaped(block, BF), tile, shaped((2, T, 2 * T), BF)]
    ext = pltpu.VMEM((6, T, 2 * T), BF)
    v, p, q = call(join_kernel, m, [own, other], parts, "join")

    def apply_ham(o, x, p, q, before):
        last = before is not None
        p, q = swap(sizes, p, 0, 1), swap(sizes, q, 0, 2)
        ends = jnp.concatenate([p, q[:1]], axis=0)
        a, b = swap(sizes, x, 1, 0), swap(sizes, x, 2, 0)
        o, a, b = lax.optimization_barrier((o, a, b))
        a_ends, b_ends = swap(sizes, ends, 1, 0), swap(sizes, ends, 2, 0)
        (acc,) = call(core_kernel, m, [o, x, ends, a, b], [shaped(block, F32)], "core", 32, scratch=[ext])
        arrays = [o, a_ends, b_ends, acc] + ([before] if last else [])
        outs = [shaped(block, BF), tile, tile] if last else parts
        return o, call(functools.partial(rim_kernel, last=last), m, arrays, outs, "rim", 4)

    o, (first, p, q) = apply_ham(o, v, p, q, None)
    o, (second, low, high) = apply_ham(o, first, p, q, v)

    above = shift(sizes, low, 0, -1)
    right_high = shift(sizes, low, -1, -1)
    right_low = shift(sizes, high, -1, 1)
    right = shift(sizes, second, -1, 0)
    corr, turned, acc = call(
        corr_kernel, m, [o, second], [shaped(full, F32), shaped((2 * T, 4 * T), BF), shaped(block, F32)], "corr", 15
    )
    piece = shaped((members // 2, 1, 5 * T), F32)
    mine, theirs = call(
        gram_kernel, m, [o, turned, above, right_low, right, right_high, acc, corr], [piece, piece], "gram", 29,
        scratch=[ext],
    )

    rows = members * second.shape[0] * second.shape[1]
    partial = mine + swap(sizes, theirs, 0, 1)
    total = exchange(sizes, partial).sum(axis=0, keepdims=True) / rows
    mine = exchange(sizes, jnp.broadcast_to(total, partial.shape))
    theirs = swap(sizes, mine, 0, 1)

    half = (4, T, T)
    keep, send, x = call(
        inverse_kernel, m, [mine, theirs, second],
        [shaped(half, BF), shaped(half, BF), shaped(full, F32)], "inverse", 80,
        scratch=[pltpu.VMEM(full, F32), pltpu.VMEM(full, F32)],
    )
    got = swap_col(sizes, send)
    p_shape = (2 * T, T)
    p_keep, p_send = call(
        project_kernel, m, [mine, theirs, x], [shaped(p_shape, F32), shaped(p_shape, BF)], "project", 24
    )
    p_got = swap_col(sizes, p_send).astype(F32)
    ritz = jnp.where(spin == 0, jnp.stack([keep, got]), jnp.stack([got, keep]))
    projected = jnp.where(spin == 0, jnp.stack([p_keep, p_got]), jnp.stack([p_got, p_keep]))
    return ritz[:, None], projected


def solution(mesh):
    return jax.shard_map(
        per_device,
        mesh=mesh,
        in_specs=(
            P(None, "gx", "gy", None, "col"),
            P(None, "gx", "gy", None, None, None),
            P("gx", "gy", None),
            P("gx", "gy"),
        ),
        out_specs=(P(None, "gx", "gy", None, "col"), P(None, None, "col")),
        check_vma=False,
    )
```

```python
import jax
import jax.numpy as jnp
from jax import lax
from jax.experimental import pallas as pl
from jax.experimental.pallas import tpu as pltpu
from jax.sharding import PartitionSpec as P

NB = 9
T = 128
AXES = ("gx", "gy", "col")
BF = jnp.bfloat16
F32 = jnp.float32
SPIN, COL, PAR_Y, PAR_X = 36, 37, 38, 39


def col_of(gx, spin):
    return spin ^ ((gx >> 1) & 1)


def device(sizes, gx, gy, col):
    return ((gx % sizes[0]) * sizes[1] + gy % sizes[1]) * sizes[2] + col


def pairs(sizes, target):
    out = []
    for gx in range(sizes[0]):
        for gy in range(sizes[1]):
            for spin in range(2):
                there = target(gx, gy)
                there_gx = there[0] % sizes[0]
                out.append(
                    (
                        device(sizes, gx, gy, col_of(gx, spin)),
                        device(sizes, there_gx, there[1], col_of(there_gx, spin)),
                    )
                )
    return out


def partner(index, kind):
    if kind == 0:
        return index
    return index + 1 if (index % 2 == 0) == (kind == 1) else index - 1


def swap(sizes, block, kind_x, kind_y):
    perm = pairs(sizes, lambda gx, gy: (partner(gx, kind_x), partner(gy, kind_y)))
    return lax.ppermute(block, AXES, perm)


def shift(sizes, block, dx, dy):
    return lax.ppermute(block, AXES, pairs(sizes, lambda gx, gy: (gx + dx, gy + dy)))


def swap_col(sizes, block):
    perm = [(d, d ^ 1) for d in range(sizes[0] * sizes[1] * 2)]
    return lax.ppermute(block, AXES, perm)


def exchange(sizes, pieces):
    groups = [
        [
            device(sizes, gx, gy, col_of(gx, spin))
            for gx in range(sizes[0])
            for gy in range(core, sizes[1], 2)
        ]
        for spin in range(2)
        for core in range(2)
    ]
    return lax.all_to_all(pieces, AXES, 0, 0, axis_index_groups=groups, tiled=True)


def dot(a, b, dims=((1,), (0,))):
    return lax.dot_general(a, b, (dims, ((), ())), preferred_element_type=F32)


def split(a):
    high = a.astype(BF)
    return high, (a - high.astype(F32)).astype(BF)


def dot3(a, b, dims=((1,), (0,))):
    (ah, al), (bh, bl) = split(a), split(b)
    return dot(ah, bh, dims) + (dot(ah, bl, dims) + dot(al, bh, dims))


def order_kernel(m, h, o, p, q):
    def block(tile, at):
        slot = m[tile * 9 + at]
        found = h[0, 0, tile, jnp.maximum(slot, 0)]
        return jnp.where(slot >= 0, found, jnp.zeros_like(found))

    for tile in range(4):
        for at in range(9):
            o[tile, :, at * T : (at + 1) * T] = block(tile, at)
    even = m[PAR_Y] == 0
    side = 1 + m[PAR_X]
    down, up = block(0, side * 3), block(3, side * 3 + 2)
    p[...] = jnp.where(even, up, down)
    q[...] = jnp.where(even, down, up)


def blocks(o, tile, sides, dys):
    out = []
    for side in sides:
        at = (side * 3 + dys[0]) * T
        if not isinstance(side, int):
            at = pl.multiple_of(at, T)
        out.append(o[tile, :, pl.ds(at, len(dys) * T)])
    return out[0] if len(out) == 1 else jnp.concatenate(out, axis=1)


def store_edges(m, ref, p, q):
    even = m[PAR_Y] == 0
    p[...] = ref[pl.ds(jnp.where(even, 3, 0), 1)]
    q[0:1] = ref[pl.ds(jnp.where(even, 0, 3), 1)]
    q[1:2] = ref[1:2]


def join_kernel(m, own, other, v, p, q):
    first_col = m[COL] == 0
    v[:, :, :T] = jnp.where(first_col, own[...], other[...])
    v[:, :, T:] = jnp.where(first_col, other[...], own[...])
    store_edges(m, v, p, q)


def ends_of(m, ends):
    even = m[PAR_Y] == 0
    return jnp.where(even, ends[1:2], ends[0:1]), jnp.where(even, ends[0:1], ends[1:2])


def product(o, tile, sides, at, sources):
    row = blocks(o, tile, sides, [place - tile for place in at])
    return dot(row, jnp.concatenate([x.reshape(len(at) * T, 2 * T) for x in sources], axis=0))


def core_kernel(m, o, x, ends, a, b, acc, ext):
    low, high = ends_of(m, ends)
    ext[0:1] = low
    ext[1:5] = x[...]
    ext[5:6] = high
    for tile in range(4):
        total = product(o, tile, (0,), range(tile, tile + 3), [ext[tile : tile + 3]])
        at = [place for place in range(tile, tile + 3) if 1 <= place <= 4]
        sources = [y[at[0] - 1 : at[-1]] for y in (a, b)]
        acc[tile] = total + product(o, tile, (1, 2), at, sources)


def rim_kernel(m, o, a_ends, b_ends, acc, *rest):
    *before, out, p, q = rest
    low, high = zip(ends_of(m, a_ends), ends_of(m, b_ends))
    for tile in range(4):
        total = acc[tile]
        if tile == 0:
            total += product(o, tile, (1, 2), (0,), low)
        if tile == 3:
            total += product(o, tile, (1, 2), (5,), high)
        if before:
            out[tile] = (total - before[0][tile].astype(F32)).astype(BF)
        else:
            out[tile] = (0.5 * total).astype(BF)
    store_edges(m, out, p, q)


def corr_kernel(m, o, s, p, q, corr, turned, acc):
    flat = s[...].reshape(4 * T, 2 * T)
    turned[:, : 4 * T] = flat.T
    turned[:, 4 * T : 5 * T] = p[0].T
    turned[:, 5 * T :] = q[0].T
    corr[...] = dot(turned[:, : 4 * T], flat)
    above = jnp.where(m[PAR_Y] == 0, p[0], q[0])
    for tile in range(4):
        total = 0.5 * dot(blocks(o, tile, (0,), (1,)), s[tile])
        acc[tile] = total + dot(blocks(o, tile, (0,), (2,)), s[tile + 1] if tile < 3 else above)


def places():
    shape = (2 * T, 2 * T)
    return lax.broadcasted_iota(jnp.int32, shape, 0), lax.broadcasted_iota(jnp.int32, shape, 1)


def gram_kernel(m, o, turned, right, h_p, h_q, acc, corr, mine, theirs):
    side = 1 + m[PAR_X]
    parts = []
    for tile in range(4):
        at = [place for place in range(tile, tile + 3) if 1 <= place <= 4]
        parts.append(acc[tile] + product(o, tile, (side,), at, [right[at[0] - 1 : at[-1]]]))
    even = m[PAR_Y] == 0
    parts.append(dot(h_p[...], right[jnp.where(even, 3, 0)]))
    parts.append(dot(h_q[...], right[jnp.where(even, 0, 3)]))
    high, low = split(jnp.concatenate(parts, axis=0))
    half = dot(turned[...], high) + dot(turned[...], low)
    coupling = half + half.T
    rows, cols = places()
    both = jnp.where(rows >= cols, corr[...], coupling)
    diagonal = jnp.sum(jnp.where(rows == cols, coupling, 0.0), axis=1, keepdims=True)
    first, second = pack(both[:T], diagonal[:T]), pack(both[T:], diagonal[T:])
    even = m[PAR_Y] == 0
    mine[:, 0, :] = jnp.where(even, first, second)
    theirs[:, 0, :] = jnp.where(even, second, first)


def pack(square, diagonal):
    lane = lax.broadcasted_iota(jnp.int32, (T // 2, T), 1)
    extra = jnp.where(lane == 0, diagonal[: T // 2], jnp.where(lane == 1, diagonal[T // 2 :], 0.0))
    return jnp.concatenate([square[: T // 2], square[T // 2 :], extra], axis=1)


def unpack(table):
    square = jnp.concatenate([table[:, : 2 * T], table[:, 2 * T : 4 * T]], axis=0)
    return square, jnp.concatenate([table[:, 4 * T : 4 * T + 1], table[:, 4 * T + 1 : 4 * T + 2]], axis=0)


def lower_part(e, rows, cols):
    return jnp.where(rows > cols, e, jnp.where(rows == cols, 0.5 * e, 0.0))


def square_of(m, mine, theirs):
    even = m[PAR_Y] == 0
    first, second = mine[:, 0, :], theirs[:, 0, :]
    top = unpack(jnp.where(even, first, second))
    bottom = unpack(jnp.where(even, second, first))
    return jnp.concatenate([top[0], bottom[0]], axis=0), jnp.concatenate([top[1], bottom[1]], axis=0)


def inverse_kernel(m, mine, theirs, s, keep, send, x_out, x_ref, a_ref):
    rows, cols = places()
    both, _ = square_of(m, mine, theirs)
    turned = both.T
    corr = jnp.where(rows >= cols, both, turned)
    on_diagonal = jnp.where(rows == cols, corr, 0.0)
    scale_row = 1.0 / jnp.sqrt(jnp.sum(on_diagonal, axis=0, keepdims=True))
    scale_col = 1.0 / jnp.sqrt(jnp.sum(on_diagonal, axis=1, keepdims=True))
    scaled = corr * scale_row * scale_col
    unit = (rows == cols).astype(F32)

    a_ref[...] = scaled
    x_ref[...] = unit - lower_part(scaled - unit, rows, cols)

    def step(state):
        count, _ = state
        x = x_ref[...]
        e = dot3(dot3(x, a_ref[...]), x, ((1,), (1,))) - unit
        x_ref[...] = x - dot3(lower_part(e, rows, cols), x)
        return count + 1, jnp.sum(e * e)

    def more(state):
        count, size = state
        return (count < 12) & (size >= 4e-6) & (size < 1e4)

    _, size = lax.while_loop(more, step, (0, F32(1.0)))

    @pl.when(jnp.logical_not(size < 4e-6))
    def _():
        a_ref[...] = scaled
        x_ref[...] = unit

        def eliminate(j, carry):
            row = a_ref[pl.ds(j, 1), :]
            pivot = jnp.sum(jnp.where(cols[:1] == j, row, 0.0), axis=1, keepdims=True)
            a = a_ref[...]
            column = jnp.sum(jnp.where(cols == j, a, 0.0), axis=1, keepdims=True)
            factor = jnp.where(rows[:, :1] > j, column / pivot, 0.0)
            x = x_ref[...]
            x_row = x_ref[pl.ds(j, 1), :]
            a_ref[...] = a - factor * row
            x_ref[...] = x - factor * x_row
            return carry

        lax.fori_loop(0, 2 * T, eliminate, 0)
        pivots = jnp.sum(jnp.where(rows == cols, a_ref[...], 0.0), axis=1, keepdims=True)
        x_ref[...] = x_ref[...] / jnp.sqrt(pivots)

    x = x_ref[...] * scale_row
    x_out[...] = x
    ritz = dot(s[...].reshape(4 * T, 2 * T), x.astype(BF), ((1,), (1,))).astype(BF)
    ritz = ritz.reshape(4, T, 2 * T)
    first_col = m[COL] == 0
    keep[...] = jnp.where(first_col, ritz[:, :, :T], ritz[:, :, T:])
    send[...] = jnp.where(first_col, ritz[:, :, T:], ritz[:, :, :T])


def project_kernel(m, mine, theirs, x_ref, keep, send):
    rows, cols = places()
    both, diagonal = square_of(m, mine, theirs)
    coupling = jnp.where(rows < cols, both, jnp.where(rows == cols, diagonal, both.T))
    x = x_ref[...]
    projected = dot3(dot3(x, coupling), x, ((1,), (1,)))
    first_col = m[COL] == 0
    keep[...] = jnp.where(first_col, projected[:, :T], projected[:, T:])
    send[...] = jnp.where(first_col, projected[:, T:], projected[:, :T]).astype(BF)


def whole(shape):
    return pl.BlockSpec(shape, lambda i, m, n=len(shape): (0,) * n)


def call(kernel, m, arrays, outs, name, flops=0, specs=None, scratch=()):
    arrays = list(arrays)
    moved = sum(a.size * a.dtype.itemsize for a in [*arrays, *outs])
    return pl.pallas_call(
        kernel,
        out_shape=outs,
        grid_spec=pltpu.PrefetchScalarGridSpec(
            num_scalar_prefetch=1,
            grid=(1,),
            in_specs=specs or [whole(a.shape) for a in arrays],
            out_specs=[whole(o.shape) for o in outs],
            scratch_shapes=list(scratch),
        ),
        compiler_params=pltpu.CompilerParams(vmem_limit_bytes=32 * 1024 * 1024),
        cost_estimate=pl.CostEstimate(flops=2 * T * T * 2 * T * flops, bytes_accessed=moved, transcendentals=0),
        name=name,
    )(m, *arrays)


def table(neighbour_index, block_count):
    gx, gy, col = (lax.axis_index(a) for a in AXES)
    spin = col ^ ((gx >> 1) & 1)
    toward = jnp.where(gx % 2 == 0, 1, -1)
    dx = jnp.stack([jnp.zeros_like(toward), toward, -toward])
    codes = (dx[:, None] + 1) * 3 + jnp.arange(3, dtype=jnp.int32)[None, :]
    slots = jnp.arange(NB, dtype=jnp.int32)
    index, count = neighbour_index[0], block_count[0]
    match = (index[:, None, None, :] == codes[None, :, :, None]) & (
        slots < count[:, None, None, None]
    )
    found = jnp.sum(jnp.where(match, slots + 1, 0), axis=-1) - 1
    scalars = jnp.stack([spin, col, gy % 2, gx % 2])
    return spin, col, jnp.concatenate([found.reshape(-1), scalars]).astype(jnp.int32)


def shaped(shape, dtype):
    return jax.ShapeDtypeStruct(shape, dtype)


def per_device(start_block, hamiltonian, neighbour_index, block_count):
    sizes = tuple(lax.axis_size(a) for a in AXES)
    members = sizes[0] * sizes[1]
    block, full = (4, T, 2 * T), (2 * T, 2 * T)
    spin, col, m = table(neighbour_index, block_count)

    other = swap_col(sizes, lax.dynamic_index_in_dim(start_block, 1 - spin, 0, keepdims=False)[0])
    own = lax.dynamic_index_in_dim(start_block, spin, 0, keepdims=False)[0]
    spin_block = pl.BlockSpec((1,) + hamiltonian.shape[1:], lambda i, m: (m[SPIN], 0, 0, 0, 0, 0))
    corner = shaped((T, T), BF)
    o, h_p, h_q = call(
        order_kernel, m, [hamiltonian], [shaped((4, T, NB * T), BF), corner, corner], "order", specs=[spin_block]
    )
    h_p, h_q = swap(sizes, h_p, 0, 1), swap(sizes, h_q, 0, 2)
    tile = shaped((1, T, 2 * T), BF)
    parts = [shaped(block, BF), tile, shaped((2, T, 2 * T), BF)]
    ext = pltpu.VMEM((6, T, 2 * T), BF)
    v, p, q = call(join_kernel, m, [own, other], parts, "join")

    def apply_ham(o, x, p, q, before, *kept):
        p, q = swap(sizes, p, 0, 1), swap(sizes, q, 0, 2)
        ends = jnp.concatenate([p, q[:1]], axis=0)
        a, b = swap(sizes, x, 1, 0), swap(sizes, x, 2, 0)
        o, a, b = lax.optimization_barrier((o, a, b))
        a_ends, b_ends = swap(sizes, ends, 1, 0), swap(sizes, ends, 2, 0)
        (acc,) = call(core_kernel, m, [o, x, ends, a, b], [shaped(block, F32)], "core", 32, scratch=[ext])
        acc, *kept = lax.optimization_barrier((acc, *kept))
        out = call(rim_kernel, m, [o, a_ends, b_ends, acc, *before], parts, "rim", 4)
        return o, kept, out

    o, _, (first, p, q) = apply_ham(o, v, p, q, [])
    o, (h_p, h_q), (second, p, q) = apply_ham(o, first, p, q, [v], h_p, h_q)

    right = shift(sizes, second, -1, 0)
    p, q = swap(sizes, p, 0, 1), swap(sizes, q, 0, 2)
    corr, turned, acc = call(
        corr_kernel, m, [o, second, p, q],
        [shaped(full, F32), shaped((2 * T, 6 * T), BF), shaped(block, F32)], "corr", 16,
    )
    piece = shaped((members // 2, 1, 5 * T), F32)
    mine, theirs = call(
        gram_kernel, m, [o, turned, right, h_p, h_q, acc, corr], [piece, piece], "gram", 30
    )

    rows = members * second.shape[0] * second.shape[1]
    partial = mine + swap(sizes, theirs, 0, 1)
    total = exchange(sizes, partial).sum(axis=0, keepdims=True) / rows
    mine = exchange(sizes, jnp.broadcast_to(total, partial.shape))
    theirs = swap(sizes, mine, 0, 1)

    half = (4, T, T)
    keep, send, x = call(
        inverse_kernel, m, [mine, theirs, second],
        [shaped(half, BF), shaped(half, BF), shaped(full, F32)], "inverse", 80,
        scratch=[pltpu.VMEM(full, F32), pltpu.VMEM(full, F32)],
    )
    got = swap_col(sizes, send)
    p_shape = (2 * T, T)
    p_keep, p_send = call(
        project_kernel, m, [mine, theirs, x], [shaped(p_shape, F32), shaped(p_shape, BF)], "project", 24
    )
    p_got = swap_col(sizes, p_send).astype(F32)
    ritz = jnp.where(spin == 0, jnp.stack([keep, got]), jnp.stack([got, keep]))
    projected = jnp.where(spin == 0, jnp.stack([p_keep, p_got]), jnp.stack([p_got, p_keep]))
    return ritz[:, None], projected


def solution(mesh):
    return jax.shard_map(
        per_device,
        mesh=mesh,
        in_specs=(
            P(None, "gx", "gy", None, "col"),
            P(None, "gx", "gy", None, None, None),
            P("gx", "gy", None),
            P("gx", "gy"),
        ),
        out_specs=(P(None, "gx", "gy", None, "col"), P(None, None, "col")),
        check_vma=False,
    )
```

```python
import functools

import jax
import jax.numpy as jnp
from jax import lax
from jax.experimental import pallas as pl
from jax.experimental.pallas import tpu as pltpu
from jax.sharding import PartitionSpec as P

NB = 9
T = 128
AXES = ("gx", "gy", "col")
BF = jnp.bfloat16
F32 = jnp.float32
SPIN, COL, PAR_Y, PAR_X = 36, 37, 38, 39


def col_of(gx, spin):
    return spin ^ ((gx >> 1) & 1)


def device(sizes, gx, gy, col):
    return ((gx % sizes[0]) * sizes[1] + gy % sizes[1]) * sizes[2] + col


def pairs(sizes, target):
    out = []
    for gx in range(sizes[0]):
        for gy in range(sizes[1]):
            for spin in range(2):
                there = target(gx, gy)
                there_gx = there[0] % sizes[0]
                out.append(
                    (
                        device(sizes, gx, gy, col_of(gx, spin)),
                        device(sizes, there_gx, there[1], col_of(there_gx, spin)),
                    )
                )
    return out


def partner(index, kind):
    if kind == 0:
        return index
    return index + 1 if (index % 2 == 0) == (kind == 1) else index - 1


def swap(sizes, block, kind_x, kind_y):
    perm = pairs(sizes, lambda gx, gy: (partner(gx, kind_x), partner(gy, kind_y)))
    return lax.ppermute(block, AXES, perm)


def shift(sizes, block, dx, dy):
    return lax.ppermute(block, AXES, pairs(sizes, lambda gx, gy: (gx + dx, gy + dy)))


def swap_col(sizes, block):
    perm = [(d, d ^ 1) for d in range(sizes[0] * sizes[1] * 2)]
    return lax.ppermute(block, AXES, perm)


def exchange(sizes, pieces):
    groups = [
        [
            device(sizes, gx, gy, col_of(gx, spin))
            for gx in range(sizes[0])
            for gy in range(core, sizes[1], 2)
        ]
        for spin in range(2)
        for core in range(2)
    ]
    return lax.all_to_all(pieces, AXES, 0, 0, axis_index_groups=groups, tiled=True)


def dot(a, b, dims=((1,), (0,))):
    return lax.dot_general(a, b, (dims, ((), ())), preferred_element_type=F32)


def split(a):
    high = a.astype(BF)
    return high, (a - high.astype(F32)).astype(BF)


def dot3(a, b, dims=((1,), (0,))):
    (ah, al), (bh, bl) = split(a), split(b)
    return dot(ah, bh, dims) + (dot(ah, bl, dims) + dot(al, bh, dims))


def order_kernel(m, h, o, p, q):
    def block(tile, at):
        slot = m[tile * 9 + at]
        found = h[0, 0, tile, jnp.maximum(slot, 0)]
        return jnp.where(slot >= 0, found, jnp.zeros_like(found))

    for tile in range(4):
        for at in range(9):
            o[tile, :, at * T : (at + 1) * T] = block(tile, at)
    even = m[PAR_Y] == 0
    side = 1 + m[PAR_X]
    down, up = block(0, side * 3), block(3, side * 3 + 2)
    p[...] = jnp.where(even, up, down)
    q[...] = jnp.where(even, down, up)


def blocks(o, tile, sides, dys):
    out = []
    for side in sides:
        at = (side * 3 + dys[0]) * T
        if not isinstance(side, int):
            at = pl.multiple_of(at, T)
        out.append(o[tile, :, pl.ds(at, len(dys) * T)])
    return out[0] if len(out) == 1 else jnp.concatenate(out, axis=1)


def store_edges(m, ref, p, q):
    even = m[PAR_Y] == 0
    p[0:1] = ref[pl.ds(jnp.where(even, 3, 0), 1)]
    q[0:1] = ref[pl.ds(jnp.where(even, 0, 3), 1)]


def join_kernel(m, own, other, v, p, q):
    first_col = m[COL] == 0
    v[:, :, :T] = jnp.where(first_col, own[...], other[...])
    v[:, :, T:] = jnp.where(first_col, other[...], own[...])
    store_edges(m, v, p, q)
    q[1:2] = v[1:2]


def ends_of(m, ends):
    even = m[PAR_Y] == 0
    return jnp.where(even, ends[1:2], ends[0:1]), jnp.where(even, ends[0:1], ends[1:2])


def product(o, tile, sides, at, sources):
    row = blocks(o, tile, sides, [place - tile for place in at])
    return dot(row, jnp.concatenate([x.reshape(len(at) * T, 2 * T) for x in sources], axis=0))


def core_kernel(m, o, x, ends, a, b, acc, ext):
    low, high = ends_of(m, ends)
    ext[0:1] = low
    ext[1:5] = x[...]
    ext[5:6] = high
    for tile in range(4):
        total = product(o, tile, (0,), range(tile, tile + 3), [ext[tile : tile + 3]])
        at = [place for place in range(tile, tile + 3) if 1 <= place <= 4]
        sources = [y[at[0] - 1 : at[-1]] for y in (a, b)]
        acc[tile] = total + product(o, tile, (1, 2), at, sources)


def rim_kernel(m, o, a_ends, b_ends, acc, *rest, last):
    *more, out, p, q = rest
    low, high = zip(ends_of(m, a_ends), ends_of(m, b_ends))
    for tile in range(4):
        total = acc[tile]
        if tile == 0:
            total += product(o, tile, (1, 2), (0,), low)
        if tile == 3:
            total += product(o, tile, (1, 2), (5,), high)
        if last:
            out[tile] = (total - more[0][tile].astype(F32)).astype(BF)
        else:
            out[tile] = (0.5 * total).astype(BF)
    store_edges(m, out, p, q)
    if not last:
        for to, block in zip((p, q), more):
            to[1, :, :T] = block[...]
            to[1, :, T:] = block[...]


def corr_kernel(m, o, s, p, q, corr, turned, acc):
    flat = s[...].reshape(4 * T, 2 * T)
    turned[:, : 4 * T] = flat.T
    turned[:, 4 * T : 5 * T] = p[0].T
    turned[:, 5 * T :] = q[0].T
    corr[...] = dot(turned[:, : 4 * T], flat)
    above = jnp.where(m[PAR_Y] == 0, p[0], q[0])
    for tile in range(4):
        total = 0.5 * dot(blocks(o, tile, (0,), (1,)), s[tile])
        acc[tile] = total + dot(blocks(o, tile, (0,), (2,)), s[tile + 1] if tile < 3 else above)


def places():
    shape = (2 * T, 2 * T)
    return lax.broadcasted_iota(jnp.int32, shape, 0), lax.broadcasted_iota(jnp.int32, shape, 1)


def gram_kernel(m, o, turned, right, h_p, h_q, acc, corr, mine, theirs):
    side = 1 + m[PAR_X]
    parts = []
    for tile in range(4):
        at = [place for place in range(tile, tile + 3) if 1 <= place <= 4]
        parts.append(acc[tile] + product(o, tile, (side,), at, [right[at[0] - 1 : at[-1]]]))
    even = m[PAR_Y] == 0
    parts.append(dot(h_p[1, :, :T], right[jnp.where(even, 3, 0)]))
    parts.append(dot(h_q[1, :, :T], right[jnp.where(even, 0, 3)]))
    high, low = split(jnp.concatenate(parts, axis=0))
    half = dot(turned[...], high) + dot(turned[...], low)
    coupling = half + half.T
    rows, cols = places()
    both = jnp.where(rows >= cols, corr[...], coupling)
    diagonal = jnp.sum(jnp.where(rows == cols, coupling, 0.0), axis=1, keepdims=True)
    first, second = pack(both[:T], diagonal[:T]), pack(both[T:], diagonal[T:])
    even = m[PAR_Y] == 0
    mine[:, 0, :] = jnp.where(even, first, second)
    theirs[:, 0, :] = jnp.where(even, second, first)


def pack(square, diagonal):
    lane = lax.broadcasted_iota(jnp.int32, (T // 2, T), 1)
    extra = jnp.where(lane == 0, diagonal[: T // 2], jnp.where(lane == 1, diagonal[T // 2 :], 0.0))
    return jnp.concatenate([square[: T // 2], square[T // 2 :], extra], axis=1)


def unpack(table):
    square = jnp.concatenate([table[:, : 2 * T], table[:, 2 * T : 4 * T]], axis=0)
    return square, jnp.concatenate([table[:, 4 * T : 4 * T + 1], table[:, 4 * T + 1 : 4 * T + 2]], axis=0)


def lower_part(e, rows, cols):
    return jnp.where(rows > cols, e, jnp.where(rows == cols, 0.5 * e, 0.0))


def square_of(m, mine, theirs):
    even = m[PAR_Y] == 0
    first, second = mine[:, 0, :], theirs[:, 0, :]
    top = unpack(jnp.where(even, first, second))
    bottom = unpack(jnp.where(even, second, first))
    return jnp.concatenate([top[0], bottom[0]], axis=0), jnp.concatenate([top[1], bottom[1]], axis=0)


def inverse_kernel(m, mine, theirs, s, keep, send, x_out, x_ref, a_ref):
    rows, cols = places()
    both, _ = square_of(m, mine, theirs)
    turned = both.T
    corr = jnp.where(rows >= cols, both, turned)
    on_diagonal = jnp.where(rows == cols, corr, 0.0)
    scale_row = 1.0 / jnp.sqrt(jnp.sum(on_diagonal, axis=0, keepdims=True))
    scale_col = 1.0 / jnp.sqrt(jnp.sum(on_diagonal, axis=1, keepdims=True))
    scaled = corr * scale_row * scale_col
    unit = (rows == cols).astype(F32)

    a_ref[...] = scaled
    x_ref[...] = unit - lower_part(scaled - unit, rows, cols)

    def step(state):
        count, _ = state
        x = x_ref[...]
        e = dot3(dot3(x, a_ref[...]), x, ((1,), (1,))) - unit
        x_ref[...] = x - dot3(lower_part(e, rows, cols), x)
        return count + 1, jnp.sum(e * e)

    def more(state):
        count, size = state
        return (count < 12) & (size >= 4e-6) & (size < 1e4)

    _, size = lax.while_loop(more, step, (0, F32(1.0)))

    @pl.when(jnp.logical_not(size < 4e-6))
    def _():
        a_ref[...] = scaled
        x_ref[...] = unit

        def eliminate(j, carry):
            row = a_ref[pl.ds(j, 1), :]
            pivot = jnp.sum(jnp.where(cols[:1] == j, row, 0.0), axis=1, keepdims=True)
            a = a_ref[...]
            column = jnp.sum(jnp.where(cols == j, a, 0.0), axis=1, keepdims=True)
            factor = jnp.where(rows[:, :1] > j, column / pivot, 0.0)
            x = x_ref[...]
            x_row = x_ref[pl.ds(j, 1), :]
            a_ref[...] = a - factor * row
            x_ref[...] = x - factor * x_row
            return carry

        lax.fori_loop(0, 2 * T, eliminate, 0)
        pivots = jnp.sum(jnp.where(rows == cols, a_ref[...], 0.0), axis=1, keepdims=True)
        x_ref[...] = x_ref[...] / jnp.sqrt(pivots)

    x = x_ref[...] * scale_row
    x_out[...] = x
    ritz = dot(s[...].reshape(4 * T, 2 * T), x.astype(BF), ((1,), (1,))).astype(BF)
    ritz = ritz.reshape(4, T, 2 * T)
    first_col = m[COL] == 0
    keep[...] = jnp.where(first_col, ritz[:, :, :T], ritz[:, :, T:])
    send[...] = jnp.where(first_col, ritz[:, :, T:], ritz[:, :, :T])


def project_kernel(m, mine, theirs, x_ref, keep, send):
    rows, cols = places()
    both, diagonal = square_of(m, mine, theirs)
    coupling = jnp.where(rows < cols, both, jnp.where(rows == cols, diagonal, both.T))
    x = x_ref[...]
    projected = dot3(dot3(x, coupling), x, ((1,), (1,)))
    first_col = m[COL] == 0
    keep[...] = jnp.where(first_col, projected[:, :T], projected[:, T:])
    send[...] = jnp.where(first_col, projected[:, T:], projected[:, :T]).astype(BF)


def whole(shape):
    return pl.BlockSpec(shape, lambda i, m, n=len(shape): (0,) * n)


def call(kernel, m, arrays, outs, name, flops=0, specs=None, scratch=()):
    arrays = list(arrays)
    moved = sum(a.size * a.dtype.itemsize for a in [*arrays, *outs])
    return pl.pallas_call(
        kernel,
        out_shape=outs,
        grid_spec=pltpu.PrefetchScalarGridSpec(
            num_scalar_prefetch=1,
            grid=(1,),
            in_specs=specs or [whole(a.shape) for a in arrays],
            out_specs=[whole(o.shape) for o in outs],
            scratch_shapes=list(scratch),
        ),
        compiler_params=pltpu.CompilerParams(vmem_limit_bytes=32 * 1024 * 1024),
        cost_estimate=pl.CostEstimate(flops=2 * T * T * 2 * T * flops, bytes_accessed=moved, transcendentals=0),
        name=name,
    )(m, *arrays)


def table(neighbour_index, block_count):
    gx, gy, col = (lax.axis_index(a) for a in AXES)
    spin = col ^ ((gx >> 1) & 1)
    toward = jnp.where(gx % 2 == 0, 1, -1)
    dx = jnp.stack([jnp.zeros_like(toward), toward, -toward])
    codes = (dx[:, None] + 1) * 3 + jnp.arange(3, dtype=jnp.int32)[None, :]
    slots = jnp.arange(NB, dtype=jnp.int32)
    index, count = neighbour_index[0], block_count[0]
    match = (index[:, None, None, :] == codes[None, :, :, None]) & (
        slots < count[:, None, None, None]
    )
    found = jnp.sum(jnp.where(match, slots + 1, 0), axis=-1) - 1
    scalars = jnp.stack([spin, col, gy % 2, gx % 2])
    return spin, col, jnp.concatenate([found.reshape(-1), scalars]).astype(jnp.int32)


def shaped(shape, dtype):
    return jax.ShapeDtypeStruct(shape, dtype)


def per_device(start_block, hamiltonian, neighbour_index, block_count):
    sizes = tuple(lax.axis_size(a) for a in AXES)
    members = sizes[0] * sizes[1]
    block, full = (4, T, 2 * T), (2 * T, 2 * T)
    spin, col, m = table(neighbour_index, block_count)

    other = swap_col(sizes, lax.dynamic_index_in_dim(start_block, 1 - spin, 0, keepdims=False)[0])
    own = lax.dynamic_index_in_dim(start_block, spin, 0, keepdims=False)[0]
    spin_block = pl.BlockSpec((1,) + hamiltonian.shape[1:], lambda i, m: (m[SPIN], 0, 0, 0, 0, 0))
    corner = shaped((T, T), BF)
    o, h_p, h_q = call(
        order_kernel, m, [hamiltonian], [shaped((4, T, NB * T), BF), corner, corner], "order", specs=[spin_block]
    )
    tile, two = shaped((1, T, 2 * T), BF), shaped((2, T, 2 * T), BF)
    ext = pltpu.VMEM((6, T, 2 * T), BF)
    v, p, q = call(join_kernel, m, [own, other], [shaped(block, BF), tile, two], "join")

    def apply_ham(o, x, p, q, more, edges, last):
        p, q = swap(sizes, p, 0, 1), swap(sizes, q, 0, 2)
        ends = jnp.concatenate([p[:1], q[:1]], axis=0)
        a, b = swap(sizes, x, 1, 0), swap(sizes, x, 2, 0)
        o, a, b = lax.optimization_barrier((o, a, b))
        a_ends, b_ends = swap(sizes, ends, 1, 0), swap(sizes, ends, 2, 0)
        (acc,) = call(core_kernel, m, [o, x, ends, a, b], [shaped(block, F32)], "core", 32, scratch=[ext])
        out = call(
            functools.partial(rim_kernel, last=last), m, [o, a_ends, b_ends, acc, *more],
            [shaped(block, BF), edges, edges], "rim", 4,
        )
        return o, p, q, out

    o, _, _, (first, p, q) = apply_ham(o, v, p, q, [h_p, h_q], two, False)
    o, h_p, h_q, (second, p, q) = apply_ham(o, first, p, q, [v], tile, True)

    right = shift(sizes, second, -1, 0)
    p, q = swap(sizes, p, 0, 1), swap(sizes, q, 0, 2)
    corr, turned, acc = call(
        corr_kernel, m, [o, second, p, q],
        [shaped(full, F32), shaped((2 * T, 6 * T), BF), shaped(block, F32)], "corr", 400,
    )
    piece = shaped((members // 2, 1, 5 * T), F32)
    mine, theirs = call(
        gram_kernel, m, [o, turned, right, h_p, h_q, acc, corr], [piece, piece], "gram", 30
    )

    rows = members * second.shape[0] * second.shape[1]
    partial = mine + swap(sizes, theirs, 0, 1)
    total = exchange(sizes, partial).sum(axis=0, keepdims=True) / rows
    mine = exchange(sizes, jnp.broadcast_to(total, partial.shape))
    theirs = swap(sizes, mine, 0, 1)

    half = (4, T, T)
    keep, send, x = call(
        inverse_kernel, m, [mine, theirs, second],
        [shaped(half, BF), shaped(half, BF), shaped(full, F32)], "inverse", 80,
        scratch=[pltpu.VMEM(full, F32), pltpu.VMEM(full, F32)],
    )
    got = swap_col(sizes, send)
    p_shape = (2 * T, T)
    p_keep, p_send = call(
        project_kernel, m, [mine, theirs, x], [shaped(p_shape, F32), shaped(p_shape, BF)], "project", 24
    )
    p_got = swap_col(sizes, p_send).astype(F32)
    ritz = jnp.where(spin == 0, jnp.stack([keep, got]), jnp.stack([got, keep]))
    projected = jnp.where(spin == 0, jnp.stack([p_keep, p_got]), jnp.stack([p_got, p_keep]))
    return ritz[:, None], projected


def solution(mesh):
    return jax.shard_map(
        per_device,
        mesh=mesh,
        in_specs=(
            P(None, "gx", "gy", None, "col"),
            P(None, "gx", "gy", None, None, None),
            P("gx", "gy", None),
            P("gx", "gy"),
        ),
        out_specs=(P(None, "gx", "gy", None, "col"), P(None, None, "col")),
        check_vma=False,
    )
```

```python
import functools

import jax
import jax.numpy as jnp
from jax import lax
from jax.experimental import pallas as pl
from jax.experimental.pallas import tpu as pltpu
from jax.sharding import PartitionSpec as P

NB = 9
T = 128
AXES = ("gx", "gy", "col")
BF = jnp.bfloat16
F32 = jnp.float32
SPIN, COL, PAR_Y, PAR_X = 36, 37, 38, 39


def col_of(gx, spin):
    return spin ^ ((gx >> 1) & 1)


def device(sizes, gx, gy, col):
    return ((gx % sizes[0]) * sizes[1] + gy % sizes[1]) * sizes[2] + col


def pairs(sizes, target):
    out = []
    for gx in range(sizes[0]):
        for gy in range(sizes[1]):
            for spin in range(2):
                there = target(gx, gy)
                there_gx = there[0] % sizes[0]
                out.append(
                    (
                        device(sizes, gx, gy, col_of(gx, spin)),
                        device(sizes, there_gx, there[1], col_of(there_gx, spin)),
                    )
                )
    return out


def partner(index, kind):
    if kind == 0:
        return index
    return index + 1 if (index % 2 == 0) == (kind == 1) else index - 1


def swap(sizes, block, kind_x, kind_y):
    perm = pairs(sizes, lambda gx, gy: (partner(gx, kind_x), partner(gy, kind_y)))
    return lax.ppermute(block, AXES, perm)


def shift(sizes, block, dx, dy):
    return lax.ppermute(block, AXES, pairs(sizes, lambda gx, gy: (gx + dx, gy + dy)))


def swap_col(sizes, block):
    perm = [(d, d ^ 1) for d in range(sizes[0] * sizes[1] * 2)]
    return lax.ppermute(block, AXES, perm)


def exchange(sizes, pieces, joint):
    groups = [
        [
            device(sizes, gx, gy, col_of(gx, spin))
            for gx in range(sizes[0])
            for gy in range(core, sizes[1], 2)
        ]
        for core in range(2)
        for spin in range(2)
    ]
    if joint:
        groups = [groups[0] + groups[1], groups[2] + groups[3]]
    return lax.all_to_all(pieces, AXES, 0, 0, axis_index_groups=groups, tiled=True)


def dot(a, b, dims=((1,), (0,))):
    return lax.dot_general(a, b, (dims, ((), ())), preferred_element_type=F32)


def split(a):
    high = a.astype(BF)
    return high, (a - high.astype(F32)).astype(BF)


def dot3(a, b, dims=((1,), (0,))):
    (ah, al), (bh, bl) = split(a), split(b)
    return dot(ah, bh, dims) + (dot(ah, bl, dims) + dot(al, bh, dims))


def order_kernel(m, h, o, p, q):
    def block(tile, at):
        slot = m[tile * 9 + at]
        found = h[0, 0, tile, jnp.maximum(slot, 0)]
        return jnp.where(slot >= 0, found, jnp.zeros_like(found))

    for tile in range(4):
        for at in range(9):
            o[tile, :, at * T : (at + 1) * T] = block(tile, at)
    even = m[PAR_Y] == 0
    side = 1 + m[PAR_X]
    down, up = block(0, side * 3), block(3, side * 3 + 2)
    p[...] = jnp.where(even, up, down)
    q[...] = jnp.where(even, down, up)


def blocks(o, tile, sides, dys):
    out = []
    for side in sides:
        at = (side * 3 + dys[0]) * T
        if not isinstance(side, int):
            at = pl.multiple_of(at, T)
        out.append(o[tile, :, pl.ds(at, len(dys) * T)])
    return out[0] if len(out) == 1 else jnp.concatenate(out, axis=1)


def store_edges(m, ref, p, q):
    even = m[PAR_Y] == 0
    p[0:1] = ref[pl.ds(jnp.where(even, 3, 0), 1)]
    q[0:1] = ref[pl.ds(jnp.where(even, 0, 3), 1)]


def join_kernel(m, own, other, v, p, q):
    first_col = m[COL] == 0
    v[:, :, :T] = jnp.where(first_col, own[...], other[...])
    v[:, :, T:] = jnp.where(first_col, other[...], own[...])
    store_edges(m, v, p, q)
    q[1:2] = v[1:2]


def ends_of(m, ends):
    even = m[PAR_Y] == 0
    return jnp.where(even, ends[1:2], ends[0:1]), jnp.where(even, ends[0:1], ends[1:2])


def product(o, tile, sides, at, sources):
    row = blocks(o, tile, sides, [place - tile for place in at])
    return dot(row, jnp.concatenate([x.reshape(len(at) * T, 2 * T) for x in sources], axis=0))


def core_kernel(m, o, x, ends, a, b, acc, ext):
    low, high = ends_of(m, ends)
    ext[0:1] = low
    ext[1:5] = x[...]
    ext[5:6] = high
    for tile in range(4):
        total = product(o, tile, (0,), range(tile, tile + 3), [ext[tile : tile + 3]])
        at = [place for place in range(tile, tile + 3) if 1 <= place <= 4]
        sources = [y[at[0] - 1 : at[-1]] for y in (a, b)]
        acc[tile] = total + product(o, tile, (1, 2), at, sources)


def rim_kernel(m, o, a_ends, b_ends, acc, *rest, last):
    *more, out, p, q = rest
    low, high = zip(ends_of(m, a_ends), ends_of(m, b_ends))
    for tile in range(4):
        total = acc[tile]
        if tile == 0:
            total += product(o, tile, (1, 2), (0,), low)
        if tile == 3:
            total += product(o, tile, (1, 2), (5,), high)
        if last:
            out[tile] = (total - more[0][tile].astype(F32)).astype(BF)
        else:
            out[tile] = (0.5 * total).astype(BF)
    store_edges(m, out, p, q)
    if not last:
        for to, block in zip((p, q), more):
            to[1, :, :T] = block[...]
            to[1, :, T:] = block[...]


def corr_kernel(m, o, s, p, q, corr, turned, acc):
    flat = s[...].reshape(4 * T, 2 * T)
    turned[:, : 4 * T] = flat.T
    turned[:, 4 * T : 5 * T] = p[0].T
    turned[:, 5 * T :] = q[0].T
    corr[...] = dot(turned[:, : 4 * T], flat)
    above = jnp.where(m[PAR_Y] == 0, p[0], q[0])
    for tile in range(4):
        total = 0.5 * dot(blocks(o, tile, (0,), (1,)), s[tile])
        acc[tile] = total + dot(blocks(o, tile, (0,), (2,)), s[tile + 1] if tile < 3 else above)


def places():
    shape = (2 * T, 2 * T)
    return lax.broadcasted_iota(jnp.int32, shape, 0), lax.broadcasted_iota(jnp.int32, shape, 1)


def gram_kernel(m, o, turned, right, h_p, h_q, acc, corr, mine, theirs):
    side = 1 + m[PAR_X]
    parts = []
    for tile in range(4):
        at = [place for place in range(tile, tile + 3) if 1 <= place <= 4]
        parts.append(acc[tile] + product(o, tile, (side,), at, [right[at[0] - 1 : at[-1]]]))
    even = m[PAR_Y] == 0
    parts.append(dot(h_p[1, :, :T], right[jnp.where(even, 3, 0)]))
    parts.append(dot(h_q[1, :, :T], right[jnp.where(even, 0, 3)]))
    high, low = split(jnp.concatenate(parts, axis=0))
    half = dot(turned[...], high) + dot(turned[...], low)
    coupling = half + half.T
    rows, cols = places()
    both = jnp.where(rows >= cols, corr[...], coupling)
    diagonal = jnp.sum(jnp.where(rows == cols, coupling, 0.0), axis=1, keepdims=True)
    first, second = pack(both[:T], diagonal[:T]), pack(both[T:], diagonal[T:])
    even = m[PAR_Y] == 0
    mine[:, 0, :] = jnp.where(even, first, second)
    theirs[:, 0, :] = jnp.where(even, second, first)


def pack(square, diagonal):
    lane = lax.broadcasted_iota(jnp.int32, (T // 2, T), 1)
    extra = jnp.where(lane == 0, diagonal[: T // 2], jnp.where(lane == 1, diagonal[T // 2 :], 0.0))
    return jnp.concatenate([square[: T // 2], square[T // 2 :], extra], axis=1)


def unpack(table):
    square = jnp.concatenate([table[:, : 2 * T], table[:, 2 * T : 4 * T]], axis=0)
    return square, jnp.concatenate([table[:, 4 * T : 4 * T + 1], table[:, 4 * T + 1 : 4 * T + 2]], axis=0)


def lower_part(e, rows, cols):
    return jnp.where(rows > cols, e, jnp.where(rows == cols, 0.5 * e, 0.0))


def squares(m, mine, theirs, spin):
    even = m[PAR_Y] == 0
    half = slice(spin * T // 2, (spin + 1) * T // 2)
    first, second = mine[half, 0, :], theirs[half, 0, :]
    top = unpack(jnp.where(even, first, second))
    bottom = unpack(jnp.where(even, second, first))
    both = jnp.concatenate([top[0], bottom[0]], axis=0)
    diagonal = jnp.concatenate([top[1], bottom[1]], axis=0)
    rows, cols = places()
    turned = both.T
    corr = jnp.where(rows >= cols, both, turned)
    return corr, jnp.where(rows < cols, both, jnp.where(rows == cols, diagonal, turned))


def final_kernel(m, mine, theirs, s, other, ritz, projected, x_ref, a_ref, k_ref):
    rows, cols = places()
    unit = (rows == cols).astype(F32)
    scales = []
    for spin in range(2):
        corr, k_ref[spin] = squares(m, mine, theirs, spin)
        on_diagonal = jnp.where(rows == cols, corr, 0.0)
        scale_row = 1.0 / jnp.sqrt(jnp.sum(on_diagonal, axis=0, keepdims=True))
        scale_col = 1.0 / jnp.sqrt(jnp.sum(on_diagonal, axis=1, keepdims=True))
        scaled = corr * scale_row * scale_col
        scales.append(scale_row)
        a_ref[spin] = scaled
        x_ref[spin] = unit - lower_part(scaled - unit, rows, cols)

    def step(state):
        count, _, _ = state
        xs = [x_ref[spin] for spin in range(2)]
        es = [dot3(xs[spin], a_ref[spin]) for spin in range(2)]
        es = [dot3(es[spin], xs[spin], ((1,), (1,))) - unit for spin in range(2)]
        for spin in range(2):
            x_ref[spin] = xs[spin] - dot3(lower_part(es[spin], rows, cols), xs[spin])
        return count + 1, jnp.sum(es[0] * es[0]), jnp.sum(es[1] * es[1])

    def more(state):
        count, *sizes = state
        largest = jnp.maximum(*sizes)
        return (count < 12) & (largest >= 4e-6) & (largest < 1e4)

    _, *sizes = lax.while_loop(more, step, (0, F32(1.0), F32(1.0)))

    for spin in range(2):

        @pl.when(jnp.logical_not(sizes[spin] < 4e-6))
        def _(spin=spin):
            x_ref[spin] = unit

            def eliminate(j, carry):
                row = a_ref[spin, pl.ds(j, 1), :]
                pivot = jnp.sum(jnp.where(cols[:1] == j, row, 0.0), axis=1, keepdims=True)
                a = a_ref[spin]
                column = jnp.sum(jnp.where(cols == j, a, 0.0), axis=1, keepdims=True)
                factor = jnp.where(rows[:, :1] > j, column / pivot, 0.0)
                x = x_ref[spin]
                x_row = x_ref[spin, pl.ds(j, 1), :]
                a_ref[spin] = a - factor * row
                x_ref[spin] = x - factor * x_row
                return carry

            lax.fori_loop(0, 2 * T, eliminate, 0)
            pivots = jnp.sum(jnp.where(rows == cols, a_ref[spin], 0.0), axis=1, keepdims=True)
            x_ref[spin] = x_ref[spin] / jnp.sqrt(pivots)

    mine_first = m[SPIN] == 0
    first_col = m[COL] == 0
    for spin in range(2):
        x = x_ref[spin] * scales[spin]
        part = jnp.where(first_col, x[:T], x[T:])
        block = jnp.where(mine_first == (spin == 0), s[...], other[...]).reshape(4 * T, 2 * T)
        ritz[spin, 0] = dot(block, part.astype(BF), ((1,), (1,))).astype(BF).reshape(4, T, T)
        projected[spin] = dot3(dot3(x, k_ref[spin]), part, ((1,), (1,)))


def whole(shape):
    return pl.BlockSpec(shape, lambda i, m, n=len(shape): (0,) * n)


def call(kernel, m, arrays, outs, name, flops=0, specs=None, scratch=()):
    arrays = list(arrays)
    moved = sum(a.size * a.dtype.itemsize for a in [*arrays, *outs])
    return pl.pallas_call(
        kernel,
        out_shape=outs,
        grid_spec=pltpu.PrefetchScalarGridSpec(
            num_scalar_prefetch=1,
            grid=(1,),
            in_specs=specs or [whole(a.shape) for a in arrays],
            out_specs=[whole(o.shape) for o in outs],
            scratch_shapes=list(scratch),
        ),
        compiler_params=pltpu.CompilerParams(vmem_limit_bytes=32 * 1024 * 1024),
        cost_estimate=pl.CostEstimate(flops=2 * T * T * 2 * T * flops, bytes_accessed=moved, transcendentals=0),
        name=name,
    )(m, *arrays)


def table(neighbour_index, block_count):
    gx, gy, col = (lax.axis_index(a) for a in AXES)
    spin = col ^ ((gx >> 1) & 1)
    toward = jnp.where(gx % 2 == 0, 1, -1)
    dx = jnp.stack([jnp.zeros_like(toward), toward, -toward])
    codes = (dx[:, None] + 1) * 3 + jnp.arange(3, dtype=jnp.int32)[None, :]
    slots = jnp.arange(NB, dtype=jnp.int32)
    index, count = neighbour_index[0], block_count[0]
    match = (index[:, None, None, :] == codes[None, :, :, None]) & (
        slots < count[:, None, None, None]
    )
    found = jnp.sum(jnp.where(match, slots + 1, 0), axis=-1) - 1
    scalars = jnp.stack([spin, col, gy % 2, gx % 2])
    return spin, col, jnp.concatenate([found.reshape(-1), scalars]).astype(jnp.int32)


def shaped(shape, dtype):
    return jax.ShapeDtypeStruct(shape, dtype)


def per_device(start_block, hamiltonian, neighbour_index, block_count):
    sizes = tuple(lax.axis_size(a) for a in AXES)
    members = sizes[0] * sizes[1]
    block, full = (4, T, 2 * T), (2 * T, 2 * T)
    spin, col, m = table(neighbour_index, block_count)

    other = swap_col(sizes, lax.dynamic_index_in_dim(start_block, 1 - spin, 0, keepdims=False)[0])
    own = lax.dynamic_index_in_dim(start_block, spin, 0, keepdims=False)[0]
    spin_block = pl.BlockSpec((1,) + hamiltonian.shape[1:], lambda i, m: (m[SPIN], 0, 0, 0, 0, 0))
    corner = shaped((T, T), BF)
    o, h_p, h_q = call(
        order_kernel, m, [hamiltonian], [shaped((4, T, NB * T), BF), corner, corner], "order", specs=[spin_block]
    )
    tile, two = shaped((1, T, 2 * T), BF), shaped((2, T, 2 * T), BF)
    ext = pltpu.VMEM((6, T, 2 * T), BF)
    v, p, q = call(join_kernel, m, [own, other], [shaped(block, BF), tile, two], "join")

    def apply_ham(o, x, p, q, more, edges, last):
        p, q = swap(sizes, p, 0, 1), swap(sizes, q, 0, 2)
        ends = jnp.concatenate([p[:1], q[:1]], axis=0)
        a, b = swap(sizes, x, 1, 0), swap(sizes, x, 2, 0)
        o, a, b = lax.optimization_barrier((o, a, b))
        a_ends, b_ends = swap(sizes, ends, 1, 0), swap(sizes, ends, 2, 0)
        (acc,) = call(core_kernel, m, [o, x, ends, a, b], [shaped(block, F32)], "core", 32, scratch=[ext])
        out = call(
            functools.partial(rim_kernel, last=last), m, [o, a_ends, b_ends, acc, *more],
            [shaped(block, BF), edges, edges], "rim", 4,
        )
        return o, p, q, out

    o, _, _, (first, p, q) = apply_ham(o, v, p, q, [h_p, h_q], two, False)
    o, h_p, h_q, (second, p, q) = apply_ham(o, first, p, q, [v], tile, True)

    right = shift(sizes, second, -1, 0)
    p, q = swap(sizes, p, 0, 1), swap(sizes, q, 0, 2)
    corr, turned, acc = call(
        corr_kernel, m, [o, second, p, q],
        [shaped(full, F32), shaped((2 * T, 6 * T), BF), shaped(block, F32)], "corr", 16,
    )
    piece = shaped((members // 2, 1, 5 * T), F32)
    mine, theirs = call(
        gram_kernel, m, [o, turned, right, h_p, h_q, acc, corr], [piece, piece], "gram", 30
    )

    rows = members * second.shape[0] * second.shape[1]
    partial = mine + swap(sizes, theirs, 0, 1)
    partner_second = swap_col(sizes, second)
    total = exchange(sizes, partial, False).sum(axis=0, keepdims=True) / rows
    total, partner_second = lax.optimization_barrier((total, partner_second))
    mine = exchange(sizes, jnp.broadcast_to(total, (members, 1, 5 * T)), True)
    theirs = swap(sizes, mine, 0, 1)
    squared = pltpu.VMEM((2, *full), F32)
    return tuple(
        call(
            final_kernel, m, [mine, theirs, second, partner_second],
            [shaped((2, 1, 4, T, T), BF), shaped((2, 2 * T, T), F32)], "final", 200,
            scratch=[squared, squared, squared],
        )
    )


def solution(mesh):
    return jax.shard_map(
        per_device,
        mesh=mesh,
        in_specs=(
            P(None, "gx", "gy", None, "col"),
            P(None, "gx", "gy", None, None, None),
            P("gx", "gy", None),
            P("gx", "gy"),
        ),
        out_specs=(P(None, "gx", "gy", None, "col"), P(None, None, "col")),
        check_vma=False,
    )
```

```python
import functools

import jax
import jax.numpy as jnp
from jax import lax
from jax.experimental import pallas as pl
from jax.experimental.pallas import tpu as pltpu
from jax.sharding import PartitionSpec as P

NB = 9
T = 128
AXES = ("gx", "gy", "col")
BF = jnp.bfloat16
F32 = jnp.float32
SPIN, COL, PAR_Y, PAR_X = 36, 37, 38, 39


def col_of(gx, spin):
    return spin ^ ((gx >> 1) & 1)


def device(sizes, gx, gy, col):
    return ((gx % sizes[0]) * sizes[1] + gy % sizes[1]) * sizes[2] + col


def pairs(sizes, target):
    out = []
    for gx in range(sizes[0]):
        for gy in range(sizes[1]):
            for spin in range(2):
                there = target(gx, gy)
                there_gx = there[0] % sizes[0]
                out.append(
                    (
                        device(sizes, gx, gy, col_of(gx, spin)),
                        device(sizes, there_gx, there[1], col_of(there_gx, spin)),
                    )
                )
    return out


def partner(index, kind):
    if kind == 0:
        return index
    return index + 1 if (index % 2 == 0) == (kind == 1) else index - 1


def swap(sizes, block, kind_x, kind_y):
    perm = pairs(sizes, lambda gx, gy: (partner(gx, kind_x), partner(gy, kind_y)))
    return lax.ppermute(block, AXES, perm)


def shift(sizes, block, dx, dy):
    return lax.ppermute(block, AXES, pairs(sizes, lambda gx, gy: (gx + dx, gy + dy)))


def swap_col(sizes, block):
    perm = [(d, d ^ 1) for d in range(sizes[0] * sizes[1] * 2)]
    return lax.ppermute(block, AXES, perm)


def exchange(sizes, pieces, joint):
    groups = [
        [
            device(sizes, gx, gy, col_of(gx, spin))
            for gx in range(sizes[0])
            for gy in range(core, sizes[1], 2)
        ]
        for core in range(2)
        for spin in range(2)
    ]
    if joint:
        groups = [groups[0] + groups[1], groups[2] + groups[3]]
    return lax.all_to_all(pieces, AXES, 0, 0, axis_index_groups=groups, tiled=True)


def dot(a, b, dims=((1,), (0,))):
    return lax.dot_general(a, b, (dims, ((), ())), preferred_element_type=F32)


def split(a):
    high = a.astype(BF)
    return high, (a - high.astype(F32)).astype(BF)


def dot3(a, b, dims=((1,), (0,))):
    (ah, al), (bh, bl) = split(a), split(b)
    return dot(ah, bh, dims) + (dot(ah, bl, dims) + dot(al, bh, dims))


def order_kernel(m, h, o, p, q):
    def block(tile, at):
        slot = m[tile * 9 + at]
        found = h[0, 0, tile, jnp.maximum(slot, 0)]
        return jnp.where(slot >= 0, found, jnp.zeros_like(found))

    for tile in range(4):
        for at in range(9):
            o[tile, :, at * T : (at + 1) * T] = block(tile, at)
    even = m[PAR_Y] == 0
    side = 1 + m[PAR_X]
    down, up = block(0, side * 3), block(3, side * 3 + 2)
    p[...] = jnp.where(even, up, down)
    q[...] = jnp.where(even, down, up)


def blocks(o, tile, sides, dys):
    out = []
    for side in sides:
        at = (side * 3 + dys[0]) * T
        if not isinstance(side, int):
            at = pl.multiple_of(at, T)
        out.append(o[tile, :, pl.ds(at, len(dys) * T)])
    return out[0] if len(out) == 1 else jnp.concatenate(out, axis=1)


def store_edges(m, ref, p, q):
    even = m[PAR_Y] == 0
    p[0:1] = ref[pl.ds(jnp.where(even, 3, 0), 1)]
    q[0:1] = ref[pl.ds(jnp.where(even, 0, 3), 1)]


def join_kernel(m, own, other, v, p, q):
    first_col = m[COL] == 0
    v[:, :, :T] = jnp.where(first_col, own[...], other[...])
    v[:, :, T:] = jnp.where(first_col, other[...], own[...])
    store_edges(m, v, p, q)
    q[1:2] = v[1:2]


def ends_of(m, ends):
    even = m[PAR_Y] == 0
    return jnp.where(even, ends[1:2], ends[0:1]), jnp.where(even, ends[0:1], ends[1:2])


def product(o, tile, sides, at, sources):
    row = blocks(o, tile, sides, [place - tile for place in at])
    return dot(row, jnp.concatenate([x.reshape(len(at) * T, 2 * T) for x in sources], axis=0))


def core_kernel(m, o, x, ends, a, b, acc, ext):
    low, high = ends_of(m, ends)
    ext[0:1] = low
    ext[1:5] = x[...]
    ext[5:6] = high
    for tile in range(4):
        total = product(o, tile, (0,), range(tile, tile + 3), [ext[tile : tile + 3]])
        at = [place for place in range(tile, tile + 3) if 1 <= place <= 4]
        sources = [y[at[0] - 1 : at[-1]] for y in (a, b)]
        acc[tile] = total + product(o, tile, (1, 2), at, sources)


def rim_kernel(m, o, a_ends, b_ends, acc, *rest, last):
    *more, out, p, q = rest
    low, high = zip(ends_of(m, a_ends), ends_of(m, b_ends))
    for tile in range(4):
        total = acc[tile]
        if tile == 0:
            total += product(o, tile, (1, 2), (0,), low)
        if tile == 3:
            total += product(o, tile, (1, 2), (5,), high)
        if last:
            out[tile] = (total - more[0][tile].astype(F32)).astype(BF)
        else:
            out[tile] = (0.5 * total).astype(BF)
    store_edges(m, out, p, q)
    if not last:
        for to, block in zip((p, q), more):
            to[1, :, :T] = block[...]
            to[1, :, T:] = block[...]


def corr_kernel(m, o, s, p, q, corr, turned, acc):
    flat = s[...].reshape(4 * T, 2 * T)
    turned[:, : 4 * T] = flat.T
    turned[:, 4 * T : 5 * T] = p[0].T
    turned[:, 5 * T :] = q[0].T
    corr[...] = dot(turned[:, : 4 * T], flat)
    above = jnp.where(m[PAR_Y] == 0, p[0], q[0])
    for tile in range(4):
        total = 0.5 * dot(blocks(o, tile, (0,), (1,)), s[tile])
        acc[tile] = total + dot(blocks(o, tile, (0,), (2,)), s[tile + 1] if tile < 3 else above)


def places():
    shape = (2 * T, 2 * T)
    return lax.broadcasted_iota(jnp.int32, shape, 0), lax.broadcasted_iota(jnp.int32, shape, 1)


def gram_kernel(m, o, turned, right, h_p, h_q, acc, corr, mine, theirs):
    side = 1 + m[PAR_X]
    parts = []
    for tile in range(4):
        at = [place for place in range(tile, tile + 3) if 1 <= place <= 4]
        parts.append(acc[tile] + product(o, tile, (side,), at, [right[at[0] - 1 : at[-1]]]))
    even = m[PAR_Y] == 0
    parts.append(dot(h_p[1, :, :T], right[jnp.where(even, 3, 0)]))
    parts.append(dot(h_q[1, :, :T], right[jnp.where(even, 0, 3)]))
    high, low = split(jnp.concatenate(parts, axis=0))
    half = dot(turned[...], high) + dot(turned[...], low)
    coupling = half + half.T
    rows, cols = places()
    both = jnp.where(rows >= cols, corr[...], coupling)
    diagonal = jnp.sum(jnp.where(rows == cols, coupling, 0.0), axis=1, keepdims=True)
    first, second = pack(both[:T], diagonal[:T]), pack(both[T:], diagonal[T:])
    even = m[PAR_Y] == 0
    mine[:, 0, :] = jnp.where(even, first, second)
    theirs[:, 0, :] = jnp.where(even, second, first)


def pack(square, diagonal):
    lane = lax.broadcasted_iota(jnp.int32, (T // 2, T), 1)
    extra = jnp.where(lane == 0, diagonal[: T // 2], jnp.where(lane == 1, diagonal[T // 2 :], 0.0))
    return jnp.concatenate([square[: T // 2], square[T // 2 :], extra], axis=1)


def unpack(table):
    square = jnp.concatenate([table[:, : 2 * T], table[:, 2 * T : 4 * T]], axis=0)
    return square, jnp.concatenate([table[:, 4 * T : 4 * T + 1], table[:, 4 * T + 1 : 4 * T + 2]], axis=0)


def lower_part(e, rows, cols):
    return jnp.where(rows > cols, e, jnp.where(rows == cols, 0.5 * e, 0.0))


def squares(m, mine, theirs, spin):
    even = m[PAR_Y] == 0
    half = slice(spin * T // 2, (spin + 1) * T // 2)
    first, second = mine[half, 0, :], theirs[half, 0, :]
    top = unpack(jnp.where(even, first, second))
    bottom = unpack(jnp.where(even, second, first))
    both = jnp.concatenate([top[0], bottom[0]], axis=0)
    diagonal = jnp.concatenate([top[1], bottom[1]], axis=0)
    rows, cols = places()
    turned = both.T
    corr = jnp.where(rows >= cols, both, turned)
    return corr, jnp.where(rows < cols, both, jnp.where(rows == cols, diagonal, turned))


def stack_kernel(m, s, other, both):
    both[pl.ds(m[SPIN], 1)] = s[...][None]
    both[pl.ds(1 - m[SPIN], 1)] = other[...][None]


def final_kernel(m, mine, theirs, both, ritz, projected, x_ref, a_ref, k_ref):
    rows, cols = places()
    unit = (rows == cols).astype(F32)
    scales = []
    for spin in range(2):
        corr, k_ref[spin] = squares(m, mine, theirs, spin)
        on_diagonal = jnp.where(rows == cols, corr, 0.0)
        scale_row = 1.0 / jnp.sqrt(jnp.sum(on_diagonal, axis=0, keepdims=True))
        scale_col = 1.0 / jnp.sqrt(jnp.sum(on_diagonal, axis=1, keepdims=True))
        scaled = corr * scale_row * scale_col
        scales.append(scale_row)
        a_ref[spin] = scaled
        x_ref[spin] = unit - lower_part(scaled - unit, rows, cols)

    def step(state):
        count, _, _ = state
        xs = [x_ref[spin] for spin in range(2)]
        es = [dot3(xs[spin], a_ref[spin]) for spin in range(2)]
        es = [dot3(es[spin], xs[spin], ((1,), (1,))) - unit for spin in range(2)]
        for spin in range(2):
            x_ref[spin] = xs[spin] - dot3(lower_part(es[spin], rows, cols), xs[spin])
        return count + 1, jnp.sum(es[0] * es[0]), jnp.sum(es[1] * es[1])

    def more(state):
        count, *sizes = state
        largest = jnp.maximum(*sizes)
        return (count < 12) & (largest >= 4e-6) & (largest < 1e4)

    _, *sizes = lax.while_loop(more, step, (0, F32(1.0), F32(1.0)))

    for spin in range(2):

        @pl.when(jnp.logical_not(sizes[spin] < 4e-6))
        def _(spin=spin):
            x_ref[spin] = unit

            def eliminate(j, carry):
                row = a_ref[spin, pl.ds(j, 1), :]
                pivot = jnp.sum(jnp.where(cols[:1] == j, row, 0.0), axis=1, keepdims=True)
                a = a_ref[spin]
                column = jnp.sum(jnp.where(cols == j, a, 0.0), axis=1, keepdims=True)
                factor = jnp.where(rows[:, :1] > j, column / pivot, 0.0)
                x = x_ref[spin]
                x_row = x_ref[spin, pl.ds(j, 1), :]
                a_ref[spin] = a - factor * row
                x_ref[spin] = x - factor * x_row
                return carry

            lax.fori_loop(0, 2 * T, eliminate, 0)
            pivots = jnp.sum(jnp.where(rows == cols, a_ref[spin], 0.0), axis=1, keepdims=True)
            x_ref[spin] = x_ref[spin] / jnp.sqrt(pivots)

    first_col = m[COL] == 0
    for spin in range(2):
        x = x_ref[spin] * scales[spin]
        part = jnp.where(first_col, x[:T], x[T:])
        ritz[spin, 0] = dot(both[spin].reshape(4 * T, 2 * T), part.astype(BF), ((1,), (1,))).astype(BF).reshape(4, T, T)
        projected[spin] = dot3(dot3(x, k_ref[spin]), part, ((1,), (1,)))


def whole(shape):
    return pl.BlockSpec(shape, lambda i, m, n=len(shape): (0,) * n)


def call(kernel, m, arrays, outs, name, flops=0, specs=None, scratch=()):
    arrays = list(arrays)
    moved = sum(a.size * a.dtype.itemsize for a in [*arrays, *outs])
    return pl.pallas_call(
        kernel,
        out_shape=outs,
        grid_spec=pltpu.PrefetchScalarGridSpec(
            num_scalar_prefetch=1,
            grid=(1,),
            in_specs=specs or [whole(a.shape) for a in arrays],
            out_specs=[whole(o.shape) for o in outs],
            scratch_shapes=list(scratch),
        ),
        compiler_params=pltpu.CompilerParams(vmem_limit_bytes=32 * 1024 * 1024),
        cost_estimate=pl.CostEstimate(flops=2 * T * T * 2 * T * flops, bytes_accessed=moved, transcendentals=0),
        name=name,
    )(m, *arrays)


def table(neighbour_index, block_count):
    gx, gy, col = (lax.axis_index(a) for a in AXES)
    spin = col ^ ((gx >> 1) & 1)
    toward = jnp.where(gx % 2 == 0, 1, -1)
    dx = jnp.stack([jnp.zeros_like(toward), toward, -toward])
    codes = (dx[:, None] + 1) * 3 + jnp.arange(3, dtype=jnp.int32)[None, :]
    slots = jnp.arange(NB, dtype=jnp.int32)
    index, count = neighbour_index[0], block_count[0]
    match = (index[:, None, None, :] == codes[None, :, :, None]) & (
        slots < count[:, None, None, None]
    )
    found = jnp.sum(jnp.where(match, slots + 1, 0), axis=-1) - 1
    scalars = jnp.stack([spin, col, gy % 2, gx % 2])
    return spin, col, jnp.concatenate([found.reshape(-1), scalars]).astype(jnp.int32)


def shaped(shape, dtype):
    return jax.ShapeDtypeStruct(shape, dtype)


def per_device(start_block, hamiltonian, neighbour_index, block_count):
    sizes = tuple(lax.axis_size(a) for a in AXES)
    members = sizes[0] * sizes[1]
    block, full = (4, T, 2 * T), (2 * T, 2 * T)
    spin, col, m = table(neighbour_index, block_count)

    other = swap_col(sizes, lax.dynamic_index_in_dim(start_block, 1 - spin, 0, keepdims=False)[0])
    own = lax.dynamic_index_in_dim(start_block, spin, 0, keepdims=False)[0]
    spin_block = pl.BlockSpec((1,) + hamiltonian.shape[1:], lambda i, m: (m[SPIN], 0, 0, 0, 0, 0))
    corner = shaped((T, T), BF)
    o, h_p, h_q = call(
        order_kernel, m, [hamiltonian], [shaped((4, T, NB * T), BF), corner, corner], "order", specs=[spin_block]
    )
    tile, two = shaped((1, T, 2 * T), BF), shaped((2, T, 2 * T), BF)
    ext = pltpu.VMEM((6, T, 2 * T), BF)
    v, p, q = call(join_kernel, m, [own, other], [shaped(block, BF), tile, two], "join")

    def apply_ham(o, x, p, q, more, edges, last):
        p, q = swap(sizes, p, 0, 1), swap(sizes, q, 0, 2)
        ends = jnp.concatenate([p[:1], q[:1]], axis=0)
        a, b = swap(sizes, x, 1, 0), swap(sizes, x, 2, 0)
        o, a, b = lax.optimization_barrier((o, a, b))
        a_ends, b_ends = swap(sizes, ends, 1, 0), swap(sizes, ends, 2, 0)
        (acc,) = call(core_kernel, m, [o, x, ends, a, b], [shaped(block, F32)], "core", 32, scratch=[ext])
        out = call(
            functools.partial(rim_kernel, last=last), m, [o, a_ends, b_ends, acc, *more],
            [shaped(block, BF), edges, edges], "rim", 4,
        )
        return o, p, q, out

    o, _, _, (first, p, q) = apply_ham(o, v, p, q, [h_p, h_q], two, False)
    o, h_p, h_q, (second, p, q) = apply_ham(o, first, p, q, [v], tile, True)

    right = shift(sizes, second, -1, 0)
    p, q = swap(sizes, p, 0, 1), swap(sizes, q, 0, 2)
    corr, turned, acc = call(
        corr_kernel, m, [o, second, p, q],
        [shaped(full, F32), shaped((2 * T, 6 * T), BF), shaped(block, F32)], "corr", 16,
    )
    piece = shaped((members // 2, 1, 5 * T), F32)
    mine, theirs = call(
        gram_kernel, m, [o, turned, right, h_p, h_q, acc, corr], [piece, piece], "gram", 30
    )

    rows = members * second.shape[0] * second.shape[1]
    partial = mine + swap(sizes, theirs, 0, 1)
    (both,) = call(stack_kernel, m, [second, swap_col(sizes, second)], [shaped((2, *block), BF)], "stack", 200)
    total = exchange(sizes, partial, False)
    total, both = lax.optimization_barrier((total, both))
    total = total.sum(axis=0, keepdims=True) / rows
    mine = exchange(sizes, jnp.broadcast_to(total, (members, 1, 5 * T)), True)
    theirs = swap(sizes, mine, 0, 1)
    squared = pltpu.VMEM((2, *full), F32)
    return tuple(
        call(
            final_kernel, m, [mine, theirs, both],
            [shaped((2, 1, 4, T, T), BF), shaped((2, 2 * T, T), F32)], "final", 200,
            scratch=[squared, squared, squared],
        )
    )


def solution(mesh):
    return jax.shard_map(
        per_device,
        mesh=mesh,
        in_specs=(
            P(None, "gx", "gy", None, "col"),
            P(None, "gx", "gy", None, None, None),
            P("gx", "gy", None),
            P("gx", "gy"),
        ),
        out_specs=(P(None, "gx", "gy", None, "col"), P(None, None, "col")),
        check_vma=False,
    )
```

```python
import functools

import jax
import jax.numpy as jnp
from jax import lax
from jax.experimental import pallas as pl
from jax.experimental.pallas import tpu as pltpu
from jax.sharding import PartitionSpec as P

NB = 9
T = 128
AXES = ("gx", "gy", "col")
BF = jnp.bfloat16
F32 = jnp.float32
SPIN, COL, PAR_Y, PAR_X = 36, 37, 38, 39


def col_of(gx, spin):
    return spin ^ ((gx >> 1) & 1)


def device(sizes, gx, gy, col):
    return ((gx % sizes[0]) * sizes[1] + gy % sizes[1]) * sizes[2] + col


def pairs(sizes, target):
    out = []
    for gx in range(sizes[0]):
        for gy in range(sizes[1]):
            for spin in range(2):
                there = target(gx, gy)
                there_gx = there[0] % sizes[0]
                out.append(
                    (
                        device(sizes, gx, gy, col_of(gx, spin)),
                        device(sizes, there_gx, there[1], col_of(there_gx, spin)),
                    )
                )
    return out


def partner(index, kind):
    if kind == 0:
        return index
    return index + 1 if (index % 2 == 0) == (kind == 1) else index - 1


def swap(sizes, block, kind_x, kind_y):
    perm = pairs(sizes, lambda gx, gy: (partner(gx, kind_x), partner(gy, kind_y)))
    return lax.ppermute(block, AXES, perm)


def shift(sizes, block, dx, dy):
    return lax.ppermute(block, AXES, pairs(sizes, lambda gx, gy: (gx + dx, gy + dy)))


def swap_col(sizes, block):
    perm = [(d, d ^ 1) for d in range(sizes[0] * sizes[1] * 2)]
    return lax.ppermute(block, AXES, perm)


def exchange(sizes, pieces, joint):
    groups = [
        [
            device(sizes, gx, gy, col_of(gx, spin))
            for gx in range(sizes[0])
            for gy in range(core, sizes[1], 2)
        ]
        for core in range(2)
        for spin in range(2)
    ]
    if joint:
        groups = [groups[0] + groups[1], groups[2] + groups[3]]
    return lax.all_to_all(pieces, AXES, 0, 0, axis_index_groups=groups, tiled=True)


def dot(a, b, dims=((1,), (0,))):
    return lax.dot_general(a, b, (dims, ((), ())), preferred_element_type=F32)


def split(a):
    high = a.astype(BF)
    return high, (a - high.astype(F32)).astype(BF)


def dot3(a, b, dims=((1,), (0,))):
    (ah, al), (bh, bl) = split(a), split(b)
    return dot(ah, bh, dims) + (dot(ah, bl, dims) + dot(al, bh, dims))


def order_kernel(m, h, o, p, q):
    def block(tile, at):
        slot = m[tile * 9 + at]
        found = h[0, 0, tile, jnp.maximum(slot, 0)]
        return jnp.where(slot >= 0, found, jnp.zeros_like(found))

    for tile in range(4):
        for at in range(9):
            o[tile, :, at * T : (at + 1) * T] = block(tile, at)
    even = m[PAR_Y] == 0
    side = 1 + m[PAR_X]
    down, up = block(0, side * 3), block(3, side * 3 + 2)
    p[...] = jnp.where(even, up, down)
    q[...] = jnp.where(even, down, up)


def blocks(o, tile, sides, dys):
    out = []
    for side in sides:
        at = (side * 3 + dys[0]) * T
        if not isinstance(side, int):
            at = pl.multiple_of(at, T)
        out.append(o[tile, :, pl.ds(at, len(dys) * T)])
    return out[0] if len(out) == 1 else jnp.concatenate(out, axis=1)


def store_edges(m, ref, p, q):
    even = m[PAR_Y] == 0
    p[0:1] = ref[pl.ds(jnp.where(even, 3, 0), 1)]
    q[0:1] = ref[pl.ds(jnp.where(even, 0, 3), 1)]


def join_kernel(m, own, other, v, p, q):
    first_col = m[COL] == 0
    v[:, :, :T] = jnp.where(first_col, own[...], other[...])
    v[:, :, T:] = jnp.where(first_col, other[...], own[...])
    store_edges(m, v, p, q)
    q[1:2] = v[1:2]


def ends_of(m, ends):
    even = m[PAR_Y] == 0
    return jnp.where(even, ends[1:2], ends[0:1]), jnp.where(even, ends[0:1], ends[1:2])


def product(o, tile, sides, at, sources):
    row = blocks(o, tile, sides, [place - tile for place in at])
    return dot(row, jnp.concatenate([x.reshape(len(at) * T, 2 * T) for x in sources], axis=0))


def core_kernel(m, o, x, ends, a, b, acc, ext):
    low, high = ends_of(m, ends)
    ext[0:1] = low
    ext[1:5] = x[...]
    ext[5:6] = high
    for tile in range(4):
        total = product(o, tile, (0,), range(tile, tile + 3), [ext[tile : tile + 3]])
        at = [place for place in range(tile, tile + 3) if 1 <= place <= 4]
        sources = [y[at[0] - 1 : at[-1]] for y in (a, b)]
        acc[tile] = total + product(o, tile, (1, 2), at, sources)


def rim_kernel(m, o, a_ends, b_ends, acc, *rest, last):
    *more, out, p, q = rest
    low, high = zip(ends_of(m, a_ends), ends_of(m, b_ends))
    for tile in range(4):
        total = acc[tile]
        if tile == 0:
            total += product(o, tile, (1, 2), (0,), low)
        if tile == 3:
            total += product(o, tile, (1, 2), (5,), high)
        if last:
            out[tile] = (total - more[0][tile].astype(F32)).astype(BF)
        else:
            out[tile] = (0.5 * total).astype(BF)
    store_edges(m, out, p, q)
    if not last:
        for to, block in zip((p, q), more):
            to[1, :, :T] = block[...]
            to[1, :, T:] = block[...]


def corr_kernel(m, o, s, corr, turned, acc):
    flat = s[...].reshape(4 * T, 2 * T)
    turned[...] = flat.T
    corr[...] = dot(turned[...], flat)
    for tile in range(4):
        total = 0.5 * dot(blocks(o, tile, (0,), (1,)), s[tile])
        if tile < 3:
            total += dot(blocks(o, tile, (0,), (2,)), s[tile + 1])
        acc[tile] = total


def places():
    shape = (2 * T, 2 * T)
    return lax.broadcasted_iota(jnp.int32, shape, 0), lax.broadcasted_iota(jnp.int32, shape, 1)


def gram_kernel(m, o, turned, p, q, right, h_p, h_q, acc, corr, mine, theirs):
    side = 1 + m[PAR_X]
    parts = []
    for tile in range(4):
        at = [place for place in range(tile, tile + 3) if 1 <= place <= 4]
        parts.append(acc[tile] + product(o, tile, (side,), at, [right[at[0] - 1 : at[-1]]]))
    even = m[PAR_Y] == 0
    above = jnp.where(even, p[...], q[...])
    parts[3] += product(o, 3, (0,), (5,), [above])
    high, low = split(jnp.concatenate(parts, axis=0))
    half = dot(turned[...], high) + dot(turned[...], low)
    for tile, block, at in ((p, h_p, jnp.where(even, 3, 0)), (q, h_q, jnp.where(even, 0, 3))):
        high, low = split(dot(block[1, :, :T], right[at]))
        half += dot(tile[0], high, ((0,), (0,))) + dot(tile[0], low, ((0,), (0,)))
    coupling = half + half.T
    rows, cols = places()
    both = jnp.where(rows >= cols, corr[...], coupling)
    diagonal = jnp.sum(jnp.where(rows == cols, coupling, 0.0), axis=1, keepdims=True)
    first, second = pack(both[:T], diagonal[:T]), pack(both[T:], diagonal[T:])
    even = m[PAR_Y] == 0
    mine[:, 0, :] = jnp.where(even, first, second)
    theirs[:, 0, :] = jnp.where(even, second, first)


def pack(square, diagonal):
    lane = lax.broadcasted_iota(jnp.int32, (T // 2, T), 1)
    extra = jnp.where(lane == 0, diagonal[: T // 2], jnp.where(lane == 1, diagonal[T // 2 :], 0.0))
    return jnp.concatenate([square[: T // 2], square[T // 2 :], extra], axis=1)


def unpack(table):
    square = jnp.concatenate([table[:, : 2 * T], table[:, 2 * T : 4 * T]], axis=0)
    return square, jnp.concatenate([table[:, 4 * T : 4 * T + 1], table[:, 4 * T + 1 : 4 * T + 2]], axis=0)


def lower_part(e, rows, cols):
    return jnp.where(rows > cols, e, jnp.where(rows == cols, 0.5 * e, 0.0))


def squares(m, mine, theirs, spin):
    even = m[PAR_Y] == 0
    half = slice(spin * T // 2, (spin + 1) * T // 2)
    first, second = mine[half, 0, :], theirs[half, 0, :]
    top = unpack(jnp.where(even, first, second))
    bottom = unpack(jnp.where(even, second, first))
    both = jnp.concatenate([top[0], bottom[0]], axis=0)
    diagonal = jnp.concatenate([top[1], bottom[1]], axis=0)
    rows, cols = places()
    turned = both.T
    corr = jnp.where(rows >= cols, both, turned)
    return corr, jnp.where(rows < cols, both, jnp.where(rows == cols, diagonal, turned))


def stack_kernel(m, s, other, both):
    both[pl.ds(m[SPIN], 1)] = s[...][None]
    both[pl.ds(1 - m[SPIN], 1)] = other[...][None]


def final_kernel(m, mine, theirs, both, ritz, projected, x_ref, a_ref, k_ref):
    rows, cols = places()
    unit = (rows == cols).astype(F32)
    scales = []
    for spin in range(2):
        corr, k_ref[spin] = squares(m, mine, theirs, spin)
        on_diagonal = jnp.where(rows == cols, corr, 0.0)
        scale_row = 1.0 / jnp.sqrt(jnp.sum(on_diagonal, axis=0, keepdims=True))
        scale_col = 1.0 / jnp.sqrt(jnp.sum(on_diagonal, axis=1, keepdims=True))
        scaled = corr * scale_row * scale_col
        scales.append(scale_row)
        a_ref[spin] = scaled
        e = scaled - unit
        f = lower_part(e, rows, cols)
        f_half = f.astype(BF)
        fe = dot(f_half, e.astype(BF))
        e = dot((f + fe - e).astype(BF), f_half, ((1,), (1,))) - fe
        x = unit - f
        x_ref[spin] = x - dot(lower_part(e, rows, cols).astype(BF), x.astype(BF))

    def step(state):
        count, _, _ = state
        xs = [x_ref[spin] for spin in range(2)]
        es = [dot3(xs[spin], a_ref[spin]) for spin in range(2)]
        es = [dot3(es[spin], xs[spin], ((1,), (1,))) - unit for spin in range(2)]
        for spin in range(2):
            x_ref[spin] = xs[spin] - dot(lower_part(es[spin], rows, cols).astype(BF), xs[spin].astype(BF))
        return count + 1, jnp.sum(es[0] * es[0]), jnp.sum(es[1] * es[1])

    def more(state):
        count, *sizes = state
        largest = jnp.maximum(*sizes)
        return (count < 12) & (largest >= 4e-6) & (largest < 1e4)

    _, *sizes = lax.while_loop(more, step, (0, F32(1.0), F32(1.0)))

    for spin in range(2):

        @pl.when(jnp.logical_not(sizes[spin] < 4e-6))
        def _(spin=spin):
            x_ref[spin] = unit

            def eliminate(j, carry):
                row = a_ref[spin, pl.ds(j, 1), :]
                pivot = jnp.sum(jnp.where(cols[:1] == j, row, 0.0), axis=1, keepdims=True)
                a = a_ref[spin]
                column = jnp.sum(jnp.where(cols == j, a, 0.0), axis=1, keepdims=True)
                factor = jnp.where(rows[:, :1] > j, column / pivot, 0.0)
                x = x_ref[spin]
                x_row = x_ref[spin, pl.ds(j, 1), :]
                a_ref[spin] = a - factor * row
                x_ref[spin] = x - factor * x_row
                return carry

            lax.fori_loop(0, 2 * T, eliminate, 0)
            pivots = jnp.sum(jnp.where(rows == cols, a_ref[spin], 0.0), axis=1, keepdims=True)
            x_ref[spin] = x_ref[spin] / jnp.sqrt(pivots)

    first_col = m[COL] == 0
    for spin in range(2):
        x = x_ref[spin] * scales[spin]
        part = jnp.where(first_col, x[:T], x[T:])
        ritz[spin, 0] = dot(both[spin].reshape(4 * T, 2 * T), part.astype(BF), ((1,), (1,))).astype(BF).reshape(4, T, T)
        projected[spin] = dot3(dot3(x, k_ref[spin]), part, ((1,), (1,)))


def whole(shape):
    return pl.BlockSpec(shape, lambda i, m, n=len(shape): (0,) * n)


def call(kernel, m, arrays, outs, name, flops=0, specs=None, scratch=()):
    arrays = list(arrays)
    moved = sum(a.size * a.dtype.itemsize for a in [*arrays, *outs])
    return pl.pallas_call(
        kernel,
        out_shape=outs,
        grid_spec=pltpu.PrefetchScalarGridSpec(
            num_scalar_prefetch=1,
            grid=(1,),
            in_specs=specs or [whole(a.shape) for a in arrays],
            out_specs=[whole(o.shape) for o in outs],
            scratch_shapes=list(scratch),
        ),
        compiler_params=pltpu.CompilerParams(vmem_limit_bytes=32 * 1024 * 1024),
        cost_estimate=pl.CostEstimate(flops=2 * T * T * 2 * T * flops, bytes_accessed=moved, transcendentals=0),
        name=name,
    )(m, *arrays)


def table(neighbour_index, block_count):
    gx, gy, col = (lax.axis_index(a) for a in AXES)
    spin = col ^ ((gx >> 1) & 1)
    toward = jnp.where(gx % 2 == 0, 1, -1)
    dx = jnp.stack([jnp.zeros_like(toward), toward, -toward])
    codes = (dx[:, None] + 1) * 3 + jnp.arange(3, dtype=jnp.int32)[None, :]
    slots = jnp.arange(NB, dtype=jnp.int32)
    index, count = neighbour_index[0], block_count[0]
    match = (index[:, None, None, :] == codes[None, :, :, None]) & (
        slots < count[:, None, None, None]
    )
    found = jnp.sum(jnp.where(match, slots + 1, 0), axis=-1) - 1
    scalars = jnp.stack([spin, col, gy % 2, gx % 2])
    return spin, col, jnp.concatenate([found.reshape(-1), scalars]).astype(jnp.int32)


def shaped(shape, dtype):
    return jax.ShapeDtypeStruct(shape, dtype)


def per_device(start_block, hamiltonian, neighbour_index, block_count):
    sizes = tuple(lax.axis_size(a) for a in AXES)
    members = sizes[0] * sizes[1]
    block, full = (4, T, 2 * T), (2 * T, 2 * T)
    spin, col, m = table(neighbour_index, block_count)

    other = swap_col(sizes, lax.dynamic_index_in_dim(start_block, 1 - spin, 0, keepdims=False)[0])
    own = lax.dynamic_index_in_dim(start_block, spin, 0, keepdims=False)[0]
    spin_block = pl.BlockSpec((1,) + hamiltonian.shape[1:], lambda i, m: (m[SPIN], 0, 0, 0, 0, 0))
    corner = shaped((T, T), BF)
    o, h_p, h_q = call(
        order_kernel, m, [hamiltonian], [shaped((4, T, NB * T), BF), corner, corner], "order", specs=[spin_block]
    )
    tile, two = shaped((1, T, 2 * T), BF), shaped((2, T, 2 * T), BF)
    ext = pltpu.VMEM((6, T, 2 * T), BF)
    v, p, q = call(join_kernel, m, [own, other], [shaped(block, BF), tile, two], "join")

    def apply_ham(o, x, p, q, more, edges, last):
        p, q = swap(sizes, p, 0, 1), swap(sizes, q, 0, 2)
        ends = jnp.concatenate([p[:1], q[:1]], axis=0)
        a, b = swap(sizes, x, 1, 0), swap(sizes, x, 2, 0)
        o, a, b = lax.optimization_barrier((o, a, b))
        a_ends, b_ends = swap(sizes, ends, 1, 0), swap(sizes, ends, 2, 0)
        (acc,) = call(core_kernel, m, [o, x, ends, a, b], [shaped(block, F32)], "core", 32, scratch=[ext])
        out = call(
            functools.partial(rim_kernel, last=last), m, [o, a_ends, b_ends, acc, *more],
            [shaped(block, BF), edges, edges], "rim", 4,
        )
        return o, p, q, out

    o, _, _, (first, p, q) = apply_ham(o, v, p, q, [h_p, h_q], two, False)
    o, h_p, h_q, (second, p, q) = apply_ham(o, first, p, q, [v], tile, True)

    right = shift(sizes, second, -1, 0)
    p, q = swap(sizes, p, 0, 1), swap(sizes, q, 0, 2)
    corr, turned, acc = call(
        corr_kernel, m, [o, second], [shaped(full, F32), shaped((2 * T, 4 * T), BF), shaped(block, F32)], "corr", 15
    )
    piece = shaped((members // 2, 1, 5 * T), F32)
    mine, theirs = call(
        gram_kernel, m, [o, turned, p, q, right, h_p, h_q, acc, corr], [piece, piece], "gram", 30
    )

    rows = members * second.shape[0] * second.shape[1]
    partial = mine + swap(sizes, theirs, 0, 1)
    (both,) = call(stack_kernel, m, [second, swap_col(sizes, second)], [shaped((2, *block), BF)], "stack", 200)
    total = exchange(sizes, partial, False)
    total, both = lax.optimization_barrier((total, both))
    total = total.sum(axis=0, keepdims=True) / rows
    mine = exchange(sizes, jnp.broadcast_to(total, (members, 1, 5 * T)), True)
    theirs = swap(sizes, mine, 0, 1)
    squared = pltpu.VMEM((2, *full), F32)
    return tuple(
        call(
            final_kernel, m, [mine, theirs, both],
            [shaped((2, 1, 4, T, T), BF), shaped((2, 2 * T, T), F32)], "final", 200,
            scratch=[squared, squared, squared],
        )
    )


def solution(mesh):
    return jax.shard_map(
        per_device,
        mesh=mesh,
        in_specs=(
            P(None, "gx", "gy", None, "col"),
            P(None, "gx", "gy", None, None, None),
            P("gx", "gy", None),
            P("gx", "gy"),
        ),
        out_specs=(P(None, "gx", "gy", None, "col"), P(None, None, "col")),
        check_vma=False,
    )
```

```python
import functools

import jax
import jax.numpy as jnp
from jax import lax
from jax.experimental import pallas as pl
from jax.experimental.pallas import tpu as pltpu
from jax.sharding import PartitionSpec as P

NB = 9
T = 128
AXES = ("gx", "gy", "col")
BF = jnp.bfloat16
F32 = jnp.float32
SPIN, COL, PAR_Y, PAR_X = 36, 37, 38, 39
HEAD = 16
PAD = 32


def col_of(gx, spin):
    return spin ^ ((gx >> 1) & 1)


def device(sizes, gx, gy, col):
    return ((gx % sizes[0]) * sizes[1] + gy % sizes[1]) * sizes[2] + col


def pairs(sizes, target):
    out = []
    for gx in range(sizes[0]):
        for gy in range(sizes[1]):
            for spin in range(2):
                there = target(gx, gy)
                there_gx = there[0] % sizes[0]
                out.append(
                    (
                        device(sizes, gx, gy, col_of(gx, spin)),
                        device(sizes, there_gx, there[1], col_of(there_gx, spin)),
                    )
                )
    return out


def partner(index, kind):
    if kind == 0:
        return index
    return index + 1 if (index % 2 == 0) == (kind == 1) else index - 1


def swap(sizes, block, kind_x, kind_y):
    perm = pairs(sizes, lambda gx, gy: (partner(gx, kind_x), partner(gy, kind_y)))
    return lax.ppermute(block, AXES, perm)


def shift(sizes, block, dx, dy):
    return lax.ppermute(block, AXES, pairs(sizes, lambda gx, gy: (gx + dx, gy + dy)))


def swap_col(sizes, block):
    perm = [(d, d ^ 1) for d in range(sizes[0] * sizes[1] * 2)]
    return lax.ppermute(block, AXES, perm)


def exchange(sizes, pieces, joint):
    groups = [
        [
            device(sizes, gx, gy, col_of(gx, spin))
            for gx in range(sizes[0])
            for gy in range(core, sizes[1], 2)
        ]
        for core in range(2)
        for spin in range(2)
    ]
    if joint:
        groups = [groups[0] + groups[1], groups[2] + groups[3]]
    return lax.all_to_all(pieces, AXES, 0, 0, axis_index_groups=groups, tiled=True)


def dot(a, b, dims=((1,), (0,))):
    return lax.dot_general(a, b, (dims, ((), ())), preferred_element_type=F32)


def split(a):
    high = a.astype(BF)
    return high, (a - high.astype(F32)).astype(BF)


def dot3(a, b, dims=((1,), (0,))):
    (ah, al), (bh, bl) = split(a), split(b)
    return dot(ah, bh, dims) + (dot(ah, bl, dims) + dot(al, bh, dims))


def order_kernel(m, h, o, p, q):
    def block(tile, at):
        slot = m[tile * 9 + at]
        found = h[0, 0, tile, jnp.maximum(slot, 0)]
        return jnp.where(slot >= 0, found, jnp.zeros_like(found))

    for tile in range(4):
        for at in range(9):
            o[tile, :, at * T : (at + 1) * T] = block(tile, at)
    even = m[PAR_Y] == 0
    side = 1 + m[PAR_X]
    down, up = block(0, side * 3), block(3, side * 3 + 2)
    p[...] = jnp.where(even, up, down)
    q[...] = jnp.where(even, down, up)


def blocks(o, tile, sides, dys):
    out = []
    for side in sides:
        at = (side * 3 + dys[0]) * T
        if not isinstance(side, int):
            at = pl.multiple_of(at, T)
        out.append(o[tile, :, pl.ds(at, len(dys) * T)])
    return out[0] if len(out) == 1 else jnp.concatenate(out, axis=1)


def store_edges(m, ref, p, q):
    even = m[PAR_Y] == 0
    p[...] = ref[pl.ds(jnp.where(even, 3, 0), 1)].reshape(T, 2 * T)
    q[...] = ref[pl.ds(jnp.where(even, 0, 3), 1)].reshape(T, 2 * T)


def store_bulk(ref, to_b, to_a):
    flat = ref[...].reshape(4 * T, 2 * T)
    to_b[...] = flat[HEAD:]
    to_a[: 4 * T] = flat
    to_a[4 * T :] = flat[:PAD]


def join_kernel(m, own, other, v, p, q, to_b, to_a):
    first_col = m[COL] == 0
    v[:, :, :T] = jnp.where(first_col, own[...], other[...])
    v[:, :, T:] = jnp.where(first_col, other[...], own[...])
    store_edges(m, v, p, q)
    store_bulk(v, to_b, to_a)


def ends_of(m, ends):
    even = m[PAR_Y] == 0
    p, q = ends[:T], ends[ends.shape[0] - T :]
    return jnp.where(even, q, p), jnp.where(even, p, q)


def product(o, tile, sides, at, sources):
    row = blocks(o, tile, sides, [place - tile for place in at])
    return dot(row, jnp.concatenate([x.reshape(len(at) * T, 2 * T) for x in sources], axis=0))


def core_kernel(m, o, x, ends, a, b, acc, ext):
    low, high = ends_of(m, ends)
    ext[0] = low
    ext[1:5] = x[...]
    ext[5] = high
    for tile in range(4):
        total = product(o, tile, (0,), range(tile, tile + 3), [ext[tile : tile + 3]])
        at = [place for place in range(tile, tile + 3) if 1 <= place <= 4]
        total += product(o, tile, (1,), at, [a[(at[0] - 1) * T : at[-1] * T]])
        at = [place for place in at if place > 1]
        acc[tile] = total + product(o, tile, (2,), at, [b[(at[0] - 1) * T - HEAD : at[-1] * T - HEAD]])


def rim_kernel(m, o, b, a_ends, b_ends, acc, *rest, last):
    if last:
        before, out, p, q = rest
    else:
        out, p, q, to_b, to_a = rest
    low, high = zip(ends_of(m, a_ends), ends_of(m, b_ends))
    first = jnp.concatenate([b_ends[T : T + HEAD], b[: T - HEAD]], axis=0)
    for tile in range(4):
        total = acc[tile]
        if tile == 0:
            total += product(o, tile, (2,), (0, 1), [jnp.concatenate([low[1], first], axis=0)])
            total += product(o, tile, (1,), (0,), [low[0]])
        if tile == 1:
            total += product(o, tile, (2,), (1,), [first])
        if tile == 3:
            total += product(o, tile, (1, 2), (5,), high)
        if last:
            out[tile] = (total - before[tile].astype(F32)).astype(BF)
        else:
            out[tile] = (0.5 * total).astype(BF)
    store_edges(m, out, p, q)
    if not last:
        store_bulk(out, to_b, to_a)


def corr_kernel(m, o, s, corr, turned, acc):
    flat = s[...].reshape(4 * T, 2 * T)
    turned[...] = flat.T
    corr[...] = dot(turned[...], flat)
    for tile in range(4):
        total = 0.5 * dot(blocks(o, tile, (0,), (1,)), s[tile])
        if tile < 3:
            total += dot(blocks(o, tile, (0,), (2,)), s[tile + 1])
        acc[tile] = total


def places():
    shape = (2 * T, 2 * T)
    return lax.broadcasted_iota(jnp.int32, shape, 0), lax.broadcasted_iota(jnp.int32, shape, 1)


def gram_kernel(m, o, turned, p, q, right, h_p, h_q, acc, corr, mine, theirs):
    side = 1 + m[PAR_X]
    parts = []
    for tile in range(4):
        at = [place for place in range(tile, tile + 3) if 1 <= place <= 4]
        parts.append(acc[tile] + product(o, tile, (side,), at, [right[at[0] - 1 : at[-1]]]))
    even = m[PAR_Y] == 0
    above = jnp.where(even, p[...], q[...])
    parts[3] += product(o, 3, (0,), (5,), [above])
    high, low = split(jnp.concatenate(parts, axis=0))
    half = dot(turned[...], high) + dot(turned[...], low)
    for tile, block, at in ((p, h_p, jnp.where(even, 3, 0)), (q, h_q, jnp.where(even, 0, 3))):
        high, low = split(dot(block[...], right[at]))
        half += dot(tile[...], high, ((0,), (0,))) + dot(tile[...], low, ((0,), (0,)))
    coupling = half + half.T
    rows, cols = places()
    both = jnp.where(rows >= cols, corr[...], coupling)
    diagonal = jnp.sum(jnp.where(rows == cols, coupling, 0.0), axis=1, keepdims=True)
    first, second = pack(both[:T], diagonal[:T]), pack(both[T:], diagonal[T:])
    even = m[PAR_Y] == 0
    mine[:, 0, :] = jnp.where(even, first, second)
    theirs[:, 0, :] = jnp.where(even, second, first)


def pack(square, diagonal):
    lane = lax.broadcasted_iota(jnp.int32, (T // 2, T), 1)
    extra = jnp.where(lane == 0, diagonal[: T // 2], jnp.where(lane == 1, diagonal[T // 2 :], 0.0))
    return jnp.concatenate([square[: T // 2], square[T // 2 :], extra], axis=1)


def unpack(table):
    square = jnp.concatenate([table[:, : 2 * T], table[:, 2 * T : 4 * T]], axis=0)
    return square, jnp.concatenate([table[:, 4 * T : 4 * T + 1], table[:, 4 * T + 1 : 4 * T + 2]], axis=0)


def lower_part(e, rows, cols):
    return jnp.where(rows > cols, e, jnp.where(rows == cols, 0.5 * e, 0.0))


def squares(m, mine, theirs, spin):
    even = m[PAR_Y] == 0
    half = slice(spin * T // 2, (spin + 1) * T // 2)
    first, second = mine[half, 0, :], theirs[half, 0, :]
    top = unpack(jnp.where(even, first, second))
    bottom = unpack(jnp.where(even, second, first))
    both = jnp.concatenate([top[0], bottom[0]], axis=0)
    diagonal = jnp.concatenate([top[1], bottom[1]], axis=0)
    rows, cols = places()
    turned = both.T
    corr = jnp.where(rows >= cols, both, turned)
    return corr, jnp.where(rows < cols, both, jnp.where(rows == cols, diagonal, turned))


def stack_kernel(m, s, other, both):
    both[pl.ds(m[SPIN], 1)] = s[...][None]
    both[pl.ds(1 - m[SPIN], 1)] = other[...][None]


def final_kernel(m, mine, theirs, both, ritz, projected, x_ref, a_ref, k_ref):
    rows, cols = places()
    unit = (rows == cols).astype(F32)
    scales = []
    for spin in range(2):
        corr, k_ref[spin] = squares(m, mine, theirs, spin)
        on_diagonal = jnp.where(rows == cols, corr, 0.0)
        scale_row = 1.0 / jnp.sqrt(jnp.sum(on_diagonal, axis=0, keepdims=True))
        scale_col = 1.0 / jnp.sqrt(jnp.sum(on_diagonal, axis=1, keepdims=True))
        scaled = corr * scale_row * scale_col
        scales.append(scale_row)
        a_ref[spin] = scaled
        e = scaled - unit
        f = lower_part(e, rows, cols)
        f_half = f.astype(BF)
        fe = dot(f_half, e.astype(BF))
        e = dot((f + fe - e).astype(BF), f_half, ((1,), (1,))) - fe
        x = unit - f
        x_ref[spin] = x - dot(lower_part(e, rows, cols).astype(BF), x.astype(BF))

    def step(state):
        count, _, _ = state
        xs = [x_ref[spin] for spin in range(2)]
        es = [dot3(xs[spin], a_ref[spin]) for spin in range(2)]
        es = [dot3(es[spin], xs[spin], ((1,), (1,))) - unit for spin in range(2)]
        for spin in range(2):
            x_ref[spin] = xs[spin] - dot(lower_part(es[spin], rows, cols).astype(BF), xs[spin].astype(BF))
        return count + 1, jnp.sum(es[0] * es[0]), jnp.sum(es[1] * es[1])

    def more(state):
        count, *sizes = state
        largest = jnp.maximum(*sizes)
        return (count < 12) & (largest >= 4e-6) & (largest < 1e4)

    _, *sizes = lax.while_loop(more, step, (0, F32(1.0), F32(1.0)))

    for spin in range(2):

        @pl.when(jnp.logical_not(sizes[spin] < 4e-6))
        def _(spin=spin):
            x_ref[spin] = unit

            def eliminate(j, carry):
                row = a_ref[spin, pl.ds(j, 1), :]
                pivot = jnp.sum(jnp.where(cols[:1] == j, row, 0.0), axis=1, keepdims=True)
                a = a_ref[spin]
                column = jnp.sum(jnp.where(cols == j, a, 0.0), axis=1, keepdims=True)
                factor = jnp.where(rows[:, :1] > j, column / pivot, 0.0)
                x = x_ref[spin]
                x_row = x_ref[spin, pl.ds(j, 1), :]
                a_ref[spin] = a - factor * row
                x_ref[spin] = x - factor * x_row
                return carry

            lax.fori_loop(0, 2 * T, eliminate, 0)
            pivots = jnp.sum(jnp.where(rows == cols, a_ref[spin], 0.0), axis=1, keepdims=True)
            x_ref[spin] = x_ref[spin] / jnp.sqrt(pivots)

    first_col = m[COL] == 0
    for spin in range(2):
        x = x_ref[spin] * scales[spin]
        part = jnp.where(first_col, x[:T], x[T:])
        ritz[spin, 0] = dot(both[spin].reshape(4 * T, 2 * T), part.astype(BF), ((1,), (1,))).astype(BF).reshape(4, T, T)
        projected[spin] = dot3(dot3(x, k_ref[spin]), part, ((1,), (1,)))


def whole(shape):
    return pl.BlockSpec(shape, lambda i, m, n=len(shape): (0,) * n)


def call(kernel, m, arrays, outs, name, flops=0, specs=None, scratch=()):
    arrays = list(arrays)
    moved = sum(a.size * a.dtype.itemsize for a in [*arrays, *outs])
    return pl.pallas_call(
        kernel,
        out_shape=outs,
        grid_spec=pltpu.PrefetchScalarGridSpec(
            num_scalar_prefetch=1,
            grid=(1,),
            in_specs=specs or [whole(a.shape) for a in arrays],
            out_specs=[whole(o.shape) for o in outs],
            scratch_shapes=list(scratch),
        ),
        compiler_params=pltpu.CompilerParams(vmem_limit_bytes=32 * 1024 * 1024),
        cost_estimate=pl.CostEstimate(flops=2 * T * T * 2 * T * flops, bytes_accessed=moved, transcendentals=0),
        name=name,
    )(m, *arrays)


def table(neighbour_index, block_count):
    gx, gy, col = (lax.axis_index(a) for a in AXES)
    spin = col ^ ((gx >> 1) & 1)
    toward = jnp.where(gx % 2 == 0, 1, -1)
    dx = jnp.stack([jnp.zeros_like(toward), toward, -toward])
    codes = (dx[:, None] + 1) * 3 + jnp.arange(3, dtype=jnp.int32)[None, :]
    slots = jnp.arange(NB, dtype=jnp.int32)
    index, count = neighbour_index[0], block_count[0]
    match = (index[:, None, None, :] == codes[None, :, :, None]) & (
        slots < count[:, None, None, None]
    )
    found = jnp.sum(jnp.where(match, slots + 1, 0), axis=-1) - 1
    scalars = jnp.stack([spin, col, gy % 2, gx % 2])
    return spin, col, jnp.concatenate([found.reshape(-1), scalars]).astype(jnp.int32)


def shaped(shape, dtype):
    return jax.ShapeDtypeStruct(shape, dtype)


def per_device(start_block, hamiltonian, neighbour_index, block_count):
    sizes = tuple(lax.axis_size(a) for a in AXES)
    members = sizes[0] * sizes[1]
    block, full = (4, T, 2 * T), (2 * T, 2 * T)
    spin, col, m = table(neighbour_index, block_count)

    other = swap_col(sizes, lax.dynamic_index_in_dim(start_block, 1 - spin, 0, keepdims=False)[0])
    own = lax.dynamic_index_in_dim(start_block, spin, 0, keepdims=False)[0]
    spin_block = pl.BlockSpec((1,) + hamiltonian.shape[1:], lambda i, m: (m[SPIN], 0, 0, 0, 0, 0))
    corner = shaped((T, T), BF)
    o, h_p, h_q = call(
        order_kernel, m, [hamiltonian], [shaped((4, T, NB * T), BF), corner, corner], "order", specs=[spin_block]
    )
    h_p, h_q = swap(sizes, h_p, 0, 1), swap(sizes, h_q, 0, 2)
    tile = shaped((T, 2 * T), BF)
    ext = pltpu.VMEM((6, T, 2 * T), BF)
    other, o = lax.optimization_barrier((other, o))
    bulk = [shaped((4 * T - HEAD, 2 * T), BF), shaped((4 * T + PAD, 2 * T), BF)]
    outs = [shaped(block, BF), tile, tile, *bulk]
    v, p, q, *rest = call(join_kernel, m, [own, other], outs, "join")

    def apply_ham(x, p, q, rest, more, outs, *kept):
        p, q = swap(sizes, p, 0, 1), swap(sizes, q, 0, 2)
        ends = jnp.concatenate([p, q], axis=0)
        a, b = swap(sizes, rest[1], 1, 0), swap(sizes, rest[0], 2, 0)
        a_ends = swap(sizes, ends, 1, 0)
        b_ends = swap(sizes, jnp.concatenate([p, x[0, :HEAD], q], axis=0), 2, 0)
        (acc,) = call(core_kernel, m, [o, x, ends, a, b], [shaped(block, F32)], "core", 31, scratch=[ext])
        acc, *kept = lax.optimization_barrier((acc, *kept))
        kernel = functools.partial(rim_kernel, last=len(more) > 0)
        return call(kernel, m, [o, b, a_ends, b_ends, acc, *more], outs, "rim", 6), kept

    (first, p, q, *rest), (h_p, h_q) = apply_ham(v, p, q, rest, [], outs, h_p, h_q)
    (second, p, q), _ = apply_ham(first, p, q, rest, [v], outs[:3])

    right = shift(sizes, second, -1, 0)
    p, q = swap(sizes, p, 0, 1), swap(sizes, q, 0, 2)
    corr, turned, acc = call(
        corr_kernel, m, [o, second], [shaped(full, F32), shaped((2 * T, 4 * T), BF), shaped(block, F32)], "corr", 15
    )
    piece = shaped((members // 2, 1, 5 * T), F32)
    mine, theirs = call(
        gram_kernel, m, [o, turned, p, q, right, h_p, h_q, acc, corr], [piece, piece], "gram", 30
    )

    rows = members * second.shape[0] * second.shape[1]
    partial = mine + swap(sizes, theirs, 0, 1)
    (both,) = call(stack_kernel, m, [second, swap_col(sizes, second)], [shaped((2, *block), BF)], "stack", 200)
    total = exchange(sizes, partial, False)
    total, both = lax.optimization_barrier((total, both))
    total = total.sum(axis=0, keepdims=True) / rows
    mine = exchange(sizes, jnp.broadcast_to(total, (members, 1, 5 * T)), True)
    theirs = swap(sizes, mine, 0, 1)
    squared = pltpu.VMEM((2, *full), F32)
    return tuple(
        call(
            final_kernel, m, [mine, theirs, both],
            [shaped((2, 1, 4, T, T), BF), shaped((2, 2 * T, T), F32)], "final", 200,
            scratch=[squared, squared, squared],
        )
    )


def solution(mesh):
    return jax.shard_map(
        per_device,
        mesh=mesh,
        in_specs=(
            P(None, "gx", "gy", None, "col"),
            P(None, "gx", "gy", None, None, None),
            P("gx", "gy", None),
            P("gx", "gy"),
        ),
        out_specs=(P(None, "gx", "gy", None, "col"), P(None, None, "col")),
        check_vma=False,
    )
```

```python
import functools

import jax
import jax.numpy as jnp
from jax import lax
from jax.experimental import pallas as pl
from jax.experimental.pallas import tpu as pltpu
from jax.sharding import PartitionSpec as P

NB = 9
T = 128
AXES = ("gx", "gy", "col")
BF = jnp.bfloat16
F32 = jnp.float32
SPIN, COL, PAR_Y, PAR_X = 36, 37, 38, 39
HEAD = 16
PAD = 32


def col_of(gx, spin):
    return spin ^ ((gx >> 1) & 1)


def device(sizes, gx, gy, col):
    return ((gx % sizes[0]) * sizes[1] + gy % sizes[1]) * sizes[2] + col


def pairs(sizes, target):
    out = []
    for gx in range(sizes[0]):
        for gy in range(sizes[1]):
            for spin in range(2):
                there = target(gx, gy)
                there_gx = there[0] % sizes[0]
                out.append(
                    (
                        device(sizes, gx, gy, col_of(gx, spin)),
                        device(sizes, there_gx, there[1], col_of(there_gx, spin)),
                    )
                )
    return out


def partner(index, kind):
    if kind == 0:
        return index
    return index + 1 if (index % 2 == 0) == (kind == 1) else index - 1


def swap(sizes, block, kind_x, kind_y):
    perm = pairs(sizes, lambda gx, gy: (partner(gx, kind_x), partner(gy, kind_y)))
    return lax.ppermute(block, AXES, perm)


def shift(sizes, block, dx, dy):
    return lax.ppermute(block, AXES, pairs(sizes, lambda gx, gy: (gx + dx, gy + dy)))


def swap_col(sizes, block):
    perm = [(d, d ^ 1) for d in range(sizes[0] * sizes[1] * 2)]
    return lax.ppermute(block, AXES, perm)


def exchange(sizes, pieces, joint):
    groups = [
        [
            device(sizes, gx, gy, col_of(gx, spin))
            for gx in range(sizes[0])
            for gy in range(core, sizes[1], 2)
        ]
        for core in range(2)
        for spin in range(2)
    ]
    if joint:
        groups = [groups[0] + groups[1], groups[2] + groups[3]]
    return lax.all_to_all(pieces, AXES, 0, 0, axis_index_groups=groups, tiled=True)


def dot(a, b, dims=((1,), (0,))):
    return lax.dot_general(a, b, (dims, ((), ())), preferred_element_type=F32)


def split(a):
    high = a.astype(BF)
    return high, (a - high.astype(F32)).astype(BF)


def dot3(a, b, dims=((1,), (0,))):
    (ah, al), (bh, bl) = split(a), split(b)
    return dot(ah, bh, dims) + (dot(ah, bl, dims) + dot(al, bh, dims))


def order_kernel(m, h, o, p, q):
    def block(tile, at):
        slot = m[tile * 9 + at]
        found = h[0, 0, tile, jnp.maximum(slot, 0)]
        return jnp.where(slot >= 0, found, jnp.zeros_like(found))

    for tile in range(4):
        for at in range(9):
            o[tile, :, at * T : (at + 1) * T] = block(tile, at)
    even = m[PAR_Y] == 0
    side = 1 + m[PAR_X]
    down, up = block(0, side * 3), block(3, side * 3 + 2)
    p[...] = jnp.where(even, up, down)
    q[...] = jnp.where(even, down, up)


def blocks(o, tile, sides, dys):
    out = []
    for side in sides:
        at = (side * 3 + dys[0]) * T
        if not isinstance(side, int):
            at = pl.multiple_of(at, T)
        out.append(o[tile, :, pl.ds(at, len(dys) * T)])
    return out[0] if len(out) == 1 else jnp.concatenate(out, axis=1)


def store_edges(m, ref, p, q):
    even = m[PAR_Y] == 0
    p[:T] = ref[pl.ds(jnp.where(even, 3, 0), 1)].reshape(T, 2 * T)
    q[:T] = ref[pl.ds(jnp.where(even, 0, 3), 1)].reshape(T, 2 * T)


def store_bulk(ref, to_b, to_a):
    flat = ref[...].reshape(4 * T, 2 * T)
    to_b[...] = flat[HEAD:]
    to_a[: 4 * T] = flat
    to_a[4 * T :] = flat[:PAD]


def join_kernel(m, own, other, v, p, q, to_b, to_a):
    first_col = m[COL] == 0
    v[:, :, :T] = jnp.where(first_col, own[...], other[...])
    v[:, :, T:] = jnp.where(first_col, other[...], own[...])
    store_edges(m, v, p, q)
    store_bulk(v, to_b, to_a)


def ends_of(m, ends):
    even = m[PAR_Y] == 0
    p, q = ends[:T], ends[ends.shape[0] - T :]
    return jnp.where(even, q, p), jnp.where(even, p, q)


def product(o, tile, sides, at, sources):
    row = blocks(o, tile, sides, [place - tile for place in at])
    return dot(row, jnp.concatenate([x.reshape(len(at) * T, 2 * T) for x in sources], axis=0))


def core_kernel(m, o, x, ends, a, b, acc, ext):
    low, high = ends_of(m, ends)
    ext[0] = low
    ext[1:5] = x[...]
    ext[5] = high
    for tile in range(4):
        total = product(o, tile, (0,), range(tile, tile + 3), [ext[tile : tile + 3]])
        at = [place for place in range(tile, tile + 3) if 1 <= place <= 4]
        total += product(o, tile, (1,), at, [a[(at[0] - 1) * T : at[-1] * T]])
        at = [place for place in at if place > 1]
        acc[tile] = total + product(o, tile, (2,), at, [b[(at[0] - 1) * T - HEAD : at[-1] * T - HEAD]])


def rim_kernel(m, o, b, a_ends, b_ends, acc, *rest, last):
    if last:
        before, h_p, h_q, out, p, q = rest
    else:
        out, p, q, to_b, to_a = rest
    low, high = zip(ends_of(m, a_ends), ends_of(m, b_ends))
    first = jnp.concatenate([b_ends[T : T + HEAD], b[: T - HEAD]], axis=0)
    for tile in range(4):
        total = acc[tile]
        if tile == 0:
            total += product(o, tile, (2,), (0, 1), [jnp.concatenate([low[1], first], axis=0)])
            total += product(o, tile, (1,), (0,), [low[0]])
        if tile == 1:
            total += product(o, tile, (2,), (1,), [first])
        if tile == 3:
            total += product(o, tile, (1, 2), (5,), high)
        if last:
            out[tile] = (total - before[tile].astype(F32)).astype(BF)
        else:
            out[tile] = (0.5 * total).astype(BF)
    store_edges(m, out, p, q)
    if last:
        for to, block in ((p, h_p), (q, h_q)):
            to[T:, :T] = block[: T // 2]
            to[T:, T:] = block[T // 2 :]
    else:
        store_bulk(out, to_b, to_a)


def corr_kernel(m, o, s, corr, turned, acc):
    flat = s[...].reshape(4 * T, 2 * T)
    turned[...] = flat.T
    corr[...] = dot(turned[...], flat)
    for tile in range(4):
        total = 0.5 * dot(blocks(o, tile, (0,), (1,)), s[tile])
        if tile < 3:
            total += dot(blocks(o, tile, (0,), (2,)), s[tile + 1])
        acc[tile] = total


def places():
    shape = (2 * T, 2 * T)
    return lax.broadcasted_iota(jnp.int32, shape, 0), lax.broadcasted_iota(jnp.int32, shape, 1)


def gram_kernel(m, o, turned, p, q, right, acc, corr, mine, theirs):
    side = 1 + m[PAR_X]
    parts = []
    for tile in range(4):
        at = [place for place in range(tile, tile + 3) if 1 <= place <= 4]
        parts.append(acc[tile] + product(o, tile, (side,), at, [right[at[0] - 1 : at[-1]]]))
    even = m[PAR_Y] == 0
    above = jnp.where(even, p[:T], q[:T])
    parts[3] += product(o, 3, (0,), (5,), [above])
    high, low = split(jnp.concatenate(parts, axis=0))
    half = dot(turned[...], high) + dot(turned[...], low)
    for got, at in ((p, jnp.where(even, 3, 0)), (q, jnp.where(even, 0, 3))):
        block = jnp.concatenate([got[T:, :T], got[T:, T:]], axis=0)
        high, low = split(dot(block, right[at]))
        half += dot(got[:T], high, ((0,), (0,))) + dot(got[:T], low, ((0,), (0,)))
    coupling = half + half.T
    rows, cols = places()
    both = jnp.where(rows >= cols, corr[...], coupling)
    diagonal = jnp.sum(jnp.where(rows == cols, coupling, 0.0), axis=1, keepdims=True)
    first, second = pack(both[:T], diagonal[:T]), pack(both[T:], diagonal[T:])
    even = m[PAR_Y] == 0
    mine[:, 0, :] = jnp.where(even, first, second)
    theirs[:, 0, :] = jnp.where(even, second, first)


def pack(square, diagonal):
    lane = lax.broadcasted_iota(jnp.int32, (T // 2, T), 1)
    extra = jnp.where(lane == 0, diagonal[: T // 2], jnp.where(lane == 1, diagonal[T // 2 :], 0.0))
    return jnp.concatenate([square[: T // 2], square[T // 2 :], extra], axis=1)


def unpack(table):
    square = jnp.concatenate([table[:, : 2 * T], table[:, 2 * T : 4 * T]], axis=0)
    return square, jnp.concatenate([table[:, 4 * T : 4 * T + 1], table[:, 4 * T + 1 : 4 * T + 2]], axis=0)


def lower_part(e, rows, cols):
    return jnp.where(rows > cols, e, jnp.where(rows == cols, 0.5 * e, 0.0))


def squares(m, mine, theirs, spin):
    even = m[PAR_Y] == 0
    half = slice(spin * T // 2, (spin + 1) * T // 2)
    first, second = mine[half, 0, :], theirs[half, 0, :]
    top = unpack(jnp.where(even, first, second))
    bottom = unpack(jnp.where(even, second, first))
    both = jnp.concatenate([top[0], bottom[0]], axis=0)
    diagonal = jnp.concatenate([top[1], bottom[1]], axis=0)
    rows, cols = places()
    turned = both.T
    corr = jnp.where(rows >= cols, both, turned)
    return corr, jnp.where(rows < cols, both, jnp.where(rows == cols, diagonal, turned))


def stack_kernel(m, s, other, both):
    both[pl.ds(m[SPIN], 1)] = s[...][None]
    both[pl.ds(1 - m[SPIN], 1)] = other[...][None]


def final_kernel(m, mine, theirs, both, ritz, projected, x_ref, a_ref, k_ref):
    rows, cols = places()
    unit = (rows == cols).astype(F32)
    scales = []
    for spin in range(2):
        corr, k_ref[spin] = squares(m, mine, theirs, spin)
        on_diagonal = jnp.where(rows == cols, corr, 0.0)
        scale_row = 1.0 / jnp.sqrt(jnp.sum(on_diagonal, axis=0, keepdims=True))
        scale_col = 1.0 / jnp.sqrt(jnp.sum(on_diagonal, axis=1, keepdims=True))
        scaled = corr * scale_row * scale_col
        scales.append(scale_row)
        a_ref[spin] = scaled
        e = scaled - unit
        f = lower_part(e, rows, cols)
        f_half = f.astype(BF)
        fe = dot(f_half, e.astype(BF))
        e = dot((f + fe - e).astype(BF), f_half, ((1,), (1,))) - fe
        x = unit - f
        x_ref[spin] = x - dot(lower_part(e, rows, cols).astype(BF), x.astype(BF))

    def step(state):
        count, _, _ = state
        xs = [x_ref[spin] for spin in range(2)]
        es = [dot3(xs[spin], a_ref[spin]) for spin in range(2)]
        es = [dot3(es[spin], xs[spin], ((1,), (1,))) - unit for spin in range(2)]
        for spin in range(2):
            x_ref[spin] = xs[spin] - dot(lower_part(es[spin], rows, cols).astype(BF), xs[spin].astype(BF))
        return count + 1, jnp.sum(es[0] * es[0]), jnp.sum(es[1] * es[1])

    def more(state):
        count, *sizes = state
        largest = jnp.maximum(*sizes)
        return (count < 12) & (largest >= 4e-6) & (largest < 1e4)

    _, *sizes = lax.while_loop(more, step, (0, F32(1.0), F32(1.0)))

    for spin in range(2):

        @pl.when(jnp.logical_not(sizes[spin] < 4e-6))
        def _(spin=spin):
            x_ref[spin] = unit

            def eliminate(j, carry):
                row = a_ref[spin, pl.ds(j, 1), :]
                pivot = jnp.sum(jnp.where(cols[:1] == j, row, 0.0), axis=1, keepdims=True)
                a = a_ref[spin]
                column = jnp.sum(jnp.where(cols == j, a, 0.0), axis=1, keepdims=True)
                factor = jnp.where(rows[:, :1] > j, column / pivot, 0.0)
                x = x_ref[spin]
                x_row = x_ref[spin, pl.ds(j, 1), :]
                a_ref[spin] = a - factor * row
                x_ref[spin] = x - factor * x_row
                return carry

            lax.fori_loop(0, 2 * T, eliminate, 0)
            pivots = jnp.sum(jnp.where(rows == cols, a_ref[spin], 0.0), axis=1, keepdims=True)
            x_ref[spin] = x_ref[spin] / jnp.sqrt(pivots)

    first_col = m[COL] == 0
    for spin in range(2):
        x = x_ref[spin] * scales[spin]
        part = jnp.where(first_col, x[:T], x[T:])
        ritz[spin, 0] = dot(both[spin].reshape(4 * T, 2 * T), part.astype(BF), ((1,), (1,))).astype(BF).reshape(4, T, T)
        projected[spin] = dot3(dot3(x, k_ref[spin]), part, ((1,), (1,)))


def whole(shape):
    return pl.BlockSpec(shape, lambda i, m, n=len(shape): (0,) * n)


def call(kernel, m, arrays, outs, name, flops=0, specs=None, scratch=()):
    arrays = list(arrays)
    moved = sum(a.size * a.dtype.itemsize for a in [*arrays, *outs])
    return pl.pallas_call(
        kernel,
        out_shape=outs,
        grid_spec=pltpu.PrefetchScalarGridSpec(
            num_scalar_prefetch=1,
            grid=(1,),
            in_specs=specs or [whole(a.shape) for a in arrays],
            out_specs=[whole(o.shape) for o in outs],
            scratch_shapes=list(scratch),
        ),
        compiler_params=pltpu.CompilerParams(vmem_limit_bytes=32 * 1024 * 1024),
        cost_estimate=pl.CostEstimate(flops=2 * T * T * 2 * T * flops, bytes_accessed=moved, transcendentals=0),
        name=name,
    )(m, *arrays)


def table(neighbour_index, block_count):
    gx, gy, col = (lax.axis_index(a) for a in AXES)
    spin = col ^ ((gx >> 1) & 1)
    toward = jnp.where(gx % 2 == 0, 1, -1)
    dx = jnp.stack([jnp.zeros_like(toward), toward, -toward])
    codes = (dx[:, None] + 1) * 3 + jnp.arange(3, dtype=jnp.int32)[None, :]
    slots = jnp.arange(NB, dtype=jnp.int32)
    index, count = neighbour_index[0], block_count[0]
    match = (index[:, None, None, :] == codes[None, :, :, None]) & (
        slots < count[:, None, None, None]
    )
    found = jnp.sum(jnp.where(match, slots + 1, 0), axis=-1) - 1
    scalars = jnp.stack([spin, col, gy % 2, gx % 2])
    return spin, col, jnp.concatenate([found.reshape(-1), scalars]).astype(jnp.int32)


def shaped(shape, dtype):
    return jax.ShapeDtypeStruct(shape, dtype)


def per_device(start_block, hamiltonian, neighbour_index, block_count):
    sizes = tuple(lax.axis_size(a) for a in AXES)
    members = sizes[0] * sizes[1]
    block, full = (4, T, 2 * T), (2 * T, 2 * T)
    spin, col, m = table(neighbour_index, block_count)

    other = swap_col(sizes, lax.dynamic_index_in_dim(start_block, 1 - spin, 0, keepdims=False)[0])
    own = lax.dynamic_index_in_dim(start_block, spin, 0, keepdims=False)[0]
    spin_block = pl.BlockSpec((1,) + hamiltonian.shape[1:], lambda i, m: (m[SPIN], 0, 0, 0, 0, 0))
    corner = shaped((T, T), BF)
    o, h_p, h_q = call(
        order_kernel, m, [hamiltonian], [shaped((4, T, NB * T), BF), corner, corner], "order", specs=[spin_block]
    )
    tile = shaped((T, 2 * T), BF)
    ext = pltpu.VMEM((6, T, 2 * T), BF)
    other, o = lax.optimization_barrier((other, o))
    bulk = [shaped((4 * T - HEAD, 2 * T), BF), shaped((4 * T + PAD, 2 * T), BF)]
    outs = [shaped(block, BF), tile, tile, *bulk]
    v, p, q, *rest = call(join_kernel, m, [own, other], outs, "join")

    def apply_ham(x, p, q, rest, more, outs):
        p, q = swap(sizes, p, 0, 1), swap(sizes, q, 0, 2)
        ends = jnp.concatenate([p, q], axis=0)
        a, b = swap(sizes, rest[1], 1, 0), swap(sizes, rest[0], 2, 0)
        a_ends = swap(sizes, ends, 1, 0)
        b_ends = swap(sizes, jnp.concatenate([p, x[0, :HEAD], q], axis=0), 2, 0)
        (acc,) = call(core_kernel, m, [o, x, ends, a, b], [shaped(block, F32)], "core", 31, scratch=[ext])
        kernel = functools.partial(rim_kernel, last=len(more) > 0)
        return call(kernel, m, [o, b, a_ends, b_ends, acc, *more], outs, "rim", 6)

    first, p, q, *rest = apply_ham(v, p, q, rest, [], outs)
    longer = shaped((3 * T // 2, 2 * T), BF)
    second, p, q = apply_ham(first, p, q, rest, [v, h_p, h_q], [shaped(block, BF), longer, longer])

    right = shift(sizes, second, -1, 0)
    p, q = swap(sizes, p, 0, 1), swap(sizes, q, 0, 2)
    corr, turned, acc = call(
        corr_kernel, m, [o, second], [shaped(full, F32), shaped((2 * T, 4 * T), BF), shaped(block, F32)], "corr", 15
    )
    piece = shaped((members // 2, 1, 5 * T), F32)
    mine, theirs = call(
        gram_kernel, m, [o, turned, p, q, right, acc, corr], [piece, piece], "gram", 30
    )

    rows = members * second.shape[0] * second.shape[1]
    partial = mine + swap(sizes, theirs, 0, 1)
    (both,) = call(stack_kernel, m, [second, swap_col(sizes, second)], [shaped((2, *block), BF)], "stack", 200)
    total = exchange(sizes, partial, False)
    total, both = lax.optimization_barrier((total, both))
    total = total.sum(axis=0, keepdims=True) / rows
    mine = exchange(sizes, jnp.broadcast_to(total, (members, 1, 5 * T)), True)
    theirs = swap(sizes, mine, 0, 1)
    squared = pltpu.VMEM((2, *full), F32)
    return tuple(
        call(
            final_kernel, m, [mine, theirs, both],
            [shaped((2, 1, 4, T, T), BF), shaped((2, 2 * T, T), F32)], "final", 200,
            scratch=[squared, squared, squared],
        )
    )


def solution(mesh):
    return jax.shard_map(
        per_device,
        mesh=mesh,
        in_specs=(
            P(None, "gx", "gy", None, "col"),
            P(None, "gx", "gy", None, None, None),
            P("gx", "gy", None),
            P("gx", "gy"),
        ),
        out_specs=(P(None, "gx", "gy", None, "col"), P(None, None, "col")),
        check_vma=False,
    )
```

```python
import functools

import jax
import jax.numpy as jnp
from jax import lax
from jax.experimental import pallas as pl
from jax.experimental.pallas import tpu as pltpu
from jax.sharding import PartitionSpec as P

NB = 9
T = 128
AXES = ("gx", "gy", "col")
BF = jnp.bfloat16
F32 = jnp.float32
SPIN, COL, PAR_Y, PAR_X = 36, 37, 38, 39


def col_of(gx, spin):
    return spin ^ ((gx >> 1) & 1)


def device(sizes, gx, gy, col):
    return ((gx % sizes[0]) * sizes[1] + gy % sizes[1]) * sizes[2] + col


def pairs(sizes, target):
    out = []
    for gx in range(sizes[0]):
        for gy in range(sizes[1]):
            for spin in range(2):
                there = target(gx, gy)
                there_gx = there[0] % sizes[0]
                out.append(
                    (
                        device(sizes, gx, gy, col_of(gx, spin)),
                        device(sizes, there_gx, there[1], col_of(there_gx, spin)),
                    )
                )
    return out


def partner(index, kind):
    if kind == 0:
        return index
    return index + 1 if (index % 2 == 0) == (kind == 1) else index - 1


def swap(sizes, block, kind_x, kind_y):
    perm = pairs(sizes, lambda gx, gy: (partner(gx, kind_x), partner(gy, kind_y)))
    return lax.ppermute(block, AXES, perm)


def shift(sizes, block, dx, dy):
    return lax.ppermute(block, AXES, pairs(sizes, lambda gx, gy: (gx + dx, gy + dy)))


def swap_col(sizes, block):
    perm = [(d, d ^ 1) for d in range(sizes[0] * sizes[1] * 2)]
    return lax.ppermute(block, AXES, perm)


def exchange(sizes, pieces, joint):
    groups = [
        [
            device(sizes, gx, gy, col_of(gx, spin))
            for gx in range(sizes[0])
            for gy in range(core, sizes[1], 2)
        ]
        for core in range(2)
        for spin in range(2)
    ]
    if joint:
        groups = [groups[0] + groups[1], groups[2] + groups[3]]
    return lax.all_to_all(pieces, AXES, 0, 0, axis_index_groups=groups, tiled=True)


def dot(a, b, dims=((1,), (0,))):
    return lax.dot_general(a, b, (dims, ((), ())), preferred_element_type=F32)


def split(a):
    high = a.astype(BF)
    return high, (a - high.astype(F32)).astype(BF)


def dot3(a, b, dims=((1,), (0,))):
    (ah, al), (bh, bl) = split(a), split(b)
    return dot(ah, bh, dims) + (dot(ah, bl, dims) + dot(al, bh, dims))


def order_kernel(m, h, o, p, q):
    def block(tile, at):
        slot = m[tile * 9 + at]
        found = h[0, 0, tile, jnp.maximum(slot, 0)]
        return jnp.where(slot >= 0, found, jnp.zeros_like(found))

    for tile in range(4):
        for at in range(9):
            o[tile, :, at * T : (at + 1) * T] = block(tile, at)
    even = m[PAR_Y] == 0
    side = 1 + m[PAR_X]
    down, up = block(0, side * 3), block(3, side * 3 + 2)
    p[...] = jnp.where(even, up, down)
    q[...] = jnp.where(even, down, up)


def blocks(o, tile, sides, dys):
    out = []
    for side in sides:
        at = (side * 3 + dys[0]) * T
        if not isinstance(side, int):
            at = pl.multiple_of(at, T)
        out.append(o[tile, :, pl.ds(at, len(dys) * T)])
    return out[0] if len(out) == 1 else jnp.concatenate(out, axis=1)


def store_edges(m, ref, p, q):
    even = m[PAR_Y] == 0
    p[:T] = ref[pl.ds(jnp.where(even, 3, 0), 1)].reshape(T, 2 * T)
    q[:T] = ref[pl.ds(jnp.where(even, 0, 3), 1)].reshape(T, 2 * T)


def join_kernel(m, own, other, v, p, q):
    first_col = m[COL] == 0
    v[:, :, :T] = jnp.where(first_col, own[...], other[...])
    v[:, :, T:] = jnp.where(first_col, other[...], own[...])
    store_edges(m, v, p, q)


def edge_kernel(m, a, b, out):
    at = pl.ds(jnp.where(m[PAR_Y] == 0, 3, 0), 1)
    out[0:1] = a[at]
    out[1:2] = b[at]


def low_high(m, p, q):
    even = m[PAR_Y] == 0
    return jnp.where(even, q, p), jnp.where(even, p, q)


def product(o, tile, sides, at, sources):
    row = blocks(o, tile, sides, [place - tile for place in at])
    return dot(row, jnp.concatenate([x.reshape(len(at) * T, 2 * T) for x in sources], axis=0))


def outer_product(m, o, at_p, tiles):
    high = m[PAR_Y] == 0 if at_p else m[PAR_Y] != 0
    top = blocks(o, 3, (1, 2), (2,))
    bottom = blocks(o, 0, (1, 2), (0,))
    return dot(jnp.where(high, top, bottom), jnp.concatenate(tiles, axis=0)), high


def core_kernel(m, o, x, p, q, a, b, a_corner, b_corner, acc, ext):
    ext[0], ext[5] = low_high(m, p[...], q[...])
    ext[1:5] = x[...]
    for tile in range(4):
        total = product(o, tile, (0,), range(tile, tile + 3), [ext[tile : tile + 3]])
        at = [place for place in range(tile, tile + 3) if 1 <= place <= 4]
        acc[tile] = total + product(o, tile, (1, 2), at, [y[at[0] - 1 : at[-1]] for y in (a, b)])
    part, high = outer_product(m, o, False, [a_corner[...], b_corner[...]])
    acc[pl.ds(jnp.where(high, 3, 0), 1)] += part[None]


def rim_kernel(m, o, edge, acc, *rest, last):
    if last:
        before, h_p, h_q, out, p, q = rest
    else:
        out, p, q = rest
    part, high = outer_product(m, o, True, [edge[0], edge[1]])
    nothing = jnp.zeros_like(part)
    for tile in range(4):
        total = acc[tile]
        if tile == 0:
            total += jnp.where(high, nothing, part)
        if tile == 3:
            total += jnp.where(high, part, nothing)
        if last:
            out[tile] = (total - before[tile].astype(F32)).astype(BF)
        else:
            out[tile] = (0.5 * total).astype(BF)
    store_edges(m, out, p, q)
    if last:
        for to, block in ((p, h_p), (q, h_q)):
            to[T:, :T] = block[: T // 2]
            to[T:, T:] = block[T // 2 :]


def corr_kernel(m, o, s, corr, turned, acc):
    flat = s[...].reshape(4 * T, 2 * T)
    turned[...] = flat.T
    corr[...] = dot(turned[...], flat)
    for tile in range(4):
        total = 0.5 * dot(blocks(o, tile, (0,), (1,)), s[tile])
        if tile < 3:
            total += dot(blocks(o, tile, (0,), (2,)), s[tile + 1])
        acc[tile] = total


def places():
    shape = (2 * T, 2 * T)
    return lax.broadcasted_iota(jnp.int32, shape, 0), lax.broadcasted_iota(jnp.int32, shape, 1)


def gram_kernel(m, o, turned, p, q, right, acc, corr, mine, theirs):
    side = 1 + m[PAR_X]
    parts = []
    for tile in range(4):
        at = [place for place in range(tile, tile + 3) if 1 <= place <= 4]
        parts.append(acc[tile] + product(o, tile, (side,), at, [right[at[0] - 1 : at[-1]]]))
    even = m[PAR_Y] == 0
    above = jnp.where(even, p[:T], q[:T])
    parts[3] += product(o, 3, (0,), (5,), [above])
    high, low = split(jnp.concatenate(parts, axis=0))
    half = dot(turned[...], high) + dot(turned[...], low)
    for got, at in ((p, jnp.where(even, 3, 0)), (q, jnp.where(even, 0, 3))):
        block = jnp.concatenate([got[T:, :T], got[T:, T:]], axis=0)
        high, low = split(dot(block, right[at]))
        half += dot(got[:T], high, ((0,), (0,))) + dot(got[:T], low, ((0,), (0,)))
    coupling = half + half.T
    rows, cols = places()
    both = jnp.where(rows >= cols, corr[...], coupling)
    diagonal = jnp.sum(jnp.where(rows == cols, coupling, 0.0), axis=1, keepdims=True)
    first, second = pack(both[:T], diagonal[:T]), pack(both[T:], diagonal[T:])
    even = m[PAR_Y] == 0
    mine[:, 0, :] = jnp.where(even, first, second)
    theirs[:, 0, :] = jnp.where(even, second, first)


def pack(square, diagonal):
    lane = lax.broadcasted_iota(jnp.int32, (T // 2, T), 1)
    extra = jnp.where(lane == 0, diagonal[: T // 2], jnp.where(lane == 1, diagonal[T // 2 :], 0.0))
    return jnp.concatenate([square[: T // 2], square[T // 2 :], extra], axis=1)


def unpack(table):
    square = jnp.concatenate([table[:, : 2 * T], table[:, 2 * T : 4 * T]], axis=0)
    return square, jnp.concatenate([table[:, 4 * T : 4 * T + 1], table[:, 4 * T + 1 : 4 * T + 2]], axis=0)


def lower_part(e, rows, cols):
    return jnp.where(rows > cols, e, jnp.where(rows == cols, 0.5 * e, 0.0))


def squares(m, mine, theirs, spin):
    even = m[PAR_Y] == 0
    half = slice(spin * T // 2, (spin + 1) * T // 2)
    first, second = mine[half, 0, :], theirs[half, 0, :]
    top = unpack(jnp.where(even, first, second))
    bottom = unpack(jnp.where(even, second, first))
    both = jnp.concatenate([top[0], bottom[0]], axis=0)
    diagonal = jnp.concatenate([top[1], bottom[1]], axis=0)
    rows, cols = places()
    turned = both.T
    corr = jnp.where(rows >= cols, both, turned)
    return corr, jnp.where(rows < cols, both, jnp.where(rows == cols, diagonal, turned))


def stack_kernel(m, s, other, both):
    both[pl.ds(m[SPIN], 1)] = s[...][None]
    both[pl.ds(1 - m[SPIN], 1)] = other[...][None]


def final_kernel(m, mine, theirs, both, ritz, projected, x_ref, a_ref, k_ref):
    rows, cols = places()
    unit = (rows == cols).astype(F32)
    scales = []
    for spin in range(2):
        corr, k_ref[spin] = squares(m, mine, theirs, spin)
        on_diagonal = jnp.where(rows == cols, corr, 0.0)
        scale_row = 1.0 / jnp.sqrt(jnp.sum(on_diagonal, axis=0, keepdims=True))
        scale_col = 1.0 / jnp.sqrt(jnp.sum(on_diagonal, axis=1, keepdims=True))
        scaled = corr * scale_row * scale_col
        scales.append(scale_row)
        a_ref[spin] = scaled
        e = scaled - unit
        f = lower_part(e, rows, cols)
        f_half = f.astype(BF)
        fe = dot(f_half, e.astype(BF))
        e = dot((f + fe - e).astype(BF), f_half, ((1,), (1,))) - fe
        x = unit - f
        x_ref[spin] = x - dot(lower_part(e, rows, cols).astype(BF), x.astype(BF))

    def step(state):
        count, _, _ = state
        xs = [x_ref[spin] for spin in range(2)]
        es = [dot3(xs[spin], a_ref[spin]) for spin in range(2)]
        es = [dot3(es[spin], xs[spin], ((1,), (1,))) - unit for spin in range(2)]
        for spin in range(2):
            x_ref[spin] = xs[spin] - dot(lower_part(es[spin], rows, cols).astype(BF), xs[spin].astype(BF))
        return count + 1, jnp.sum(es[0] * es[0]), jnp.sum(es[1] * es[1])

    def more(state):
        count, *sizes = state
        largest = jnp.maximum(*sizes)
        return (count < 12) & (largest >= 4e-6) & (largest < 1e4)

    _, *sizes = lax.while_loop(more, step, (0, F32(1.0), F32(1.0)))

    for spin in range(2):

        @pl.when(jnp.logical_not(sizes[spin] < 4e-6))
        def _(spin=spin):
            x_ref[spin] = unit

            def eliminate(j, carry):
                row = a_ref[spin, pl.ds(j, 1), :]
                pivot = jnp.sum(jnp.where(cols[:1] == j, row, 0.0), axis=1, keepdims=True)
                a = a_ref[spin]
                column = jnp.sum(jnp.where(cols == j, a, 0.0), axis=1, keepdims=True)
                factor = jnp.where(rows[:, :1] > j, column / pivot, 0.0)
                x = x_ref[spin]
                x_row = x_ref[spin, pl.ds(j, 1), :]
                a_ref[spin] = a - factor * row
                x_ref[spin] = x - factor * x_row
                return carry

            lax.fori_loop(0, 2 * T, eliminate, 0)
            pivots = jnp.sum(jnp.where(rows == cols, a_ref[spin], 0.0), axis=1, keepdims=True)
            x_ref[spin] = x_ref[spin] / jnp.sqrt(pivots)

    first_col = m[COL] == 0
    for spin in range(2):
        x = x_ref[spin] * scales[spin]
        part = jnp.where(first_col, x[:T], x[T:])
        ritz[spin, 0] = dot(both[spin].reshape(4 * T, 2 * T), part.astype(BF), ((1,), (1,))).astype(BF).reshape(4, T, T)
        projected[spin] = dot3(dot3(x, k_ref[spin]), part, ((1,), (1,)))


def whole(shape):
    return pl.BlockSpec(shape, lambda i, m, n=len(shape): (0,) * n)


def call(kernel, m, arrays, outs, name, flops=0, specs=None, scratch=()):
    arrays = list(arrays)
    moved = sum(a.size * a.dtype.itemsize for a in [*arrays, *outs])
    return pl.pallas_call(
        kernel,
        out_shape=outs,
        grid_spec=pltpu.PrefetchScalarGridSpec(
            num_scalar_prefetch=1,
            grid=(1,),
            in_specs=specs or [whole(a.shape) for a in arrays],
            out_specs=[whole(o.shape) for o in outs],
            scratch_shapes=list(scratch),
        ),
        compiler_params=pltpu.CompilerParams(vmem_limit_bytes=32 * 1024 * 1024),
        cost_estimate=pl.CostEstimate(flops=2 * T * T * 2 * T * flops, bytes_accessed=moved, transcendentals=0),
        name=name,
    )(m, *arrays)


def table(neighbour_index, block_count):
    gx, gy, col = (lax.axis_index(a) for a in AXES)
    spin = col ^ ((gx >> 1) & 1)
    toward = jnp.where(gx % 2 == 0, 1, -1)
    dx = jnp.stack([jnp.zeros_like(toward), toward, -toward])
    codes = (dx[:, None] + 1) * 3 + jnp.arange(3, dtype=jnp.int32)[None, :]
    slots = jnp.arange(NB, dtype=jnp.int32)
    index, count = neighbour_index[0], block_count[0]
    match = (index[:, None, None, :] == codes[None, :, :, None]) & (
        slots < count[:, None, None, None]
    )
    found = jnp.sum(jnp.where(match, slots + 1, 0), axis=-1) - 1
    scalars = jnp.stack([spin, col, gy % 2, gx % 2])
    return spin, col, jnp.concatenate([found.reshape(-1), scalars]).astype(jnp.int32)


def shaped(shape, dtype):
    return jax.ShapeDtypeStruct(shape, dtype)


def per_device(start_block, hamiltonian, neighbour_index, block_count):
    sizes = tuple(lax.axis_size(a) for a in AXES)
    members = sizes[0] * sizes[1]
    block, full = (4, T, 2 * T), (2 * T, 2 * T)
    spin, col, m = table(neighbour_index, block_count)

    other = swap_col(sizes, lax.dynamic_index_in_dim(start_block, 1 - spin, 0, keepdims=False)[0])
    own = lax.dynamic_index_in_dim(start_block, spin, 0, keepdims=False)[0]
    spin_block = pl.BlockSpec((1,) + hamiltonian.shape[1:], lambda i, m: (m[SPIN], 0, 0, 0, 0, 0))
    corner = shaped((T, T), BF)
    o, h_p, h_q = call(
        order_kernel, m, [hamiltonian], [shaped((4, T, NB * T), BF), corner, corner], "order", specs=[spin_block]
    )
    tile = shaped((T, 2 * T), BF)
    ext = pltpu.VMEM((6, T, 2 * T), BF)
    other, o = lax.optimization_barrier((other, o))
    outs = [shaped(block, BF), tile, tile]
    v, p, q = call(join_kernel, m, [own, other], outs, "join")

    def apply_ham(x, p, q, more, outs):
        p, q = swap(sizes, p, 0, 1), swap(sizes, q, 0, 2)
        a, b = swap(sizes, x, 1, 0), swap(sizes, x, 2, 0)
        a_corner, b_corner = swap(sizes, q, 1, 0), swap(sizes, q, 2, 0)
        (edge,) = call(edge_kernel, m, [a, b], [shaped((2, T, 2 * T), BF)], "edge")
        edge = swap(sizes, edge, 0, 1)
        (acc,) = call(
            core_kernel, m, [o, x, p, q, a, b, a_corner, b_corner], [shaped(block, F32)], "core", 150, scratch=[ext]
        )
        kernel = functools.partial(rim_kernel, last=len(more) > 0)
        return call(kernel, m, [o, edge, acc, *more], outs, "rim", 2)

    first, p, q = apply_ham(v, p, q, [], outs)
    longer = shaped((3 * T // 2, 2 * T), BF)
    second, p, q = apply_ham(first, p, q, [v, h_p, h_q], [shaped(block, BF), longer, longer])

    right = shift(sizes, second, -1, 0)
    p, q = swap(sizes, p, 0, 1), swap(sizes, q, 0, 2)
    corr, turned, acc = call(
        corr_kernel, m, [o, second], [shaped(full, F32), shaped((2 * T, 4 * T), BF), shaped(block, F32)], "corr", 15
    )
    piece = shaped((members // 2, 1, 5 * T), F32)
    mine, theirs = call(
        gram_kernel, m, [o, turned, p, q, right, acc, corr], [piece, piece], "gram", 30
    )

    rows = members * second.shape[0] * second.shape[1]
    partial = mine + swap(sizes, theirs, 0, 1)
    (both,) = call(stack_kernel, m, [second, swap_col(sizes, second)], [shaped((2, *block), BF)], "stack", 200)
    total = exchange(sizes, partial, False)
    total, both = lax.optimization_barrier((total, both))
    total = total.sum(axis=0, keepdims=True) / rows
    mine = exchange(sizes, jnp.broadcast_to(total, (members, 1, 5 * T)), True)
    theirs = swap(sizes, mine, 0, 1)
    squared = pltpu.VMEM((2, *full), F32)
    return tuple(
        call(
            final_kernel, m, [mine, theirs, both],
            [shaped((2, 1, 4, T, T), BF), shaped((2, 2 * T, T), F32)], "final", 200,
            scratch=[squared, squared, squared],
        )
    )


def solution(mesh):
    return jax.shard_map(
        per_device,
        mesh=mesh,
        in_specs=(
            P(None, "gx", "gy", None, "col"),
            P(None, "gx", "gy", None, None, None),
            P("gx", "gy", None),
            P("gx", "gy"),
        ),
        out_specs=(P(None, "gx", "gy", None, "col"), P(None, None, "col")),
        check_vma=False,
    )
```

```python
import functools

import jax
import jax.numpy as jnp
from jax import lax
from jax.experimental import pallas as pl
from jax.experimental.pallas import tpu as pltpu
from jax.sharding import PartitionSpec as P

NB = 9
T = 128
AXES = ("gx", "gy", "col")
BF = jnp.bfloat16
F32 = jnp.float32
SPIN, COL, PAR_Y, PAR_X = 36, 37, 38, 39


def col_of(gx, spin):
    return spin ^ ((gx >> 1) & 1)


def device(sizes, gx, gy, col):
    return ((gx % sizes[0]) * sizes[1] + gy % sizes[1]) * sizes[2] + col


def pairs(sizes, target):
    out = []
    for gx in range(sizes[0]):
        for gy in range(sizes[1]):
            for spin in range(2):
                there = target(gx, gy)
                there_gx = there[0] % sizes[0]
                out.append(
                    (
                        device(sizes, gx, gy, col_of(gx, spin)),
                        device(sizes, there_gx, there[1], col_of(there_gx, spin)),
                    )
                )
    return out


def partner(index, kind):
    if kind == 0:
        return index
    return index + 1 if (index % 2 == 0) == (kind == 1) else index - 1


def swap(sizes, block, kind_x, kind_y):
    perm = pairs(sizes, lambda gx, gy: (partner(gx, kind_x), partner(gy, kind_y)))
    return lax.ppermute(block, AXES, perm)


def shift(sizes, block, dx, dy):
    return lax.ppermute(block, AXES, pairs(sizes, lambda gx, gy: (gx + dx, gy + dy)))


def swap_col(sizes, block):
    perm = [(d, d ^ 1) for d in range(sizes[0] * sizes[1] * 2)]
    return lax.ppermute(block, AXES, perm)


def exchange(sizes, pieces, joint):
    groups = [
        [
            device(sizes, gx, gy, col_of(gx, spin))
            for gx in range(sizes[0])
            for gy in range(core, sizes[1], 2)
        ]
        for core in range(2)
        for spin in range(2)
    ]
    if joint:
        groups = [groups[0] + groups[1], groups[2] + groups[3]]
    return lax.all_to_all(pieces, AXES, 0, 0, axis_index_groups=groups, tiled=True)


def dot(a, b, dims=((1,), (0,))):
    return lax.dot_general(a, b, (dims, ((), ())), preferred_element_type=F32)


def split(a):
    high = a.astype(BF)
    return high, (a - high.astype(F32)).astype(BF)


def dot3(a, b, dims=((1,), (0,))):
    (ah, al), (bh, bl) = split(a), split(b)
    return dot(ah, bh, dims) + (dot(ah, bl, dims) + dot(al, bh, dims))


def order_kernel(m, h, o, p, q):
    def block(tile, at):
        slot = m[tile * 9 + at]
        found = h[0, 0, tile, jnp.maximum(slot, 0)]
        return jnp.where(slot >= 0, found, jnp.zeros_like(found))

    for tile in range(4):
        for at in range(9):
            o[tile, :, at * T : (at + 1) * T] = block(tile, at)
    even = m[PAR_Y] == 0
    side = 1 + m[PAR_X]
    down, up = block(0, side * 3), block(3, side * 3 + 2)
    p[...] = jnp.where(even, up, down)
    q[...] = jnp.where(even, down, up)


def blocks(o, tile, sides, dys):
    out = []
    for side in sides:
        at = (side * 3 + dys[0]) * T
        if not isinstance(side, int):
            at = pl.multiple_of(at, T)
        out.append(o[tile, :, pl.ds(at, len(dys) * T)])
    return out[0] if len(out) == 1 else jnp.concatenate(out, axis=1)


def store_edges(m, ref, p, q):
    even = m[PAR_Y] == 0
    p[:T] = ref[pl.ds(jnp.where(even, 3, 0), 1)].reshape(T, 2 * T)
    q[:T] = ref[pl.ds(jnp.where(even, 0, 3), 1)].reshape(T, 2 * T)


def join_kernel(m, own, other, v, p, q):
    first_col = m[COL] == 0
    v[:, :, :T] = jnp.where(first_col, own[...], other[...])
    v[:, :, T:] = jnp.where(first_col, other[...], own[...])
    store_edges(m, v, p, q)


def edge_kernel(m, a, b, out):
    at = pl.ds(jnp.where(m[PAR_Y] == 0, 3, 0), 1)
    out[0:1] = a[at]
    out[1:2] = b[at]


def low_high(m, p, q):
    even = m[PAR_Y] == 0
    return jnp.where(even, q, p), jnp.where(even, p, q)


def product(o, tile, sides, at, sources):
    row = blocks(o, tile, sides, [place - tile for place in at])
    return dot(row, jnp.concatenate([x.reshape(len(at) * T, 2 * T) for x in sources], axis=0))


def outer_product(m, o, at_p, tiles):
    high = m[PAR_Y] == 0 if at_p else m[PAR_Y] != 0
    top = blocks(o, 3, (1, 2), (2,))
    bottom = blocks(o, 0, (1, 2), (0,))
    return dot(jnp.where(high, top, bottom), jnp.concatenate(tiles, axis=0)), high


def core_kernel(m, o, x, p, q, a, b, a_corner, b_corner, acc, ext):
    ext[0], ext[5] = low_high(m, p[...], q[...])
    ext[1:5] = x[...]
    for tile in range(4):
        total = product(o, tile, (0,), range(tile, tile + 3), [ext[tile : tile + 3]])
        at = [place for place in range(tile, tile + 3) if 1 <= place <= 4]
        acc[tile] = total + product(o, tile, (1, 2), at, [y[at[0] - 1 : at[-1]] for y in (a, b)])
    part, high = outer_product(m, o, False, [a_corner[...], b_corner[...]])
    acc[pl.ds(jnp.where(high, 3, 0), 1)] += part[None]


def rim_kernel(m, o, edge, acc, *rest, last):
    if last:
        before, h_p, h_q, out, p, q = rest
    else:
        out, p, q = rest
    part, high = outer_product(m, o, True, [edge[0], edge[1]])
    nothing = jnp.zeros_like(part)
    for tile in range(4):
        total = acc[tile]
        if tile == 0:
            total += jnp.where(high, nothing, part)
        if tile == 3:
            total += jnp.where(high, part, nothing)
        if last:
            out[tile] = (total - before[tile].astype(F32)).astype(BF)
        else:
            out[tile] = (0.5 * total).astype(BF)
    store_edges(m, out, p, q)
    if last:
        for to, block in ((p, h_p), (q, h_q)):
            to[T:, :T] = block[: T // 2]
            to[T:, T:] = block[T // 2 :]


def corr_kernel(m, o, s, corr, turned, acc):
    flat = s[...].reshape(4 * T, 2 * T)
    turned[...] = flat.T
    corr[...] = dot(turned[...], flat)
    for tile in range(4):
        total = 0.5 * dot(blocks(o, tile, (0,), (1,)), s[tile])
        if tile < 3:
            total += dot(blocks(o, tile, (0,), (2,)), s[tile + 1])
        acc[tile] = total


def places():
    shape = (2 * T, 2 * T)
    return lax.broadcasted_iota(jnp.int32, shape, 0), lax.broadcasted_iota(jnp.int32, shape, 1)


def gram_kernel(m, o, turned, p, q, right, acc, corr, mine, theirs):
    side = 1 + m[PAR_X]
    parts = []
    for tile in range(4):
        at = [place for place in range(tile, tile + 3) if 1 <= place <= 4]
        parts.append(acc[tile] + product(o, tile, (side,), at, [right[at[0] - 1 : at[-1]]]))
    even = m[PAR_Y] == 0
    above = jnp.where(even, p[:T], q[:T])
    parts[3] += product(o, 3, (0,), (5,), [above])
    high, low = split(jnp.concatenate(parts, axis=0))
    half = dot(turned[...], high) + dot(turned[...], low)
    for got, at in ((p, jnp.where(even, 3, 0)), (q, jnp.where(even, 0, 3))):
        block = jnp.concatenate([got[T:, :T], got[T:, T:]], axis=0)
        high, low = split(dot(block, right[at]))
        half += dot(got[:T], high, ((0,), (0,))) + dot(got[:T], low, ((0,), (0,)))
    coupling = half + half.T
    rows, cols = places()
    both = jnp.where(rows >= cols, corr[...], coupling)
    diagonal = jnp.sum(jnp.where(rows == cols, coupling, 0.0), axis=1, keepdims=True)
    first, second = pack(both[:T], diagonal[:T]), pack(both[T:], diagonal[T:])
    even = m[PAR_Y] == 0
    mine[:, 0, :] = jnp.where(even, first, second)
    theirs[:, 0, :] = jnp.where(even, second, first)


def pack(square, diagonal):
    lane = lax.broadcasted_iota(jnp.int32, (T // 2, T), 1)
    extra = jnp.where(lane == 0, diagonal[: T // 2], jnp.where(lane == 1, diagonal[T // 2 :], 0.0))
    return jnp.concatenate([square[: T // 2], square[T // 2 :], extra], axis=1)


def unpack(table):
    square = jnp.concatenate([table[:, : 2 * T], table[:, 2 * T : 4 * T]], axis=0)
    return square, jnp.concatenate([table[:, 4 * T : 4 * T + 1], table[:, 4 * T + 1 : 4 * T + 2]], axis=0)


def lower_part(e, rows, cols):
    return jnp.where(rows > cols, e, jnp.where(rows == cols, 0.5 * e, 0.0))


def squares(m, mine, theirs, spin):
    even = m[PAR_Y] == 0
    half = slice(spin * T // 2, (spin + 1) * T // 2)
    first, second = mine[half, 0, :], theirs[half, 0, :]
    top = unpack(jnp.where(even, first, second))
    bottom = unpack(jnp.where(even, second, first))
    both = jnp.concatenate([top[0], bottom[0]], axis=0)
    diagonal = jnp.concatenate([top[1], bottom[1]], axis=0)
    rows, cols = places()
    turned = both.T
    corr = jnp.where(rows >= cols, both, turned)
    return corr, jnp.where(rows < cols, both, jnp.where(rows == cols, diagonal, turned))


def stack_kernel(m, s, other, both):
    both[pl.ds(m[SPIN], 1)] = s[...][None]
    both[pl.ds(1 - m[SPIN], 1)] = other[...][None]


def final_kernel(m, mine, theirs, both, ritz, projected, x_ref, a_ref, k_ref):
    rows, cols = places()
    unit = (rows == cols).astype(F32)
    scales = []
    for spin in range(2):
        corr, k_ref[spin] = squares(m, mine, theirs, spin)
        on_diagonal = jnp.where(rows == cols, corr, 0.0)
        scale_row = 1.0 / jnp.sqrt(jnp.sum(on_diagonal, axis=0, keepdims=True))
        scale_col = 1.0 / jnp.sqrt(jnp.sum(on_diagonal, axis=1, keepdims=True))
        scaled = corr * scale_row * scale_col
        scales.append(scale_row)
        a_ref[spin] = scaled
        e = scaled - unit
        f = lower_part(e, rows, cols)
        f_half = f.astype(BF)
        fe = dot(f_half, e.astype(BF))
        e = dot((f + fe - e).astype(BF), f_half, ((1,), (1,))) - fe
        x = unit - f
        x_ref[spin] = x - dot(lower_part(e, rows, cols).astype(BF), x.astype(BF))

    def step(state):
        count, _, _ = state
        xs = [x_ref[spin] for spin in range(2)]
        es = [dot3(xs[spin], a_ref[spin]) for spin in range(2)]
        es = [dot3(es[spin], xs[spin], ((1,), (1,))) - unit for spin in range(2)]
        for spin in range(2):
            x_ref[spin] = xs[spin] - dot(lower_part(es[spin], rows, cols).astype(BF), xs[spin].astype(BF))
        return count + 1, jnp.sum(es[0] * es[0]), jnp.sum(es[1] * es[1])

    def more(state):
        count, *sizes = state
        largest = jnp.maximum(*sizes)
        return (count < 12) & (largest >= 4e-6) & (largest < 1e4)

    _, *sizes = lax.while_loop(more, step, (0, F32(1.0), F32(1.0)))

    for spin in range(2):

        @pl.when(jnp.logical_not(sizes[spin] < 4e-6))
        def _(spin=spin):
            x_ref[spin] = unit

            def eliminate(j, carry):
                row = a_ref[spin, pl.ds(j, 1), :]
                pivot = jnp.sum(jnp.where(cols[:1] == j, row, 0.0), axis=1, keepdims=True)
                a = a_ref[spin]
                column = jnp.sum(jnp.where(cols == j, a, 0.0), axis=1, keepdims=True)
                factor = jnp.where(rows[:, :1] > j, column / pivot, 0.0)
                x = x_ref[spin]
                x_row = x_ref[spin, pl.ds(j, 1), :]
                a_ref[spin] = a - factor * row
                x_ref[spin] = x - factor * x_row
                return carry

            lax.fori_loop(0, 2 * T, eliminate, 0)
            pivots = jnp.sum(jnp.where(rows == cols, a_ref[spin], 0.0), axis=1, keepdims=True)
            x_ref[spin] = x_ref[spin] / jnp.sqrt(pivots)

    first_col = m[COL] == 0
    for spin in range(2):
        x = x_ref[spin] * scales[spin]
        part = jnp.where(first_col, x[:T], x[T:])
        ritz[spin, 0] = dot(both[spin].reshape(4 * T, 2 * T), part.astype(BF), ((1,), (1,))).astype(BF).reshape(4, T, T)
        projected[spin] = dot3(dot3(x, k_ref[spin]), part, ((1,), (1,)))


def whole(shape):
    return pl.BlockSpec(shape, lambda i, m, n=len(shape): (0,) * n)


def call(kernel, m, arrays, outs, name, flops=0, specs=None, scratch=()):
    arrays = list(arrays)
    moved = sum(a.size * a.dtype.itemsize for a in [*arrays, *outs])
    return pl.pallas_call(
        kernel,
        out_shape=outs,
        grid_spec=pltpu.PrefetchScalarGridSpec(
            num_scalar_prefetch=1,
            grid=(1,),
            in_specs=specs or [whole(a.shape) for a in arrays],
            out_specs=[whole(o.shape) for o in outs],
            scratch_shapes=list(scratch),
        ),
        compiler_params=pltpu.CompilerParams(vmem_limit_bytes=32 * 1024 * 1024),
        cost_estimate=pl.CostEstimate(flops=2 * T * T * 2 * T * flops, bytes_accessed=moved, transcendentals=0),
        name=name,
    )(m, *arrays)


def table(neighbour_index, block_count):
    gx, gy, col = (lax.axis_index(a) for a in AXES)
    spin = col ^ ((gx >> 1) & 1)
    toward = jnp.where(gx % 2 == 0, 1, -1)
    dx = jnp.stack([jnp.zeros_like(toward), toward, -toward])
    codes = (dx[:, None] + 1) * 3 + jnp.arange(3, dtype=jnp.int32)[None, :]
    slots = jnp.arange(NB, dtype=jnp.int32)
    index, count = neighbour_index[0], block_count[0]
    match = (index[:, None, None, :] == codes[None, :, :, None]) & (
        slots < count[:, None, None, None]
    )
    found = jnp.sum(jnp.where(match, slots + 1, 0), axis=-1) - 1
    scalars = jnp.stack([spin, col, gy % 2, gx % 2])
    return spin, col, jnp.concatenate([found.reshape(-1), scalars]).astype(jnp.int32)


def shaped(shape, dtype):
    return jax.ShapeDtypeStruct(shape, dtype)


def per_device(start_block, hamiltonian, neighbour_index, block_count):
    sizes = tuple(lax.axis_size(a) for a in AXES)
    members = sizes[0] * sizes[1]
    block, full = (4, T, 2 * T), (2 * T, 2 * T)
    spin, col, m = table(neighbour_index, block_count)

    other = swap_col(sizes, lax.dynamic_index_in_dim(start_block, 1 - spin, 0, keepdims=False)[0])
    own = lax.dynamic_index_in_dim(start_block, spin, 0, keepdims=False)[0]
    spin_block = pl.BlockSpec((1,) + hamiltonian.shape[1:], lambda i, m: (m[SPIN], 0, 0, 0, 0, 0))
    corner = shaped((T, T), BF)
    o, h_p, h_q = call(
        order_kernel, m, [hamiltonian], [shaped((4, T, NB * T), BF), corner, corner], "order", specs=[spin_block]
    )
    tile = shaped((T, 2 * T), BF)
    ext = pltpu.VMEM((6, T, 2 * T), BF)
    other, o = lax.optimization_barrier((other, o))
    outs = [shaped(block, BF), tile, tile]
    v, p, q = call(join_kernel, m, [own, other], outs, "join")

    def apply_ham(x, p, q, more, outs):
        p, q = swap(sizes, p, 0, 1), swap(sizes, q, 0, 2)
        a, b = swap(sizes, x, 1, 0), swap(sizes, x, 2, 0)
        a_corner, b_corner = swap(sizes, q, 1, 0), swap(sizes, q, 2, 0)
        (edge,) = call(edge_kernel, m, [a, b], [shaped((2, T, 2 * T), BF)], "edge")
        edge = swap(sizes, edge, 0, 1)
        (acc,) = call(
            core_kernel, m, [o, x, p, q, a, b, a_corner, b_corner], [shaped(block, F32)], "core", 150, scratch=[ext]
        )
        kernel = functools.partial(rim_kernel, last=len(more) > 0)
        return call(kernel, m, [o, edge, acc, *more], outs, "rim", 2)

    first, p, q = apply_ham(v, p, q, [], outs)
    longer = shaped((3 * T // 2, 2 * T), BF)
    second, p, q = apply_ham(first, p, q, [v, h_p, h_q], [shaped(block, BF), longer, longer])

    right = shift(sizes, second, -1, 0)
    p, q = swap(sizes, p, 0, 1), swap(sizes, q, 0, 2)
    corr, turned, acc = call(
        corr_kernel, m, [o, second], [shaped(full, F32), shaped((2 * T, 4 * T), BF), shaped(block, F32)], "corr", 15
    )
    piece = shaped((members // 2, 1, 5 * T), F32)
    mine, theirs = call(
        gram_kernel, m, [o, turned, p, q, right, acc, corr], [piece, piece], "gram", 30
    )

    rows = members * second.shape[0] * second.shape[1]
    partial = mine + swap(sizes, theirs, 0, 1)
    (both,) = call(stack_kernel, m, [second, swap_col(sizes, second)], [shaped((2, *block), BF)], "stack", 300)
    total = exchange(sizes, partial, False)
    total, both = lax.optimization_barrier((total, both))
    total = total.sum(axis=0, keepdims=True) / rows
    mine = exchange(sizes, jnp.broadcast_to(total, (members, 1, 5 * T)), True)
    theirs = swap(sizes, mine, 0, 1)
    squared = pltpu.VMEM((2, *full), F32)
    return tuple(
        call(
            final_kernel, m, [mine, theirs, both],
            [shaped((2, 1, 4, T, T), BF), shaped((2, 2 * T, T), F32)], "final", 200,
            scratch=[squared, squared, squared],
        )
    )


def solution(mesh):
    return jax.shard_map(
        per_device,
        mesh=mesh,
        in_specs=(
            P(None, "gx", "gy", None, "col"),
            P(None, "gx", "gy", None, None, None),
            P("gx", "gy", None),
            P("gx", "gy"),
        ),
        out_specs=(P(None, "gx", "gy", None, "col"), P(None, None, "col")),
        check_vma=False,
    )
```

```python
import functools

import jax
import jax.numpy as jnp
from jax import lax
from jax.experimental import pallas as pl
from jax.experimental.pallas import tpu as pltpu
from jax.sharding import PartitionSpec as P

NB = 9
T = 128
AXES = ("gx", "gy", "col")
BF = jnp.bfloat16
F32 = jnp.float32
SPIN, COL, PAR_Y, PAR_X = 36, 37, 38, 39


def col_of(gx, spin):
    return spin ^ ((gx >> 1) & 1)


def device(sizes, gx, gy, col):
    return ((gx % sizes[0]) * sizes[1] + gy % sizes[1]) * sizes[2] + col


def pairs(sizes, target):
    out = []
    for gx in range(sizes[0]):
        for gy in range(sizes[1]):
            for spin in range(2):
                there = target(gx, gy)
                there_gx = there[0] % sizes[0]
                out.append(
                    (
                        device(sizes, gx, gy, col_of(gx, spin)),
                        device(sizes, there_gx, there[1], col_of(there_gx, spin)),
                    )
                )
    return out


def partner(index, kind):
    if kind == 0:
        return index
    return index + 1 if (index % 2 == 0) == (kind == 1) else index - 1


def swap(sizes, block, kind_x, kind_y):
    perm = pairs(sizes, lambda gx, gy: (partner(gx, kind_x), partner(gy, kind_y)))
    return lax.ppermute(block, AXES, perm)


def shift(sizes, block, dx, dy):
    return lax.ppermute(block, AXES, pairs(sizes, lambda gx, gy: (gx + dx, gy + dy)))


def swap_col(sizes, block):
    perm = [(d, d ^ 1) for d in range(sizes[0] * sizes[1] * 2)]
    return lax.ppermute(block, AXES, perm)


def exchange(sizes, pieces, joint):
    groups = [
        [
            device(sizes, gx, gy, col_of(gx, spin))
            for gx in range(sizes[0])
            for gy in range(core, sizes[1], 2)
        ]
        for core in range(2)
        for spin in range(2)
    ]
    if joint:
        groups = [groups[0] + groups[1], groups[2] + groups[3]]
    return lax.all_to_all(pieces, AXES, 0, 0, axis_index_groups=groups, tiled=True)


def dot(a, b, dims=((1,), (0,))):
    return lax.dot_general(a, b, (dims, ((), ())), preferred_element_type=F32)


def split(a):
    high = a.astype(BF)
    return high, (a - high.astype(F32)).astype(BF)


def dot3(a, b, dims=((1,), (0,))):
    (ah, al), (bh, bl) = split(a), split(b)
    return dot(ah, bh, dims) + (dot(ah, bl, dims) + dot(al, bh, dims))


def order_kernel(m, h, o, p, q):
    def block(tile, at):
        slot = m[tile * 9 + at]
        found = h[0, 0, tile, jnp.maximum(slot, 0)]
        return jnp.where(slot >= 0, found, jnp.zeros_like(found))

    for tile in range(4):
        for at in range(9):
            o[tile, :, at * T : (at + 1) * T] = block(tile, at)
    even = m[PAR_Y] == 0
    side = 1 + m[PAR_X]
    down, up = block(0, side * 3), block(3, side * 3 + 2)
    p[...] = jnp.where(even, up, down)
    q[...] = jnp.where(even, down, up)


def blocks(o, tile, sides, dys):
    out = []
    for side in sides:
        at = (side * 3 + dys[0]) * T
        if not isinstance(side, int):
            at = pl.multiple_of(at, T)
        out.append(o[tile, :, pl.ds(at, len(dys) * T)])
    return out[0] if len(out) == 1 else jnp.concatenate(out, axis=1)


def store_edges(m, ref, p, q):
    even = m[PAR_Y] == 0
    p[:T] = ref[pl.ds(jnp.where(even, 3, 0), 1)].reshape(T, 2 * T)
    q[:T] = ref[pl.ds(jnp.where(even, 0, 3), 1)].reshape(T, 2 * T)


def join_kernel(m, own, other, v, p, q):
    first_col = m[COL] == 0
    v[:, :, :T] = jnp.where(first_col, own[...], other[...])
    v[:, :, T:] = jnp.where(first_col, other[...], own[...])
    store_edges(m, v, p, q)
    q[T:] = v[0, : q.shape[0] - T]


def edge_kernel(m, a, b, a_out, b_out):
    at = jnp.where(m[PAR_Y] == 0, 3, 0)
    a_out[...] = a[at]
    b_out[...] = b[at]


def low_high(m, p, q):
    even = m[PAR_Y] == 0
    return jnp.where(even, q, p), jnp.where(even, p, q)


def product(o, tile, sides, at, sources):
    row = blocks(o, tile, sides, [place - tile for place in at])
    return dot(row, jnp.concatenate([x.reshape(len(at) * T, 2 * T) for x in sources], axis=0))


def outer_product(m, o, at_p, tiles):
    high = m[PAR_Y] == 0 if at_p else m[PAR_Y] != 0
    top = blocks(o, 3, (1, 2), (2,))
    bottom = blocks(o, 0, (1, 2), (0,))
    return dot(jnp.where(high, top, bottom), jnp.concatenate(tiles, axis=0)), high


def core_kernel(m, o, x, p, q, a, b, acc, ext):
    ext[0], ext[5] = low_high(m, p[...], q[:T])
    ext[1:5] = x[...]
    for tile in range(4):
        total = product(o, tile, (0,), range(tile, tile + 3), [ext[tile : tile + 3]])
        at = [place for place in range(tile, tile + 3) if 1 <= place <= 4]
        acc[tile] = total + product(o, tile, (1, 2), at, [y[at[0] - 1 : at[-1]] for y in (a, b)])


def rim_kernel(m, o, a_edge, b_edge, a_corner, b_corner, acc, *rest, last):
    if last:
        before, h_p, h_q, out, p, q = rest
    else:
        out, p, q = rest
    at_p, high = outer_product(m, o, True, [a_edge[...], b_edge[...]])
    at_q, _ = outer_product(m, o, False, [a_corner[:T], b_corner[:T]])
    for tile in range(4):
        total = acc[tile]
        if tile == 0:
            total += jnp.where(high, at_q, at_p)
        if tile == 3:
            total += jnp.where(high, at_p, at_q)
        if last:
            out[tile] = (total - before[tile].astype(F32)).astype(BF)
        else:
            out[tile] = (0.5 * total).astype(BF)
    store_edges(m, out, p, q)
    if last:
        for to, block in ((p, h_p), (q, h_q)):
            to[T:, :T] = block[: T // 2]
            to[T:, T:] = block[T // 2 :]
    else:
        q[T:] = out[0, : q.shape[0] - T]


def corr_kernel(m, o, s, corr, turned, acc):
    flat = s[...].reshape(4 * T, 2 * T)
    turned[...] = flat.T
    corr[...] = dot(turned[...], flat)
    for tile in range(4):
        total = 0.5 * dot(blocks(o, tile, (0,), (1,)), s[tile])
        if tile < 3:
            total += dot(blocks(o, tile, (0,), (2,)), s[tile + 1])
        acc[tile] = total


def places():
    shape = (2 * T, 2 * T)
    return lax.broadcasted_iota(jnp.int32, shape, 0), lax.broadcasted_iota(jnp.int32, shape, 1)


def gram_kernel(m, o, turned, p, q, right, acc, corr, mine, theirs):
    side = 1 + m[PAR_X]
    parts = []
    for tile in range(4):
        at = [place for place in range(tile, tile + 3) if 1 <= place <= 4]
        parts.append(acc[tile] + product(o, tile, (side,), at, [right[at[0] - 1 : at[-1]]]))
    even = m[PAR_Y] == 0
    above = jnp.where(even, p[:T], q[:T])
    parts[3] += product(o, 3, (0,), (5,), [above])
    high, low = split(jnp.concatenate(parts, axis=0))
    half = dot(turned[...], high) + dot(turned[...], low)
    for got, at in ((p, jnp.where(even, 3, 0)), (q, jnp.where(even, 0, 3))):
        block = jnp.concatenate([got[T:, :T], got[T:, T:]], axis=0)
        high, low = split(dot(block, right[at]))
        half += dot(got[:T], high, ((0,), (0,))) + dot(got[:T], low, ((0,), (0,)))
    coupling = half + half.T
    rows, cols = places()
    both = jnp.where(rows >= cols, corr[...], coupling)
    diagonal = jnp.sum(jnp.where(rows == cols, coupling, 0.0), axis=1, keepdims=True)
    first, second = pack(both[:T], diagonal[:T]), pack(both[T:], diagonal[T:])
    even = m[PAR_Y] == 0
    mine[:, 0, :] = jnp.where(even, first, second)
    theirs[:, 0, :] = jnp.where(even, second, first)


def pack(square, diagonal):
    lane = lax.broadcasted_iota(jnp.int32, (T // 2, T), 1)
    extra = jnp.where(lane == 0, diagonal[: T // 2], jnp.where(lane == 1, diagonal[T // 2 :], 0.0))
    return jnp.concatenate([square[: T // 2], square[T // 2 :], extra], axis=1)


def unpack(table):
    square = jnp.concatenate([table[:, : 2 * T], table[:, 2 * T : 4 * T]], axis=0)
    return square, jnp.concatenate([table[:, 4 * T : 4 * T + 1], table[:, 4 * T + 1 : 4 * T + 2]], axis=0)


def lower_part(e, rows, cols):
    return jnp.where(rows > cols, e, jnp.where(rows == cols, 0.5 * e, 0.0))


def squares(m, mine, theirs, spin):
    even = m[PAR_Y] == 0
    half = slice(spin * T // 2, (spin + 1) * T // 2)
    first, second = mine[half, 0, :], theirs[half, 0, :]
    top = unpack(jnp.where(even, first, second))
    bottom = unpack(jnp.where(even, second, first))
    both = jnp.concatenate([top[0], bottom[0]], axis=0)
    diagonal = jnp.concatenate([top[1], bottom[1]], axis=0)
    rows, cols = places()
    turned = both.T
    corr = jnp.where(rows >= cols, both, turned)
    return corr, jnp.where(rows < cols, both, jnp.where(rows == cols, diagonal, turned))


def stack_kernel(m, s, other, both):
    both[pl.ds(m[SPIN], 1)] = s[...][None]
    both[pl.ds(1 - m[SPIN], 1)] = other[...][None]


def final_kernel(m, mine, theirs, both, ritz, projected, x_ref, a_ref, k_ref):
    rows, cols = places()
    unit = (rows == cols).astype(F32)
    scales = []
    for spin in range(2):
        corr, k_ref[spin] = squares(m, mine, theirs, spin)
        on_diagonal = jnp.where(rows == cols, corr, 0.0)
        scale_row = 1.0 / jnp.sqrt(jnp.sum(on_diagonal, axis=0, keepdims=True))
        scale_col = 1.0 / jnp.sqrt(jnp.sum(on_diagonal, axis=1, keepdims=True))
        scaled = corr * scale_row * scale_col
        scales.append(scale_row)
        a_ref[spin] = scaled
        e = scaled - unit
        f = lower_part(e, rows, cols)
        f_half = f.astype(BF)
        fe = dot(f_half, e.astype(BF))
        e = dot((f + fe - e).astype(BF), f_half, ((1,), (1,))) - fe
        x = unit - f
        x_ref[spin] = x - dot(lower_part(e, rows, cols).astype(BF), x.astype(BF))

    def step(state):
        count, _, _ = state
        xs = [x_ref[spin] for spin in range(2)]
        es = [dot3(xs[spin], a_ref[spin]) for spin in range(2)]
        es = [dot3(es[spin], xs[spin], ((1,), (1,))) - unit for spin in range(2)]
        for spin in range(2):
            x_ref[spin] = xs[spin] - dot(lower_part(es[spin], rows, cols).astype(BF), xs[spin].astype(BF))
        return count + 1, jnp.sum(es[0] * es[0]), jnp.sum(es[1] * es[1])

    def more(state):
        count, *sizes = state
        largest = jnp.maximum(*sizes)
        return (count < 12) & (largest >= 4e-6) & (largest < 1e4)

    _, *sizes = lax.while_loop(more, step, (0, F32(1.0), F32(1.0)))

    for spin in range(2):

        @pl.when(jnp.logical_not(sizes[spin] < 4e-6))
        def _(spin=spin):
            x_ref[spin] = unit

            def eliminate(j, carry):
                row = a_ref[spin, pl.ds(j, 1), :]
                pivot = jnp.sum(jnp.where(cols[:1] == j, row, 0.0), axis=1, keepdims=True)
                a = a_ref[spin]
                column = jnp.sum(jnp.where(cols == j, a, 0.0), axis=1, keepdims=True)
                factor = jnp.where(rows[:, :1] > j, column / pivot, 0.0)
                x = x_ref[spin]
                x_row = x_ref[spin, pl.ds(j, 1), :]
                a_ref[spin] = a - factor * row
                x_ref[spin] = x - factor * x_row
                return carry

            lax.fori_loop(0, 2 * T, eliminate, 0)
            pivots = jnp.sum(jnp.where(rows == cols, a_ref[spin], 0.0), axis=1, keepdims=True)
            x_ref[spin] = x_ref[spin] / jnp.sqrt(pivots)

    first_col = m[COL] == 0
    for spin in range(2):
        x = x_ref[spin] * scales[spin]
        part = jnp.where(first_col, x[:T], x[T:])
        ritz[spin, 0] = dot(both[spin].reshape(4 * T, 2 * T), part.astype(BF), ((1,), (1,))).astype(BF).reshape(4, T, T)
        projected[spin] = dot3(dot3(x, k_ref[spin]), part, ((1,), (1,)))


def whole(shape):
    return pl.BlockSpec(shape, lambda i, m, n=len(shape): (0,) * n)


def call(kernel, m, arrays, outs, name, flops=0, specs=None, scratch=(), free=False):
    arrays = list(arrays)
    moved = 0 if free else sum(a.size * a.dtype.itemsize for a in [*arrays, *outs])
    return pl.pallas_call(
        kernel,
        out_shape=outs,
        grid_spec=pltpu.PrefetchScalarGridSpec(
            num_scalar_prefetch=1,
            grid=(1,),
            in_specs=specs or [whole(a.shape) for a in arrays],
            out_specs=[whole(o.shape) for o in outs],
            scratch_shapes=list(scratch),
        ),
        compiler_params=pltpu.CompilerParams(vmem_limit_bytes=32 * 1024 * 1024),
        cost_estimate=pl.CostEstimate(flops=2 * T * T * 2 * T * flops, bytes_accessed=moved, transcendentals=0),
        name=name,
    )(m, *arrays)


def table(neighbour_index, block_count):
    gx, gy, col = (lax.axis_index(a) for a in AXES)
    spin = col ^ ((gx >> 1) & 1)
    toward = jnp.where(gx % 2 == 0, 1, -1)
    dx = jnp.stack([jnp.zeros_like(toward), toward, -toward])
    codes = (dx[:, None] + 1) * 3 + jnp.arange(3, dtype=jnp.int32)[None, :]
    slots = jnp.arange(NB, dtype=jnp.int32)
    index, count = neighbour_index[0], block_count[0]
    match = (index[:, None, None, :] == codes[None, :, :, None]) & (
        slots < count[:, None, None, None]
    )
    found = jnp.sum(jnp.where(match, slots + 1, 0), axis=-1) - 1
    scalars = jnp.stack([spin, col, gy % 2, gx % 2])
    return spin, col, jnp.concatenate([found.reshape(-1), scalars]).astype(jnp.int32)


def shaped(shape, dtype):
    return jax.ShapeDtypeStruct(shape, dtype)


def per_device(start_block, hamiltonian, neighbour_index, block_count):
    sizes = tuple(lax.axis_size(a) for a in AXES)
    members = sizes[0] * sizes[1]
    block, full = (4, T, 2 * T), (2 * T, 2 * T)
    spin, col, m = table(neighbour_index, block_count)

    other = swap_col(sizes, lax.dynamic_index_in_dim(start_block, 1 - spin, 0, keepdims=False)[0])
    own = lax.dynamic_index_in_dim(start_block, spin, 0, keepdims=False)[0]
    spin_block = pl.BlockSpec((1,) + hamiltonian.shape[1:], lambda i, m: (m[SPIN], 0, 0, 0, 0, 0))
    corner = shaped((T, T), BF)
    o, h_p, h_q = call(
        order_kernel, m, [hamiltonian], [shaped((4, T, NB * T), BF), corner, corner], "order", specs=[spin_block]
    )
    tile = shaped((T, 2 * T), BF)
    ext = pltpu.VMEM((6, T, 2 * T), BF)
    other, o = lax.optimization_barrier((other, o))
    outs = [shaped(block, BF), tile, shaped((T + 16, 2 * T), BF)]
    v, p, q = call(join_kernel, m, [own, other], outs, "join")

    def apply_ham(x, p, q, more, outs):
        p, q = swap(sizes, p, 0, 1), swap(sizes, q, 0, 2)
        a, b = swap(sizes, x, 1, 0), swap(sizes, x, 2, 0)
        a_corner, b_corner = swap(sizes, q, 1, 0), swap(sizes, q, 2, 0)
        a_edge, b_edge = call(edge_kernel, m, [a, b], [tile, tile], "edge", free=True)
        a_edge, b_edge = swap(sizes, a_edge, 0, 1), swap(sizes, b_edge, 0, 1)
        (acc,) = call(
            core_kernel, m, [o, x, p, q, a, b], [shaped(block, F32)], "core", free=True, scratch=[ext]
        )
        kernel = functools.partial(rim_kernel, last=len(more) > 0)
        return call(kernel, m, [o, a_edge, b_edge, a_corner, b_corner, acc, *more], outs, "rim", 2)

    first, p, q = apply_ham(v, p, q, [], outs)
    longer = shaped((3 * T // 2, 2 * T), BF)
    second, p, q = apply_ham(first, p, q, [v, h_p, h_q], [shaped(block, BF), longer, longer])

    right = shift(sizes, second, -1, 0)
    p, q = swap(sizes, p, 0, 1), swap(sizes, q, 0, 2)
    corr, turned, acc = call(
        corr_kernel, m, [o, second], [shaped(full, F32), shaped((2 * T, 4 * T), BF), shaped(block, F32)], "corr", 15
    )
    piece = shaped((members // 2, 1, 5 * T), F32)
    mine, theirs = call(
        gram_kernel, m, [o, turned, p, q, right, acc, corr], [piece, piece], "gram", 30
    )

    rows = members * second.shape[0] * second.shape[1]
    partial = mine + swap(sizes, theirs, 0, 1)
    (both,) = call(stack_kernel, m, [second, swap_col(sizes, second)], [shaped((2, *block), BF)], "stack", 200)
    total = exchange(sizes, partial, False)
    total, both = lax.optimization_barrier((total, both))
    total = total.sum(axis=0, keepdims=True) / rows
    mine = exchange(sizes, jnp.broadcast_to(total, (members, 1, 5 * T)), True)
    theirs = swap(sizes, mine, 0, 1)
    squared = pltpu.VMEM((2, *full), F32)
    return tuple(
        call(
            final_kernel, m, [mine, theirs, both],
            [shaped((2, 1, 4, T, T), BF), shaped((2, 2 * T, T), F32)], "final", 200,
            scratch=[squared, squared, squared],
        )
    )


def solution(mesh):
    return jax.shard_map(
        per_device,
        mesh=mesh,
        in_specs=(
            P(None, "gx", "gy", None, "col"),
            P(None, "gx", "gy", None, None, None),
            P("gx", "gy", None),
            P("gx", "gy"),
        ),
        out_specs=(P(None, "gx", "gy", None, "col"), P(None, None, "col")),
        check_vma=False,
    )
```

```python
import functools

import jax
import jax.numpy as jnp
from jax import lax
from jax.experimental import pallas as pl
from jax.experimental.pallas import tpu as pltpu
from jax.sharding import PartitionSpec as P

NB = 9
T = 128
AXES = ("gx", "gy", "col")
BF = jnp.bfloat16
F32 = jnp.float32
SPIN, COL, PAR_Y, PAR_X = 36, 37, 38, 39


def col_of(gx, spin):
    return spin ^ ((gx >> 1) & 1)


def device(sizes, gx, gy, col):
    return ((gx % sizes[0]) * sizes[1] + gy % sizes[1]) * sizes[2] + col


def pairs(sizes, target):
    out = []
    for gx in range(sizes[0]):
        for gy in range(sizes[1]):
            for spin in range(2):
                there = target(gx, gy)
                there_gx = there[0] % sizes[0]
                out.append(
                    (
                        device(sizes, gx, gy, col_of(gx, spin)),
                        device(sizes, there_gx, there[1], col_of(there_gx, spin)),
                    )
                )
    return out


def partner(index, kind):
    if kind == 0:
        return index
    return index + 1 if (index % 2 == 0) == (kind == 1) else index - 1


def swap(sizes, block, kind_x, kind_y):
    perm = pairs(sizes, lambda gx, gy: (partner(gx, kind_x), partner(gy, kind_y)))
    return lax.ppermute(block, AXES, perm)


def shift(sizes, block, dx, dy):
    return lax.ppermute(block, AXES, pairs(sizes, lambda gx, gy: (gx + dx, gy + dy)))


def swap_col(sizes, block):
    perm = [(d, d ^ 1) for d in range(sizes[0] * sizes[1] * 2)]
    return lax.ppermute(block, AXES, perm)


def exchange(sizes, pieces, joint):
    groups = [
        [
            device(sizes, gx, gy, col_of(gx, spin))
            for gx in range(sizes[0])
            for gy in range(core, sizes[1], 2)
        ]
        for core in range(2)
        for spin in range(2)
    ]
    if joint:
        groups = [groups[0] + groups[1], groups[2] + groups[3]]
    return lax.all_to_all(pieces, AXES, 0, 0, axis_index_groups=groups, tiled=True)


def dot(a, b, dims=((1,), (0,))):
    return lax.dot_general(a, b, (dims, ((), ())), preferred_element_type=F32)


def split(a):
    high = a.astype(BF)
    return high, (a - high.astype(F32)).astype(BF)


def dot3(a, b, dims=((1,), (0,))):
    (ah, al), (bh, bl) = split(a), split(b)
    return dot(ah, bh, dims) + (dot(ah, bl, dims) + dot(al, bh, dims))


def order_kernel(m, h, o, p, q):
    def block(tile, at):
        slot = m[tile * 9 + at]
        found = h[0, 0, tile, jnp.maximum(slot, 0)]
        return jnp.where(slot >= 0, found, jnp.zeros_like(found))

    for tile in range(4):
        for at in range(9):
            o[tile, :, at * T : (at + 1) * T] = block(tile, at)
    even = m[PAR_Y] == 0
    side = 1 + m[PAR_X]
    down, up = block(0, side * 3), block(3, side * 3 + 2)
    p[...] = jnp.where(even, up, down)
    q[...] = jnp.where(even, down, up)


def blocks(o, tile, sides, dys):
    out = []
    for side in sides:
        at = (side * 3 + dys[0]) * T
        if not isinstance(side, int):
            at = pl.multiple_of(at, T)
        out.append(o[tile, :, pl.ds(at, len(dys) * T)])
    return out[0] if len(out) == 1 else jnp.concatenate(out, axis=1)


def store_edges(m, ref, p, q):
    even = m[PAR_Y] == 0
    p[:T] = ref[pl.ds(jnp.where(even, 3, 0), 1)].reshape(T, 2 * T)
    q[:T] = ref[pl.ds(jnp.where(even, 0, 3), 1)].reshape(T, 2 * T)


def join_kernel(m, own, other, v, p, q):
    first_col = m[COL] == 0
    v[:, :, :T] = jnp.where(first_col, own[...], other[...])
    v[:, :, T:] = jnp.where(first_col, other[...], own[...])
    store_edges(m, v, p, q)


def corner_kernel(m, q, out):
    out[:T] = q[...]
    out[T:] = q[: out.shape[0] - T]


def edge_kernel(m, a, b, a_out, b_out):
    at = jnp.where(m[PAR_Y] == 0, 3, 0)
    a_out[...] = a[at]
    b_out[...] = b[at]


def low_high(m, p, q):
    even = m[PAR_Y] == 0
    return jnp.where(even, q, p), jnp.where(even, p, q)


def product(o, tile, sides, at, sources):
    row = blocks(o, tile, sides, [place - tile for place in at])
    return dot(row, jnp.concatenate([x.reshape(len(at) * T, 2 * T) for x in sources], axis=0))


def outer_product(m, o, at_p, tiles):
    high = m[PAR_Y] == 0 if at_p else m[PAR_Y] != 0
    top = blocks(o, 3, (1, 2), (2,))
    bottom = blocks(o, 0, (1, 2), (0,))
    return dot(jnp.where(high, top, bottom), jnp.concatenate(tiles, axis=0)), high


def core_kernel(m, o, x, p, q, a, b, acc, ext):
    ext[0], ext[5] = low_high(m, p[...], q[...])
    ext[1:5] = x[...]
    for tile in range(4):
        total = product(o, tile, (0,), range(tile, tile + 3), [ext[tile : tile + 3]])
        at = [place for place in range(tile, tile + 3) if 1 <= place <= 4]
        acc[tile] = total + product(o, tile, (1, 2), at, [y[at[0] - 1 : at[-1]] for y in (a, b)])


def rim_kernel(m, o, a_edge, b_edge, a_corner, b_corner, acc, *rest, last):
    if last:
        before, h_p, h_q, out, p, q = rest
    else:
        out, p, q = rest
    at_p, high = outer_product(m, o, True, [a_edge[...], b_edge[...]])
    at_q, _ = outer_product(m, o, False, [a_corner[:T], b_corner[:T]])
    for tile in range(4):
        total = acc[tile]
        if tile == 0:
            total += jnp.where(high, at_q, at_p)
        if tile == 3:
            total += jnp.where(high, at_p, at_q)
        if last:
            out[tile] = (total - before[tile].astype(F32)).astype(BF)
        else:
            out[tile] = (0.5 * total).astype(BF)
    store_edges(m, out, p, q)
    if last:
        for to, block in ((p, h_p), (q, h_q)):
            to[T:, :T] = block[: T // 2]
            to[T:, T:] = block[T // 2 :]


def corr_kernel(m, o, s, corr, turned, acc):
    flat = s[...].reshape(4 * T, 2 * T)
    turned[...] = flat.T
    corr[...] = dot(turned[...], flat)
    for tile in range(4):
        total = 0.5 * dot(blocks(o, tile, (0,), (1,)), s[tile])
        if tile < 3:
            total += dot(blocks(o, tile, (0,), (2,)), s[tile + 1])
        acc[tile] = total


def places():
    shape = (2 * T, 2 * T)
    return lax.broadcasted_iota(jnp.int32, shape, 0), lax.broadcasted_iota(jnp.int32, shape, 1)


def gram_kernel(m, o, turned, p, q, right, acc, corr, mine, theirs):
    side = 1 + m[PAR_X]
    parts = []
    for tile in range(4):
        at = [place for place in range(tile, tile + 3) if 1 <= place <= 4]
        parts.append(acc[tile] + product(o, tile, (side,), at, [right[at[0] - 1 : at[-1]]]))
    even = m[PAR_Y] == 0
    above = jnp.where(even, p[:T], q[:T])
    parts[3] += product(o, 3, (0,), (5,), [above])
    high, low = split(jnp.concatenate(parts, axis=0))
    half = dot(turned[...], high) + dot(turned[...], low)
    for got, at in ((p, jnp.where(even, 3, 0)), (q, jnp.where(even, 0, 3))):
        block = jnp.concatenate([got[T:, :T], got[T:, T:]], axis=0)
        high, low = split(dot(block, right[at]))
        half += dot(got[:T], high, ((0,), (0,))) + dot(got[:T], low, ((0,), (0,)))
    coupling = half + half.T
    rows, cols = places()
    both = jnp.where(rows >= cols, corr[...], coupling)
    diagonal = jnp.sum(jnp.where(rows == cols, coupling, 0.0), axis=1, keepdims=True)
    first, second = pack(both[:T], diagonal[:T]), pack(both[T:], diagonal[T:])
    even = m[PAR_Y] == 0
    mine[:, 0, :] = jnp.where(even, first, second)
    theirs[:, 0, :] = jnp.where(even, second, first)


def pack(square, diagonal):
    lane = lax.broadcasted_iota(jnp.int32, (T // 2, T), 1)
    extra = jnp.where(lane == 0, diagonal[: T // 2], jnp.where(lane == 1, diagonal[T // 2 :], 0.0))
    return jnp.concatenate([square[: T // 2], square[T // 2 :], extra], axis=1)


def unpack(table):
    square = jnp.concatenate([table[:, : 2 * T], table[:, 2 * T : 4 * T]], axis=0)
    return square, jnp.concatenate([table[:, 4 * T : 4 * T + 1], table[:, 4 * T + 1 : 4 * T + 2]], axis=0)


def lower_part(e, rows, cols):
    return jnp.where(rows > cols, e, jnp.where(rows == cols, 0.5 * e, 0.0))


def squares(m, mine, theirs, spin):
    even = m[PAR_Y] == 0
    half = slice(spin * T // 2, (spin + 1) * T // 2)
    first, second = mine[half, 0, :], theirs[half, 0, :]
    top = unpack(jnp.where(even, first, second))
    bottom = unpack(jnp.where(even, second, first))
    both = jnp.concatenate([top[0], bottom[0]], axis=0)
    diagonal = jnp.concatenate([top[1], bottom[1]], axis=0)
    rows, cols = places()
    turned = both.T
    corr = jnp.where(rows >= cols, both, turned)
    return corr, jnp.where(rows < cols, both, jnp.where(rows == cols, diagonal, turned))


def stack_kernel(m, s, other, both):
    both[pl.ds(m[SPIN], 1)] = s[...][None]
    both[pl.ds(1 - m[SPIN], 1)] = other[...][None]


def final_kernel(m, mine, theirs, both, ritz, projected, x_ref, a_ref, k_ref):
    rows, cols = places()
    unit = (rows == cols).astype(F32)
    scales = []
    for spin in range(2):
        corr, k_ref[spin] = squares(m, mine, theirs, spin)
        on_diagonal = jnp.where(rows == cols, corr, 0.0)
        scale_row = 1.0 / jnp.sqrt(jnp.sum(on_diagonal, axis=0, keepdims=True))
        scale_col = 1.0 / jnp.sqrt(jnp.sum(on_diagonal, axis=1, keepdims=True))
        scaled = corr * scale_row * scale_col
        scales.append(scale_row)
        a_ref[spin] = scaled
        e = scaled - unit
        f = lower_part(e, rows, cols)
        f_half = f.astype(BF)
        fe = dot(f_half, e.astype(BF))
        e = dot((f + fe - e).astype(BF), f_half, ((1,), (1,))) - fe
        x = unit - f
        x_ref[spin] = x - dot(lower_part(e, rows, cols).astype(BF), x.astype(BF))

    def step(state):
        count, _, _ = state
        xs = [x_ref[spin] for spin in range(2)]
        es = [dot3(xs[spin], a_ref[spin]) for spin in range(2)]
        es = [dot3(es[spin], xs[spin], ((1,), (1,))) - unit for spin in range(2)]
        for spin in range(2):
            x_ref[spin] = xs[spin] - dot(lower_part(es[spin], rows, cols).astype(BF), xs[spin].astype(BF))
        return count + 1, jnp.sum(es[0] * es[0]), jnp.sum(es[1] * es[1])

    def more(state):
        count, *sizes = state
        largest = jnp.maximum(*sizes)
        return (count < 12) & (largest >= 4e-6) & (largest < 1e4)

    _, *sizes = lax.while_loop(more, step, (0, F32(1.0), F32(1.0)))

    for spin in range(2):

        @pl.when(jnp.logical_not(sizes[spin] < 4e-6))
        def _(spin=spin):
            x_ref[spin] = unit

            def eliminate(j, carry):
                row = a_ref[spin, pl.ds(j, 1), :]
                pivot = jnp.sum(jnp.where(cols[:1] == j, row, 0.0), axis=1, keepdims=True)
                a = a_ref[spin]
                column = jnp.sum(jnp.where(cols == j, a, 0.0), axis=1, keepdims=True)
                factor = jnp.where(rows[:, :1] > j, column / pivot, 0.0)
                x = x_ref[spin]
                x_row = x_ref[spin, pl.ds(j, 1), :]
                a_ref[spin] = a - factor * row
                x_ref[spin] = x - factor * x_row
                return carry

            lax.fori_loop(0, 2 * T, eliminate, 0)
            pivots = jnp.sum(jnp.where(rows == cols, a_ref[spin], 0.0), axis=1, keepdims=True)
            x_ref[spin] = x_ref[spin] / jnp.sqrt(pivots)

    first_col = m[COL] == 0
    for spin in range(2):
        x = x_ref[spin] * scales[spin]
        part = jnp.where(first_col, x[:T], x[T:])
        ritz[spin, 0] = dot(both[spin].reshape(4 * T, 2 * T), part.astype(BF), ((1,), (1,))).astype(BF).reshape(4, T, T)
        projected[spin] = dot3(dot3(x, k_ref[spin]), part, ((1,), (1,)))


def whole(shape):
    return pl.BlockSpec(shape, lambda i, m, n=len(shape): (0,) * n)


def call(kernel, m, arrays, outs, name, flops=0, specs=None, scratch=(), free=False):
    arrays = list(arrays)
    moved = 0 if free else sum(a.size * a.dtype.itemsize for a in [*arrays, *outs])
    return pl.pallas_call(
        kernel,
        out_shape=outs,
        grid_spec=pltpu.PrefetchScalarGridSpec(
            num_scalar_prefetch=1,
            grid=(1,),
            in_specs=specs or [whole(a.shape) for a in arrays],
            out_specs=[whole(o.shape) for o in outs],
            scratch_shapes=list(scratch),
        ),
        compiler_params=pltpu.CompilerParams(vmem_limit_bytes=32 * 1024 * 1024),
        cost_estimate=pl.CostEstimate(flops=2 * T * T * 2 * T * flops, bytes_accessed=moved, transcendentals=0),
        name=name,
    )(m, *arrays)


def table(neighbour_index, block_count):
    gx, gy, col = (lax.axis_index(a) for a in AXES)
    spin = col ^ ((gx >> 1) & 1)
    toward = jnp.where(gx % 2 == 0, 1, -1)
    dx = jnp.stack([jnp.zeros_like(toward), toward, -toward])
    codes = (dx[:, None] + 1) * 3 + jnp.arange(3, dtype=jnp.int32)[None, :]
    slots = jnp.arange(NB, dtype=jnp.int32)
    index, count = neighbour_index[0], block_count[0]
    match = (index[:, None, None, :] == codes[None, :, :, None]) & (
        slots < count[:, None, None, None]
    )
    found = jnp.sum(jnp.where(match, slots + 1, 0), axis=-1) - 1
    scalars = jnp.stack([spin, col, gy % 2, gx % 2])
    return spin, col, jnp.concatenate([found.reshape(-1), scalars]).astype(jnp.int32)


def shaped(shape, dtype):
    return jax.ShapeDtypeStruct(shape, dtype)


def per_device(start_block, hamiltonian, neighbour_index, block_count):
    sizes = tuple(lax.axis_size(a) for a in AXES)
    members = sizes[0] * sizes[1]
    block, full = (4, T, 2 * T), (2 * T, 2 * T)
    spin, col, m = table(neighbour_index, block_count)

    other = swap_col(sizes, lax.dynamic_index_in_dim(start_block, 1 - spin, 0, keepdims=False)[0])
    own = lax.dynamic_index_in_dim(start_block, spin, 0, keepdims=False)[0]
    spin_block = pl.BlockSpec((1,) + hamiltonian.shape[1:], lambda i, m: (m[SPIN], 0, 0, 0, 0, 0))
    corner = shaped((T, T), BF)
    o, h_p, h_q = call(
        order_kernel, m, [hamiltonian], [shaped((4, T, NB * T), BF), corner, corner], "order", specs=[spin_block]
    )
    tile = shaped((T, 2 * T), BF)
    ext = pltpu.VMEM((6, T, 2 * T), BF)
    other, o = lax.optimization_barrier((other, o))
    outs = [shaped(block, BF), tile, tile]
    v, p, q = call(join_kernel, m, [own, other], outs, "join")

    def apply_ham(x, p, q, more, outs):
        p, q = swap(sizes, p, 0, 1), swap(sizes, q, 0, 2)
        a, b = swap(sizes, x, 1, 0), swap(sizes, x, 2, 0)
        (corner,) = call(corner_kernel, m, [q], [shaped((T + 16, 2 * T), BF)], "corner", 300)
        a_corner, b_corner = swap(sizes, corner, 1, 0), swap(sizes, corner, 2, 0)
        a_edge, b_edge = call(edge_kernel, m, [a, b], [tile, tile], "edge", free=True)
        a_edge, b_edge = swap(sizes, a_edge, 0, 1), swap(sizes, b_edge, 0, 1)
        (acc,) = call(
            core_kernel, m, [o, x, p, q, a, b], [shaped(block, F32)], "core", free=True, scratch=[ext]
        )
        kernel = functools.partial(rim_kernel, last=len(more) > 0)
        return call(kernel, m, [o, a_edge, b_edge, a_corner, b_corner, acc, *more], outs, "rim", 2)

    first, p, q = apply_ham(v, p, q, [], outs)
    longer = shaped((3 * T // 2, 2 * T), BF)
    second, p, q = apply_ham(first, p, q, [v, h_p, h_q], [shaped(block, BF), longer, longer])

    right = shift(sizes, second, -1, 0)
    p, q = swap(sizes, p, 0, 1), swap(sizes, q, 0, 2)
    corr, turned, acc = call(
        corr_kernel, m, [o, second], [shaped(full, F32), shaped((2 * T, 4 * T), BF), shaped(block, F32)], "corr", 15
    )
    piece = shaped((members // 2, 1, 5 * T), F32)
    mine, theirs = call(
        gram_kernel, m, [o, turned, p, q, right, acc, corr], [piece, piece], "gram", 30
    )

    rows = members * second.shape[0] * second.shape[1]
    partial = mine + swap(sizes, theirs, 0, 1)
    (both,) = call(stack_kernel, m, [second, swap_col(sizes, second)], [shaped((2, *block), BF)], "stack", 200)
    total = exchange(sizes, partial, False)
    total, both = lax.optimization_barrier((total, both))
    total = total.sum(axis=0, keepdims=True) / rows
    mine = exchange(sizes, jnp.broadcast_to(total, (members, 1, 5 * T)), True)
    theirs = swap(sizes, mine, 0, 1)
    squared = pltpu.VMEM((2, *full), F32)
    return tuple(
        call(
            final_kernel, m, [mine, theirs, both],
            [shaped((2, 1, 4, T, T), BF), shaped((2, 2 * T, T), F32)], "final", 200,
            scratch=[squared, squared, squared],
        )
    )


def solution(mesh):
    return jax.shard_map(
        per_device,
        mesh=mesh,
        in_specs=(
            P(None, "gx", "gy", None, "col"),
            P(None, "gx", "gy", None, None, None),
            P("gx", "gy", None),
            P("gx", "gy"),
        ),
        out_specs=(P(None, "gx", "gy", None, "col"), P(None, None, "col")),
        check_vma=False,
    )
```

```python
import functools

import jax
import jax.numpy as jnp
from jax import lax
from jax.experimental import pallas as pl
from jax.experimental.pallas import tpu as pltpu
from jax.sharding import PartitionSpec as P

NB = 9
T = 128
AXES = ("gx", "gy", "col")
BF = jnp.bfloat16
F32 = jnp.float32
SPIN, COL, PAR_Y, PAR_X = 36, 37, 38, 39


def col_of(gx, spin):
    return spin ^ ((gx >> 1) & 1)


def device(sizes, gx, gy, col):
    return ((gx % sizes[0]) * sizes[1] + gy % sizes[1]) * sizes[2] + col


def pairs(sizes, target):
    out = []
    for gx in range(sizes[0]):
        for gy in range(sizes[1]):
            for spin in range(2):
                there = target(gx, gy)
                there_gx = there[0] % sizes[0]
                out.append(
                    (
                        device(sizes, gx, gy, col_of(gx, spin)),
                        device(sizes, there_gx, there[1], col_of(there_gx, spin)),
                    )
                )
    return out


def partner(index, kind):
    if kind == 0:
        return index
    return index + 1 if (index % 2 == 0) == (kind == 1) else index - 1


def swap(sizes, block, kind_x, kind_y):
    perm = pairs(sizes, lambda gx, gy: (partner(gx, kind_x), partner(gy, kind_y)))
    return lax.ppermute(block, AXES, perm)


def shift(sizes, block, dx, dy):
    return lax.ppermute(block, AXES, pairs(sizes, lambda gx, gy: (gx + dx, gy + dy)))


def swap_col(sizes, block):
    perm = [(d, d ^ 1) for d in range(sizes[0] * sizes[1] * 2)]
    return lax.ppermute(block, AXES, perm)


def exchange(sizes, pieces, joint):
    groups = [
        [
            device(sizes, gx, gy, col_of(gx, spin))
            for gx in range(sizes[0])
            for gy in range(core, sizes[1], 2)
        ]
        for core in range(2)
        for spin in range(2)
    ]
    if joint:
        groups = [groups[0] + groups[1], groups[2] + groups[3]]
    return lax.all_to_all(pieces, AXES, 0, 0, axis_index_groups=groups, tiled=True)


def dot(a, b, dims=((1,), (0,))):
    return lax.dot_general(a, b, (dims, ((), ())), preferred_element_type=F32)


def split(a):
    high = a.astype(BF)
    return high, (a - high.astype(F32)).astype(BF)


def dot3(a, b, dims=((1,), (0,))):
    (ah, al), (bh, bl) = split(a), split(b)
    return dot(ah, bh, dims) + (dot(ah, bl, dims) + dot(al, bh, dims))


def order_kernel(m, h, o, p, q):
    def block(tile, at):
        slot = m[tile * 9 + at]
        found = h[0, 0, tile, jnp.maximum(slot, 0)]
        return jnp.where(slot >= 0, found, jnp.zeros_like(found))

    for tile in range(4):
        for at in range(9):
            o[tile, :, at * T : (at + 1) * T] = block(tile, at)
    even = m[PAR_Y] == 0
    side = 1 + m[PAR_X]
    down, up = block(0, side * 3), block(3, side * 3 + 2)
    p[...] = jnp.where(even, up, down)
    q[...] = jnp.where(even, down, up)


def blocks(o, tile, sides, dys):
    out = []
    for side in sides:
        at = (side * 3 + dys[0]) * T
        if not isinstance(side, int):
            at = pl.multiple_of(at, T)
        out.append(o[tile, :, pl.ds(at, len(dys) * T)])
    return out[0] if len(out) == 1 else jnp.concatenate(out, axis=1)


def store_edges(m, ref, p, q):
    even = m[PAR_Y] == 0
    p[:T] = ref[pl.ds(jnp.where(even, 3, 0), 1)].reshape(T, 2 * T)
    q[:T] = ref[pl.ds(jnp.where(even, 0, 3), 1)].reshape(T, 2 * T)


def join_kernel(m, own, other, v, p, q):
    first_col = m[COL] == 0
    v[:, :, :T] = jnp.where(first_col, own[...], other[...])
    v[:, :, T:] = jnp.where(first_col, other[...], own[...])
    store_edges(m, v, p, q)
    q[T:] = v[0, : q.shape[0] - T]


def edge_kernel(m, b, a, a_out, b_out):
    at = jnp.where(m[PAR_Y] == 0, 3, 0)
    a_out[...] = a[at]
    b_out[...] = b[at]


def low_high(m, p, q):
    even = m[PAR_Y] == 0
    return jnp.where(even, q, p), jnp.where(even, p, q)


def product(o, tile, sides, at, sources):
    row = blocks(o, tile, sides, [place - tile for place in at])
    return dot(row, jnp.concatenate([x.reshape(len(at) * T, 2 * T) for x in sources], axis=0))


def outer_product(m, o, at_p, tiles):
    high = m[PAR_Y] == 0 if at_p else m[PAR_Y] != 0
    top = blocks(o, 3, (1, 2), (2,))
    bottom = blocks(o, 0, (1, 2), (0,))
    return dot(jnp.where(high, top, bottom), jnp.concatenate(tiles, axis=0)), high


def core_kernel(m, o, x, p, q, b, a, acc, ext):
    ext[0], ext[5] = low_high(m, p[...], q[:T])
    ext[1:5] = x[...]
    for tile in range(4):
        total = product(o, tile, (0,), range(tile, tile + 3), [ext[tile : tile + 3]])
        at = [place for place in range(tile, tile + 3) if 1 <= place <= 4]
        acc[tile] = total + product(o, tile, (1, 2), at, [y[at[0] - 1 : at[-1]] for y in (a, b)])


def rim_kernel(m, o, a_edge, b_edge, b_corner, a_corner, acc, *rest, last):
    if last:
        before, h_p, h_q, out, p, q = rest
    else:
        out, p, q = rest
    at_p, high = outer_product(m, o, True, [a_edge[...], b_edge[...]])
    at_q, _ = outer_product(m, o, False, [a_corner[:T], b_corner[:T]])
    for tile in range(4):
        total = acc[tile]
        if tile == 0:
            total += jnp.where(high, at_q, at_p)
        if tile == 3:
            total += jnp.where(high, at_p, at_q)
        if last:
            out[tile] = (total - before[tile].astype(F32)).astype(BF)
        else:
            out[tile] = (0.5 * total).astype(BF)
    store_edges(m, out, p, q)
    if last:
        for to, block in ((p, h_p), (q, h_q)):
            to[T:, :T] = block[: T // 2]
            to[T:, T:] = block[T // 2 :]
    else:
        q[T:] = out[0, : q.shape[0] - T]


def corr_kernel(m, o, s, corr, turned, acc):
    flat = s[...].reshape(4 * T, 2 * T)
    turned[...] = flat.T
    corr[...] = dot(turned[...], flat)
    for tile in range(4):
        total = 0.5 * dot(blocks(o, tile, (0,), (1,)), s[tile])
        if tile < 3:
            total += dot(blocks(o, tile, (0,), (2,)), s[tile + 1])
        acc[tile] = total


def places():
    shape = (2 * T, 2 * T)
    return lax.broadcasted_iota(jnp.int32, shape, 0), lax.broadcasted_iota(jnp.int32, shape, 1)


def gram_kernel(m, o, turned, p, q, right, acc, corr, mine, theirs):
    side = 1 + m[PAR_X]
    parts = []
    for tile in range(4):
        at = [place for place in range(tile, tile + 3) if 1 <= place <= 4]
        parts.append(acc[tile] + product(o, tile, (side,), at, [right[at[0] - 1 : at[-1]]]))
    even = m[PAR_Y] == 0
    above = jnp.where(even, p[:T], q[:T])
    parts[3] += product(o, 3, (0,), (5,), [above])
    high, low = split(jnp.concatenate(parts, axis=0))
    half = dot(turned[...], high) + dot(turned[...], low)
    for got, at in ((p, jnp.where(even, 3, 0)), (q, jnp.where(even, 0, 3))):
        block = jnp.concatenate([got[T:, :T], got[T:, T:]], axis=0)
        high, low = split(dot(block, right[at]))
        half += dot(got[:T], high, ((0,), (0,))) + dot(got[:T], low, ((0,), (0,)))
    coupling = half + half.T
    rows, cols = places()
    both = jnp.where(rows >= cols, corr[...], coupling)
    diagonal = jnp.sum(jnp.where(rows == cols, coupling, 0.0), axis=1, keepdims=True)
    first, second = pack(both[:T], diagonal[:T]), pack(both[T:], diagonal[T:])
    even = m[PAR_Y] == 0
    mine[:, 0, :] = jnp.where(even, first, second)
    theirs[:, 0, :] = jnp.where(even, second, first)


def pack(square, diagonal):
    lane = lax.broadcasted_iota(jnp.int32, (T // 2, T), 1)
    extra = jnp.where(lane == 0, diagonal[: T // 2], jnp.where(lane == 1, diagonal[T // 2 :], 0.0))
    return jnp.concatenate([square[: T // 2], square[T // 2 :], extra], axis=1)


def unpack(table):
    square = jnp.concatenate([table[:, : 2 * T], table[:, 2 * T : 4 * T]], axis=0)
    return square, jnp.concatenate([table[:, 4 * T : 4 * T + 1], table[:, 4 * T + 1 : 4 * T + 2]], axis=0)


def lower_part(e, rows, cols):
    return jnp.where(rows > cols, e, jnp.where(rows == cols, 0.5 * e, 0.0))


def squares(m, mine, theirs, spin):
    even = m[PAR_Y] == 0
    half = slice(spin * T // 2, (spin + 1) * T // 2)
    first, second = mine[half, 0, :], theirs[half, 0, :]
    top = unpack(jnp.where(even, first, second))
    bottom = unpack(jnp.where(even, second, first))
    both = jnp.concatenate([top[0], bottom[0]], axis=0)
    diagonal = jnp.concatenate([top[1], bottom[1]], axis=0)
    rows, cols = places()
    turned = both.T
    corr = jnp.where(rows >= cols, both, turned)
    return corr, jnp.where(rows < cols, both, jnp.where(rows == cols, diagonal, turned))


def stack_kernel(m, s, other, both):
    both[pl.ds(m[SPIN], 1)] = s[...][None]
    both[pl.ds(1 - m[SPIN], 1)] = other[...][None]


def final_kernel(m, mine, theirs, both, ritz, projected, x_ref, a_ref, k_ref):
    rows, cols = places()
    unit = (rows == cols).astype(F32)
    scales = []
    for spin in range(2):
        corr, k_ref[spin] = squares(m, mine, theirs, spin)
        on_diagonal = jnp.where(rows == cols, corr, 0.0)
        scale_row = 1.0 / jnp.sqrt(jnp.sum(on_diagonal, axis=0, keepdims=True))
        scale_col = 1.0 / jnp.sqrt(jnp.sum(on_diagonal, axis=1, keepdims=True))
        scaled = corr * scale_row * scale_col
        scales.append(scale_row)
        a_ref[spin] = scaled
        e = scaled - unit
        f = lower_part(e, rows, cols)
        f_half = f.astype(BF)
        fe = dot(f_half, e.astype(BF))
        e = dot((f + fe - e).astype(BF), f_half, ((1,), (1,))) - fe
        x = unit - f
        x_ref[spin] = x - dot(lower_part(e, rows, cols).astype(BF), x.astype(BF))

    def step(state):
        count, _, _ = state
        xs = [x_ref[spin] for spin in range(2)]
        es = [dot3(xs[spin], a_ref[spin]) for spin in range(2)]
        es = [dot3(es[spin], xs[spin], ((1,), (1,))) - unit for spin in range(2)]
        for spin in range(2):
            x_ref[spin] = xs[spin] - dot(lower_part(es[spin], rows, cols).astype(BF), xs[spin].astype(BF))
        return count + 1, jnp.sum(es[0] * es[0]), jnp.sum(es[1] * es[1])

    def more(state):
        count, *sizes = state
        largest = jnp.maximum(*sizes)
        return (count < 12) & (largest >= 4e-6) & (largest < 1e4)

    _, *sizes = lax.while_loop(more, step, (0, F32(1.0), F32(1.0)))

    for spin in range(2):

        @pl.when(jnp.logical_not(sizes[spin] < 4e-6))
        def _(spin=spin):
            x_ref[spin] = unit

            def eliminate(j, carry):
                row = a_ref[spin, pl.ds(j, 1), :]
                pivot = jnp.sum(jnp.where(cols[:1] == j, row, 0.0), axis=1, keepdims=True)
                a = a_ref[spin]
                column = jnp.sum(jnp.where(cols == j, a, 0.0), axis=1, keepdims=True)
                factor = jnp.where(rows[:, :1] > j, column / pivot, 0.0)
                x = x_ref[spin]
                x_row = x_ref[spin, pl.ds(j, 1), :]
                a_ref[spin] = a - factor * row
                x_ref[spin] = x - factor * x_row
                return carry

            lax.fori_loop(0, 2 * T, eliminate, 0)
            pivots = jnp.sum(jnp.where(rows == cols, a_ref[spin], 0.0), axis=1, keepdims=True)
            x_ref[spin] = x_ref[spin] / jnp.sqrt(pivots)

    first_col = m[COL] == 0
    for spin in range(2):
        x = x_ref[spin] * scales[spin]
        part = jnp.where(first_col, x[:T], x[T:])
        ritz[spin, 0] = dot(both[spin].reshape(4 * T, 2 * T), part.astype(BF), ((1,), (1,))).astype(BF).reshape(4, T, T)
        projected[spin] = dot3(dot3(x, k_ref[spin]), part, ((1,), (1,)))


def whole(shape):
    return pl.BlockSpec(shape, lambda i, m, n=len(shape): (0,) * n)


def call(kernel, m, arrays, outs, name, flops=0, specs=None, scratch=(), free=False):
    arrays = list(arrays)
    moved = 0 if free else sum(a.size * a.dtype.itemsize for a in [*arrays, *outs])
    return pl.pallas_call(
        kernel,
        out_shape=outs,
        grid_spec=pltpu.PrefetchScalarGridSpec(
            num_scalar_prefetch=1,
            grid=(1,),
            in_specs=specs or [whole(a.shape) for a in arrays],
            out_specs=[whole(o.shape) for o in outs],
            scratch_shapes=list(scratch),
        ),
        compiler_params=pltpu.CompilerParams(vmem_limit_bytes=32 * 1024 * 1024),
        cost_estimate=pl.CostEstimate(flops=2 * T * T * 2 * T * flops, bytes_accessed=moved, transcendentals=0),
        name=name,
    )(m, *arrays)


def table(neighbour_index, block_count):
    gx, gy, col = (lax.axis_index(a) for a in AXES)
    spin = col ^ ((gx >> 1) & 1)
    toward = jnp.where(gx % 2 == 0, 1, -1)
    dx = jnp.stack([jnp.zeros_like(toward), toward, -toward])
    codes = (dx[:, None] + 1) * 3 + jnp.arange(3, dtype=jnp.int32)[None, :]
    slots = jnp.arange(NB, dtype=jnp.int32)
    index, count = neighbour_index[0], block_count[0]
    match = (index[:, None, None, :] == codes[None, :, :, None]) & (
        slots < count[:, None, None, None]
    )
    found = jnp.sum(jnp.where(match, slots + 1, 0), axis=-1) - 1
    scalars = jnp.stack([spin, col, gy % 2, gx % 2])
    return spin, col, jnp.concatenate([found.reshape(-1), scalars]).astype(jnp.int32)


def shaped(shape, dtype):
    return jax.ShapeDtypeStruct(shape, dtype)


def per_device(start_block, hamiltonian, neighbour_index, block_count):
    sizes = tuple(lax.axis_size(a) for a in AXES)
    members = sizes[0] * sizes[1]
    block, full = (4, T, 2 * T), (2 * T, 2 * T)
    spin, col, m = table(neighbour_index, block_count)

    other = swap_col(sizes, lax.dynamic_index_in_dim(start_block, 1 - spin, 0, keepdims=False)[0])
    own = lax.dynamic_index_in_dim(start_block, spin, 0, keepdims=False)[0]
    spin_block = pl.BlockSpec((1,) + hamiltonian.shape[1:], lambda i, m: (m[SPIN], 0, 0, 0, 0, 0))
    corner = shaped((T, T), BF)
    o, h_p, h_q = call(
        order_kernel, m, [hamiltonian], [shaped((4, T, NB * T), BF), corner, corner], "order", specs=[spin_block]
    )
    tile = shaped((T, 2 * T), BF)
    ext = pltpu.VMEM((6, T, 2 * T), BF)
    other, o = lax.optimization_barrier((other, o))
    outs = [shaped(block, BF), tile, shaped((T + 16, 2 * T), BF)]
    v, p, q = call(join_kernel, m, [own, other], outs, "join")

    def apply_ham(x, p, q, more, outs):
        p, q = swap(sizes, p, 0, 1), swap(sizes, q, 0, 2)
        b, a = swap(sizes, x, 2, 0), swap(sizes, x, 1, 0)
        b_corner, a_corner = swap(sizes, q, 2, 0), swap(sizes, q, 1, 0)
        a_edge, b_edge = call(edge_kernel, m, [b, a], [tile, tile], "edge", free=True)
        a_edge, b_edge = swap(sizes, a_edge, 0, 1), swap(sizes, b_edge, 0, 1)
        (acc,) = call(
            core_kernel, m, [o, x, p, q, b, a], [shaped(block, F32)], "core", free=True, scratch=[ext]
        )
        kernel = functools.partial(rim_kernel, last=len(more) > 0)
        return call(kernel, m, [o, a_edge, b_edge, b_corner, a_corner, acc, *more], outs, "rim", 2)

    first, p, q = apply_ham(v, p, q, [], outs)
    longer = shaped((3 * T // 2, 2 * T), BF)
    second, p, q = apply_ham(first, p, q, [v, h_p, h_q], [shaped(block, BF), longer, longer])

    right = shift(sizes, second, -1, 0)
    p, q = swap(sizes, p, 0, 1), swap(sizes, q, 0, 2)
    corr, turned, acc = call(
        corr_kernel, m, [o, second], [shaped(full, F32), shaped((2 * T, 4 * T), BF), shaped(block, F32)], "corr", 15
    )
    piece = shaped((members // 2, 1, 5 * T), F32)
    mine, theirs = call(
        gram_kernel, m, [o, turned, p, q, right, acc, corr], [piece, piece], "gram", 30
    )

    rows = members * second.shape[0] * second.shape[1]
    partial = mine + swap(sizes, theirs, 0, 1)
    (both,) = call(stack_kernel, m, [second, swap_col(sizes, second)], [shaped((2, *block), BF)], "stack", 200)
    total = exchange(sizes, partial, False)
    total, both = lax.optimization_barrier((total, both))
    total = total.sum(axis=0, keepdims=True) / rows
    mine = exchange(sizes, jnp.broadcast_to(total, (members, 1, 5 * T)), True)
    theirs = swap(sizes, mine, 0, 1)
    squared = pltpu.VMEM((2, *full), F32)
    return tuple(
        call(
            final_kernel, m, [mine, theirs, both],
            [shaped((2, 1, 4, T, T), BF), shaped((2, 2 * T, T), F32)], "final", 200,
            scratch=[squared, squared, squared],
        )
    )


def solution(mesh):
    return jax.shard_map(
        per_device,
        mesh=mesh,
        in_specs=(
            P(None, "gx", "gy", None, "col"),
            P(None, "gx", "gy", None, None, None),
            P("gx", "gy", None),
            P("gx", "gy"),
        ),
        out_specs=(P(None, "gx", "gy", None, "col"), P(None, None, "col")),
        check_vma=False,
    )
```

```python
import functools

import jax
import jax.numpy as jnp
from jax import lax
from jax.experimental import pallas as pl
from jax.experimental.pallas import tpu as pltpu
from jax.sharding import PartitionSpec as P

NB = 9
T = 128
AXES = ("gx", "gy", "col")
BF = jnp.bfloat16
F32 = jnp.float32
SPIN, COL, PAR_Y, PAR_X = 36, 37, 38, 39


def col_of(gx, spin):
    return spin ^ ((gx >> 1) & 1)


def device(sizes, gx, gy, col):
    return ((gx % sizes[0]) * sizes[1] + gy % sizes[1]) * sizes[2] + col


def pairs(sizes, target):
    out = []
    for gx in range(sizes[0]):
        for gy in range(sizes[1]):
            for spin in range(2):
                there = target(gx, gy)
                there_gx = there[0] % sizes[0]
                out.append(
                    (
                        device(sizes, gx, gy, col_of(gx, spin)),
                        device(sizes, there_gx, there[1], col_of(there_gx, spin)),
                    )
                )
    return out


def partner(index, kind):
    if kind == 0:
        return index
    return index + 1 if (index % 2 == 0) == (kind == 1) else index - 1


def swap(sizes, block, kind_x, kind_y):
    perm = pairs(sizes, lambda gx, gy: (partner(gx, kind_x), partner(gy, kind_y)))
    return lax.ppermute(block, AXES, perm)


def shift(sizes, block, dx, dy):
    return lax.ppermute(block, AXES, pairs(sizes, lambda gx, gy: (gx + dx, gy + dy)))


def swap_col(sizes, block):
    perm = [(d, d ^ 1) for d in range(sizes[0] * sizes[1] * 2)]
    return lax.ppermute(block, AXES, perm)


def exchange(sizes, pieces, joint):
    groups = [
        [
            device(sizes, gx, gy, col_of(gx, spin))
            for gx in range(sizes[0])
            for gy in range(core, sizes[1], 2)
        ]
        for core in range(2)
        for spin in range(2)
    ]
    if joint:
        groups = [groups[0] + groups[1], groups[2] + groups[3]]
    return lax.all_to_all(pieces, AXES, 0, 0, axis_index_groups=groups, tiled=True)


def dot(a, b, dims=((1,), (0,))):
    return lax.dot_general(a, b, (dims, ((), ())), preferred_element_type=F32)


def split(a):
    high = a.astype(BF)
    return high, (a - high.astype(F32)).astype(BF)


def dot3(a, b, dims=((1,), (0,))):
    (ah, al), (bh, bl) = split(a), split(b)
    return dot(ah, bh, dims) + (dot(ah, bl, dims) + dot(al, bh, dims))


def order_kernel(m, h, o, p, q):
    def block(tile, at):
        slot = m[tile * 9 + at]
        found = h[0, 0, tile, jnp.maximum(slot, 0)]
        return jnp.where(slot >= 0, found, jnp.zeros_like(found))

    for tile in range(4):
        for at in range(9):
            o[tile, :, at * T : (at + 1) * T] = block(tile, at)
    even = m[PAR_Y] == 0
    side = 1 + m[PAR_X]
    down, up = block(0, side * 3), block(3, side * 3 + 2)
    p[...] = jnp.where(even, up, down)
    q[...] = jnp.where(even, down, up)


def blocks(o, tile, sides, dys):
    out = []
    for side in sides:
        at = (side * 3 + dys[0]) * T
        if not isinstance(side, int):
            at = pl.multiple_of(at, T)
        out.append(o[tile, :, pl.ds(at, len(dys) * T)])
    return out[0] if len(out) == 1 else jnp.concatenate(out, axis=1)


def store_edges(m, ref, p, q):
    even = m[PAR_Y] == 0
    p[:T] = ref[pl.ds(jnp.where(even, 3, 0), 1)].reshape(T, 2 * T)
    q[:T] = ref[pl.ds(jnp.where(even, 0, 3), 1)].reshape(T, 2 * T)


def join_kernel(m, own, other, v, p, q):
    first_col = m[COL] == 0
    v[:, :, :T] = jnp.where(first_col, own[...], other[...])
    v[:, :, T:] = jnp.where(first_col, other[...], own[...])
    store_edges(m, v, p, q)
    q[T:] = v[0, : q.shape[0] - T]


def edge_kernel(m, b, a, a_out, b_out):
    at = jnp.where(m[PAR_Y] == 0, 3, 0)
    a_out[...] = a[at]
    b_out[...] = b[at]


def low_high(m, p, q):
    even = m[PAR_Y] == 0
    return jnp.where(even, q, p), jnp.where(even, p, q)


def product(o, tile, sides, at, sources):
    row = blocks(o, tile, sides, [place - tile for place in at])
    return dot(row, jnp.concatenate([x.reshape(len(at) * T, 2 * T) for x in sources], axis=0))


def outer_product(m, o, at_p, tiles):
    high = m[PAR_Y] == 0 if at_p else m[PAR_Y] != 0
    top = blocks(o, 3, (1, 2), (2,))
    bottom = blocks(o, 0, (1, 2), (0,))
    return dot(jnp.where(high, top, bottom), jnp.concatenate(tiles, axis=0)), high


def core_kernel(m, o, x, p, q, b, a, acc, ext):
    ext[0], ext[5] = low_high(m, p[...], q[:T])
    ext[1:5] = x[...]
    for tile in range(4):
        total = product(o, tile, (0,), range(tile, tile + 3), [ext[tile : tile + 3]])
        at = [place for place in range(tile, tile + 3) if 1 <= place <= 4]
        acc[tile] = total + product(o, tile, (1, 2), at, [y[at[0] - 1 : at[-1]] for y in (a, b)])


def rim_kernel(m, o, a_edge, b_edge, b_corner, a_corner, acc, *rest, last):
    if last:
        before, h_p, h_q, out, p, q = rest
    else:
        out, p, q = rest
    at_p, high = outer_product(m, o, True, [a_edge[...], b_edge[...]])
    at_q, _ = outer_product(m, o, False, [a_corner[:T], b_corner[:T]])
    for tile in range(4):
        total = acc[tile]
        if tile == 0:
            total += jnp.where(high, at_q, at_p)
        if tile == 3:
            total += jnp.where(high, at_p, at_q)
        if last:
            out[tile] = (total - before[tile].astype(F32)).astype(BF)
        else:
            out[tile] = (0.5 * total).astype(BF)
    store_edges(m, out, p, q)
    if last:
        for to, block in ((p, h_p), (q, h_q)):
            to[T:, :T] = block[: T // 2]
            to[T:, T:] = block[T // 2 :]
    else:
        q[T:] = out[0, : q.shape[0] - T]


def corr_kernel(m, o, s, corr, turned, acc):
    flat = s[...].reshape(4 * T, 2 * T)
    turned[...] = flat.T
    corr[...] = dot(turned[...], flat)
    for tile in range(4):
        total = 0.5 * dot(blocks(o, tile, (0,), (1,)), s[tile])
        if tile < 3:
            total += dot(blocks(o, tile, (0,), (2,)), s[tile + 1])
        acc[tile] = total


def places():
    shape = (2 * T, 2 * T)
    return lax.broadcasted_iota(jnp.int32, shape, 0), lax.broadcasted_iota(jnp.int32, shape, 1)


def gram_kernel(m, o, turned, q, p, right, acc, corr, mine, theirs):
    side = 1 + m[PAR_X]
    parts = []
    for tile in range(4):
        at = [place for place in range(tile, tile + 3) if 1 <= place <= 4]
        parts.append(acc[tile] + product(o, tile, (side,), at, [right[at[0] - 1 : at[-1]]]))
    even = m[PAR_Y] == 0
    above = jnp.where(even, p[:T], q[:T])
    parts[3] += product(o, 3, (0,), (5,), [above])
    high, low = split(jnp.concatenate(parts, axis=0))
    half = dot(turned[...], high) + dot(turned[...], low)
    for got, at in ((p, jnp.where(even, 3, 0)), (q, jnp.where(even, 0, 3))):
        block = jnp.concatenate([got[T:, :T], got[T:, T:]], axis=0)
        high, low = split(dot(block, right[at]))
        half += dot(got[:T], high, ((0,), (0,))) + dot(got[:T], low, ((0,), (0,)))
    coupling = half + half.T
    rows, cols = places()
    both = jnp.where(rows >= cols, corr[...], coupling)
    diagonal = jnp.sum(jnp.where(rows == cols, coupling, 0.0), axis=1, keepdims=True)
    first, second = pack(both[:T], diagonal[:T]), pack(both[T:], diagonal[T:])
    even = m[PAR_Y] == 0
    mine[:, 0, :] = jnp.where(even, first, second)
    theirs[:, 0, :] = jnp.where(even, second, first)


def pack(square, diagonal):
    lane = lax.broadcasted_iota(jnp.int32, (T // 2, T), 1)
    extra = jnp.where(lane == 0, diagonal[: T // 2], jnp.where(lane == 1, diagonal[T // 2 :], 0.0))
    return jnp.concatenate([square[: T // 2], square[T // 2 :], extra], axis=1)


def unpack(table):
    square = jnp.concatenate([table[:, : 2 * T], table[:, 2 * T : 4 * T]], axis=0)
    return square, jnp.concatenate([table[:, 4 * T : 4 * T + 1], table[:, 4 * T + 1 : 4 * T + 2]], axis=0)


def lower_part(e, rows, cols):
    return jnp.where(rows > cols, e, jnp.where(rows == cols, 0.5 * e, 0.0))


def squares(m, mine, theirs, spin):
    even = m[PAR_Y] == 0
    half = slice(spin * T // 2, (spin + 1) * T // 2)
    first, second = mine[half, 0, :], theirs[half, 0, :]
    top = unpack(jnp.where(even, first, second))
    bottom = unpack(jnp.where(even, second, first))
    both = jnp.concatenate([top[0], bottom[0]], axis=0)
    diagonal = jnp.concatenate([top[1], bottom[1]], axis=0)
    rows, cols = places()
    turned = both.T
    corr = jnp.where(rows >= cols, both, turned)
    return corr, jnp.where(rows < cols, both, jnp.where(rows == cols, diagonal, turned))


def stack_kernel(m, s, other, both):
    both[pl.ds(m[SPIN], 1)] = s[...][None]
    both[pl.ds(1 - m[SPIN], 1)] = other[...][None]


def final_kernel(m, mine, theirs, both, ritz, projected, x_ref, a_ref, k_ref):
    rows, cols = places()
    unit = (rows == cols).astype(F32)
    scales = []
    for spin in range(2):
        corr, k_ref[spin] = squares(m, mine, theirs, spin)
        on_diagonal = jnp.where(rows == cols, corr, 0.0)
        scale_row = 1.0 / jnp.sqrt(jnp.sum(on_diagonal, axis=0, keepdims=True))
        scale_col = 1.0 / jnp.sqrt(jnp.sum(on_diagonal, axis=1, keepdims=True))
        scaled = corr * scale_row * scale_col
        scales.append(scale_row)
        a_ref[spin] = scaled
        e = scaled - unit
        f = lower_part(e, rows, cols)
        f_half = f.astype(BF)
        fe = dot(f_half, e.astype(BF))
        e = dot((f + fe - e).astype(BF), f_half, ((1,), (1,))) - fe
        x = unit - f
        x_ref[spin] = x - dot(lower_part(e, rows, cols).astype(BF), x.astype(BF))

    def step(state):
        count, _, _ = state
        xs = [x_ref[spin] for spin in range(2)]
        es = [dot3(xs[spin], a_ref[spin]) for spin in range(2)]
        es = [dot3(es[spin], xs[spin], ((1,), (1,))) - unit for spin in range(2)]
        for spin in range(2):
            x_ref[spin] = xs[spin] - dot(lower_part(es[spin], rows, cols).astype(BF), xs[spin].astype(BF))
        return count + 1, jnp.sum(es[0] * es[0]), jnp.sum(es[1] * es[1])

    def more(state):
        count, *sizes = state
        largest = jnp.maximum(*sizes)
        return (count < 12) & (largest >= 4e-6) & (largest < 1e4)

    _, *sizes = lax.while_loop(more, step, (0, F32(1.0), F32(1.0)))

    for spin in range(2):

        @pl.when(jnp.logical_not(sizes[spin] < 4e-6))
        def _(spin=spin):
            x_ref[spin] = unit

            def eliminate(j, carry):
                row = a_ref[spin, pl.ds(j, 1), :]
                pivot = jnp.sum(jnp.where(cols[:1] == j, row, 0.0), axis=1, keepdims=True)
                a = a_ref[spin]
                column = jnp.sum(jnp.where(cols == j, a, 0.0), axis=1, keepdims=True)
                factor = jnp.where(rows[:, :1] > j, column / pivot, 0.0)
                x = x_ref[spin]
                x_row = x_ref[spin, pl.ds(j, 1), :]
                a_ref[spin] = a - factor * row
                x_ref[spin] = x - factor * x_row
                return carry

            lax.fori_loop(0, 2 * T, eliminate, 0)
            pivots = jnp.sum(jnp.where(rows == cols, a_ref[spin], 0.0), axis=1, keepdims=True)
            x_ref[spin] = x_ref[spin] / jnp.sqrt(pivots)

    first_col = m[COL] == 0
    for spin in range(2):
        x = x_ref[spin] * scales[spin]
        part = jnp.where(first_col, x[:T], x[T:])
        ritz[spin, 0] = dot(both[spin].reshape(4 * T, 2 * T), part.astype(BF), ((1,), (1,))).astype(BF).reshape(4, T, T)
        projected[spin] = dot3(dot3(x, k_ref[spin]), part, ((1,), (1,)))


def whole(shape):
    return pl.BlockSpec(shape, lambda i, m, n=len(shape): (0,) * n)


def call(kernel, m, arrays, outs, name, flops=0, specs=None, scratch=(), free=False):
    arrays = list(arrays)
    moved = 0 if free else sum(a.size * a.dtype.itemsize for a in [*arrays, *outs])
    return pl.pallas_call(
        kernel,
        out_shape=outs,
        grid_spec=pltpu.PrefetchScalarGridSpec(
            num_scalar_prefetch=1,
            grid=(1,),
            in_specs=specs or [whole(a.shape) for a in arrays],
            out_specs=[whole(o.shape) for o in outs],
            scratch_shapes=list(scratch),
        ),
        compiler_params=pltpu.CompilerParams(vmem_limit_bytes=32 * 1024 * 1024),
        cost_estimate=pl.CostEstimate(flops=2 * T * T * 2 * T * flops, bytes_accessed=moved, transcendentals=0),
        name=name,
    )(m, *arrays)


def table(neighbour_index, block_count):
    gx, gy, col = (lax.axis_index(a) for a in AXES)
    spin = col ^ ((gx >> 1) & 1)
    toward = jnp.where(gx % 2 == 0, 1, -1)
    dx = jnp.stack([jnp.zeros_like(toward), toward, -toward])
    codes = (dx[:, None] + 1) * 3 + jnp.arange(3, dtype=jnp.int32)[None, :]
    slots = jnp.arange(NB, dtype=jnp.int32)
    index, count = neighbour_index[0], block_count[0]
    match = (index[:, None, None, :] == codes[None, :, :, None]) & (
        slots < count[:, None, None, None]
    )
    found = jnp.sum(jnp.where(match, slots + 1, 0), axis=-1) - 1
    scalars = jnp.stack([spin, col, gy % 2, gx % 2])
    return spin, col, jnp.concatenate([found.reshape(-1), scalars]).astype(jnp.int32)


def shaped(shape, dtype):
    return jax.ShapeDtypeStruct(shape, dtype)


def per_device(start_block, hamiltonian, neighbour_index, block_count):
    sizes = tuple(lax.axis_size(a) for a in AXES)
    members = sizes[0] * sizes[1]
    block, full = (4, T, 2 * T), (2 * T, 2 * T)
    spin, col, m = table(neighbour_index, block_count)

    other = swap_col(sizes, lax.dynamic_index_in_dim(start_block, 1 - spin, 0, keepdims=False)[0])
    own = lax.dynamic_index_in_dim(start_block, spin, 0, keepdims=False)[0]
    spin_block = pl.BlockSpec((1,) + hamiltonian.shape[1:], lambda i, m: (m[SPIN], 0, 0, 0, 0, 0))
    corner = shaped((T, T), BF)
    o, h_p, h_q = call(
        order_kernel, m, [hamiltonian], [shaped((4, T, NB * T), BF), corner, corner], "order", specs=[spin_block]
    )
    tile = shaped((T, 2 * T), BF)
    ext = pltpu.VMEM((6, T, 2 * T), BF)
    other, o = lax.optimization_barrier((other, o))
    outs = [shaped(block, BF), tile, shaped((T + 16, 2 * T), BF)]
    v, p, q = call(join_kernel, m, [own, other], outs, "join")

    def apply_ham(x, p, q, more, outs):
        p, q = swap(sizes, p, 0, 1), swap(sizes, q, 0, 2)
        b, a = swap(sizes, x, 2, 0), swap(sizes, x, 1, 0)
        b_corner, a_corner = swap(sizes, q, 2, 0), swap(sizes, q, 1, 0)
        a_edge, b_edge = call(edge_kernel, m, [b, a], [tile, tile], "edge", free=True)
        a_edge, b_edge = swap(sizes, a_edge, 0, 1), swap(sizes, b_edge, 0, 1)
        (acc,) = call(
            core_kernel, m, [o, x, p, q, b, a], [shaped(block, F32)], "core", free=True, scratch=[ext]
        )
        kernel = functools.partial(rim_kernel, last=len(more) > 0)
        return call(kernel, m, [o, a_edge, b_edge, b_corner, a_corner, acc, *more], outs, "rim", 2)

    first, p, q = apply_ham(v, p, q, [], outs)
    longer = shaped((3 * T // 2, 2 * T), BF)
    second, p, q = apply_ham(first, p, q, [v, h_p, h_q], [shaped(block, BF), longer, longer])

    right = shift(sizes, second, -1, 0)
    q, p = swap(sizes, q, 0, 2), swap(sizes, p, 0, 1)
    corr, turned, acc = call(
        corr_kernel, m, [o, second], [shaped(full, F32), shaped((2 * T, 4 * T), BF), shaped(block, F32)], "corr", 15
    )
    piece = shaped((members // 2, 1, 5 * T), F32)
    mine, theirs = call(
        gram_kernel, m, [o, turned, q, p, right, acc, corr], [piece, piece], "gram", 30
    )

    rows = members * second.shape[0] * second.shape[1]
    partial = mine + swap(sizes, theirs, 0, 1)
    (both,) = call(stack_kernel, m, [second, swap_col(sizes, second)], [shaped((2, *block), BF)], "stack", 200)
    total = exchange(sizes, partial, False)
    total, both = lax.optimization_barrier((total, both))
    total = total.sum(axis=0, keepdims=True) / rows
    mine = exchange(sizes, jnp.broadcast_to(total, (members, 1, 5 * T)), True)
    theirs = swap(sizes, mine, 0, 1)
    squared = pltpu.VMEM((2, *full), F32)
    return tuple(
        call(
            final_kernel, m, [mine, theirs, both],
            [shaped((2, 1, 4, T, T), BF), shaped((2, 2 * T, T), F32)], "final", 200,
            scratch=[squared, squared, squared],
        )
    )


def solution(mesh):
    return jax.shard_map(
        per_device,
        mesh=mesh,
        in_specs=(
            P(None, "gx", "gy", None, "col"),
            P(None, "gx", "gy", None, None, None),
            P("gx", "gy", None),
            P("gx", "gy"),
        ),
        out_specs=(P(None, "gx", "gy", None, "col"), P(None, None, "col")),
        check_vma=False,
    )
```

```python
import functools

import jax
import jax.numpy as jnp
from jax import lax
from jax.experimental import pallas as pl
from jax.experimental.pallas import tpu as pltpu
from jax.sharding import PartitionSpec as P

NB = 9
T = 128
AXES = ("gx", "gy", "col")
BF = jnp.bfloat16
F32 = jnp.float32
SPIN, COL, PAR_Y, PAR_X = 36, 37, 38, 39


def col_of(gx, spin):
    return spin ^ ((gx >> 1) & 1)


def device(sizes, gx, gy, col):
    return ((gx % sizes[0]) * sizes[1] + gy % sizes[1]) * sizes[2] + col


def pairs(sizes, target):
    out = []
    for gx in range(sizes[0]):
        for gy in range(sizes[1]):
            for spin in range(2):
                there = target(gx, gy)
                there_gx = there[0] % sizes[0]
                out.append(
                    (
                        device(sizes, gx, gy, col_of(gx, spin)),
                        device(sizes, there_gx, there[1], col_of(there_gx, spin)),
                    )
                )
    return out


def partner(index, kind):
    if kind == 0:
        return index
    return index + 1 if (index % 2 == 0) == (kind == 1) else index - 1


def swap(sizes, block, kind_x, kind_y):
    perm = pairs(sizes, lambda gx, gy: (partner(gx, kind_x), partner(gy, kind_y)))
    return lax.ppermute(block, AXES, perm)


def shift(sizes, block, dx, dy):
    return lax.ppermute(block, AXES, pairs(sizes, lambda gx, gy: (gx + dx, gy + dy)))


def swap_col(sizes, block):
    perm = [(d, d ^ 1) for d in range(sizes[0] * sizes[1] * 2)]
    return lax.ppermute(block, AXES, perm)


def exchange(sizes, pieces, joint):
    groups = [
        [
            device(sizes, gx, gy, col_of(gx, spin))
            for gx in range(sizes[0])
            for gy in range(core, sizes[1], 2)
        ]
        for core in range(2)
        for spin in range(2)
    ]
    if joint:
        groups = [groups[0] + groups[1], groups[2] + groups[3]]
    return lax.all_to_all(pieces, AXES, 0, 0, axis_index_groups=groups, tiled=True)


def dot(a, b, dims=((1,), (0,))):
    return lax.dot_general(a, b, (dims, ((), ())), preferred_element_type=F32)


def split(a):
    high = a.astype(BF)
    return high, (a - high.astype(F32)).astype(BF)


def dot3(a, b, dims=((1,), (0,))):
    (ah, al), (bh, bl) = split(a), split(b)
    return dot(ah, bh, dims) + (dot(ah, bl, dims) + dot(al, bh, dims))


def order_kernel(m, h, o, p, q):
    def block(tile, at):
        slot = m[tile * 9 + at]
        found = h[0, 0, tile, jnp.maximum(slot, 0)]
        return jnp.where(slot >= 0, found, jnp.zeros_like(found))

    for tile in range(4):
        for at in range(9):
            o[tile, :, at * T : (at + 1) * T] = block(tile, at)
    even = m[PAR_Y] == 0
    side = 1 + m[PAR_X]
    down, up = block(0, side * 3), block(3, side * 3 + 2)
    p[...] = jnp.where(even, up, down)
    q[...] = jnp.where(even, down, up)


def blocks(o, tile, sides, dys):
    out = []
    for side in sides:
        at = (side * 3 + dys[0]) * T
        if not isinstance(side, int):
            at = pl.multiple_of(at, T)
        out.append(o[tile, :, pl.ds(at, len(dys) * T)])
    return out[0] if len(out) == 1 else jnp.concatenate(out, axis=1)


def store_edges(m, ref, p, q):
    even = m[PAR_Y] == 0
    p[:T] = ref[pl.ds(jnp.where(even, 3, 0), 1)].reshape(T, 2 * T)
    q[:T] = ref[pl.ds(jnp.where(even, 0, 3), 1)].reshape(T, 2 * T)


def join_kernel(m, own, other, v, p, q):
    first_col = m[COL] == 0
    v[:, :, :T] = jnp.where(first_col, own[...], other[...])
    v[:, :, T:] = jnp.where(first_col, other[...], own[...])
    store_edges(m, v, p, q)


def corner_kernel(m, q, out):
    out[:T] = q[...]
    out[T:] = q[: out.shape[0] - T]


def edge_kernel(m, b, a, a_out, b_out):
    at = jnp.where(m[PAR_Y] == 0, 3, 0)
    a_out[...] = a[at]
    b_out[...] = b[at]


def low_high(m, p, q):
    even = m[PAR_Y] == 0
    return jnp.where(even, q, p), jnp.where(even, p, q)


def product(o, tile, sides, at, sources):
    row = blocks(o, tile, sides, [place - tile for place in at])
    return dot(row, jnp.concatenate([x.reshape(len(at) * T, 2 * T) for x in sources], axis=0))


def outer_product(m, o, at_p, tiles):
    high = m[PAR_Y] == 0 if at_p else m[PAR_Y] != 0
    top = blocks(o, 3, (1, 2), (2,))
    bottom = blocks(o, 0, (1, 2), (0,))
    return dot(jnp.where(high, top, bottom), jnp.concatenate(tiles, axis=0)), high


def core_kernel(m, o, x, p, q, b, a, acc, ext):
    ext[0], ext[5] = low_high(m, p[...], q[...])
    ext[1:5] = x[...]
    for tile in range(4):
        total = product(o, tile, (0,), range(tile, tile + 3), [ext[tile : tile + 3]])
        at = [place for place in range(tile, tile + 3) if 1 <= place <= 4]
        acc[tile] = total + product(o, tile, (1, 2), at, [y[at[0] - 1 : at[-1]] for y in (a, b)])


def rim_kernel(m, o, a_edge, b_edge, b_corner, a_corner, acc, *rest, last):
    if last:
        before, h_p, h_q, out, p, q = rest
    else:
        out, p, q = rest
    at_p, high = outer_product(m, o, True, [a_edge[...], b_edge[...]])
    at_q, _ = outer_product(m, o, False, [a_corner[:T], b_corner[:T]])
    for tile in range(4):
        total = acc[tile]
        if tile == 0:
            total += jnp.where(high, at_q, at_p)
        if tile == 3:
            total += jnp.where(high, at_p, at_q)
        if last:
            out[tile] = (total - before[tile].astype(F32)).astype(BF)
        else:
            out[tile] = (0.5 * total).astype(BF)
    store_edges(m, out, p, q)
    if last:
        for to, block in ((p, h_p), (q, h_q)):
            to[T:, :T] = block[: T // 2]
            to[T:, T:] = block[T // 2 :]


def corr_kernel(m, o, s, corr, turned, acc):
    flat = s[...].reshape(4 * T, 2 * T)
    turned[...] = flat.T
    corr[...] = dot(turned[...], flat)
    for tile in range(4):
        total = 0.5 * dot(blocks(o, tile, (0,), (1,)), s[tile])
        if tile < 3:
            total += dot(blocks(o, tile, (0,), (2,)), s[tile + 1])
        acc[tile] = total


def places():
    shape = (2 * T, 2 * T)
    return lax.broadcasted_iota(jnp.int32, shape, 0), lax.broadcasted_iota(jnp.int32, shape, 1)


def gram_kernel(m, o, turned, p, q, right, acc, corr, mine, theirs):
    side = 1 + m[PAR_X]
    parts = []
    for tile in range(4):
        at = [place for place in range(tile, tile + 3) if 1 <= place <= 4]
        parts.append(acc[tile] + product(o, tile, (side,), at, [right[at[0] - 1 : at[-1]]]))
    even = m[PAR_Y] == 0
    above = jnp.where(even, p[:T], q[:T])
    parts[3] += product(o, 3, (0,), (5,), [above])
    high, low = split(jnp.concatenate(parts, axis=0))
    half = dot(turned[...], high) + dot(turned[...], low)
    for got, at in ((p, jnp.where(even, 3, 0)), (q, jnp.where(even, 0, 3))):
        block = jnp.concatenate([got[T:, :T], got[T:, T:]], axis=0)
        high, low = split(dot(block, right[at]))
        half += dot(got[:T], high, ((0,), (0,))) + dot(got[:T], low, ((0,), (0,)))
    coupling = half + half.T
    rows, cols = places()
    both = jnp.where(rows >= cols, corr[...], coupling)
    diagonal = jnp.sum(jnp.where(rows == cols, coupling, 0.0), axis=1, keepdims=True)
    first, second = pack(both[:T], diagonal[:T]), pack(both[T:], diagonal[T:])
    even = m[PAR_Y] == 0
    mine[:, 0, :] = jnp.where(even, first, second)
    theirs[:, 0, :] = jnp.where(even, second, first)


def pack(square, diagonal):
    lane = lax.broadcasted_iota(jnp.int32, (T // 2, T), 1)
    extra = jnp.where(lane == 0, diagonal[: T // 2], jnp.where(lane == 1, diagonal[T // 2 :], 0.0))
    return jnp.concatenate([square[: T // 2], square[T // 2 :], extra], axis=1)


def unpack(table):
    square = jnp.concatenate([table[:, : 2 * T], table[:, 2 * T : 4 * T]], axis=0)
    return square, jnp.concatenate([table[:, 4 * T : 4 * T + 1], table[:, 4 * T + 1 : 4 * T + 2]], axis=0)


def lower_part(e, rows, cols):
    return jnp.where(rows > cols, e, jnp.where(rows == cols, 0.5 * e, 0.0))


def squares(m, mine, theirs, spin):
    even = m[PAR_Y] == 0
    half = slice(spin * T // 2, (spin + 1) * T // 2)
    first, second = mine[half, 0, :], theirs[half, 0, :]
    top = unpack(jnp.where(even, first, second))
    bottom = unpack(jnp.where(even, second, first))
    both = jnp.concatenate([top[0], bottom[0]], axis=0)
    diagonal = jnp.concatenate([top[1], bottom[1]], axis=0)
    rows, cols = places()
    turned = both.T
    corr = jnp.where(rows >= cols, both, turned)
    return corr, jnp.where(rows < cols, both, jnp.where(rows == cols, diagonal, turned))


def stack_kernel(m, s, other, both):
    both[pl.ds(m[SPIN], 1)] = s[...][None]
    both[pl.ds(1 - m[SPIN], 1)] = other[...][None]


def final_kernel(m, mine, theirs, both, ritz, projected, x_ref, a_ref, k_ref):
    rows, cols = places()
    unit = (rows == cols).astype(F32)
    scales = []
    for spin in range(2):
        corr, k_ref[spin] = squares(m, mine, theirs, spin)
        on_diagonal = jnp.where(rows == cols, corr, 0.0)
        scale_row = 1.0 / jnp.sqrt(jnp.sum(on_diagonal, axis=0, keepdims=True))
        scale_col = 1.0 / jnp.sqrt(jnp.sum(on_diagonal, axis=1, keepdims=True))
        scaled = corr * scale_row * scale_col
        scales.append(scale_row)
        a_ref[spin] = scaled
        e = scaled - unit
        f = lower_part(e, rows, cols)
        f_half = f.astype(BF)
        fe = dot(f_half, e.astype(BF))
        e = dot((f + fe - e).astype(BF), f_half, ((1,), (1,))) - fe
        x = unit - f
        x_ref[spin] = x - dot(lower_part(e, rows, cols).astype(BF), x.astype(BF))

    def step(state):
        count, _, _ = state
        xs = [x_ref[spin] for spin in range(2)]
        es = [dot3(xs[spin], a_ref[spin]) for spin in range(2)]
        es = [dot3(es[spin], xs[spin], ((1,), (1,))) - unit for spin in range(2)]
        for spin in range(2):
            x_ref[spin] = xs[spin] - dot(lower_part(es[spin], rows, cols).astype(BF), xs[spin].astype(BF))
        return count + 1, jnp.sum(es[0] * es[0]), jnp.sum(es[1] * es[1])

    def more(state):
        count, *sizes = state
        largest = jnp.maximum(*sizes)
        return (count < 12) & (largest >= 4e-6) & (largest < 1e4)

    _, *sizes = lax.while_loop(more, step, (0, F32(1.0), F32(1.0)))

    for spin in range(2):

        @pl.when(jnp.logical_not(sizes[spin] < 4e-6))
        def _(spin=spin):
            x_ref[spin] = unit

            def eliminate(j, carry):
                row = a_ref[spin, pl.ds(j, 1), :]
                pivot = jnp.sum(jnp.where(cols[:1] == j, row, 0.0), axis=1, keepdims=True)
                a = a_ref[spin]
                column = jnp.sum(jnp.where(cols == j, a, 0.0), axis=1, keepdims=True)
                factor = jnp.where(rows[:, :1] > j, column / pivot, 0.0)
                x = x_ref[spin]
                x_row = x_ref[spin, pl.ds(j, 1), :]
                a_ref[spin] = a - factor * row
                x_ref[spin] = x - factor * x_row
                return carry

            lax.fori_loop(0, 2 * T, eliminate, 0)
            pivots = jnp.sum(jnp.where(rows == cols, a_ref[spin], 0.0), axis=1, keepdims=True)
            x_ref[spin] = x_ref[spin] / jnp.sqrt(pivots)

    first_col = m[COL] == 0
    for spin in range(2):
        x = x_ref[spin] * scales[spin]
        part = jnp.where(first_col, x[:T], x[T:])
        ritz[spin, 0] = dot(both[spin].reshape(4 * T, 2 * T), part.astype(BF), ((1,), (1,))).astype(BF).reshape(4, T, T)
        projected[spin] = dot3(dot3(x, k_ref[spin]), part, ((1,), (1,)))


def whole(shape):
    return pl.BlockSpec(shape, lambda i, m, n=len(shape): (0,) * n)


def call(kernel, m, arrays, outs, name, flops=0, specs=None, scratch=(), free=False):
    arrays = list(arrays)
    moved = 0 if free else sum(a.size * a.dtype.itemsize for a in [*arrays, *outs])
    return pl.pallas_call(
        kernel,
        out_shape=outs,
        grid_spec=pltpu.PrefetchScalarGridSpec(
            num_scalar_prefetch=1,
            grid=(1,),
            in_specs=specs or [whole(a.shape) for a in arrays],
            out_specs=[whole(o.shape) for o in outs],
            scratch_shapes=list(scratch),
        ),
        compiler_params=pltpu.CompilerParams(vmem_limit_bytes=32 * 1024 * 1024),
        cost_estimate=pl.CostEstimate(flops=2 * T * T * 2 * T * flops, bytes_accessed=moved, transcendentals=0),
        name=name,
    )(m, *arrays)


def table(neighbour_index, block_count):
    gx, gy, col = (lax.axis_index(a) for a in AXES)
    spin = col ^ ((gx >> 1) & 1)
    toward = jnp.where(gx % 2 == 0, 1, -1)
    dx = jnp.stack([jnp.zeros_like(toward), toward, -toward])
    codes = (dx[:, None] + 1) * 3 + jnp.arange(3, dtype=jnp.int32)[None, :]
    slots = jnp.arange(NB, dtype=jnp.int32)
    index, count = neighbour_index[0], block_count[0]
    match = (index[:, None, None, :] == codes[None, :, :, None]) & (
        slots < count[:, None, None, None]
    )
    found = jnp.sum(jnp.where(match, slots + 1, 0), axis=-1) - 1
    scalars = jnp.stack([spin, col, gy % 2, gx % 2])
    return spin, col, jnp.concatenate([found.reshape(-1), scalars]).astype(jnp.int32)


def shaped(shape, dtype):
    return jax.ShapeDtypeStruct(shape, dtype)


def per_device(start_block, hamiltonian, neighbour_index, block_count):
    sizes = tuple(lax.axis_size(a) for a in AXES)
    members = sizes[0] * sizes[1]
    block, full = (4, T, 2 * T), (2 * T, 2 * T)
    spin, col, m = table(neighbour_index, block_count)

    other = swap_col(sizes, lax.dynamic_index_in_dim(start_block, 1 - spin, 0, keepdims=False)[0])
    own = lax.dynamic_index_in_dim(start_block, spin, 0, keepdims=False)[0]
    spin_block = pl.BlockSpec((1,) + hamiltonian.shape[1:], lambda i, m: (m[SPIN], 0, 0, 0, 0, 0))
    corner = shaped((T, T), BF)
    o, h_p, h_q = call(
        order_kernel, m, [hamiltonian], [shaped((4, T, NB * T), BF), corner, corner], "order", specs=[spin_block]
    )
    tile = shaped((T, 2 * T), BF)
    ext = pltpu.VMEM((6, T, 2 * T), BF)
    other, o = lax.optimization_barrier((other, o))
    outs = [shaped(block, BF), tile, tile]
    v, p, q = call(join_kernel, m, [own, other], outs, "join")

    def apply_ham(x, p, q, more, outs):
        p, q = swap(sizes, p, 0, 1), swap(sizes, q, 0, 2)
        b, a = swap(sizes, x, 2, 0), swap(sizes, x, 1, 0)
        (corner,) = call(corner_kernel, m, [q], [shaped((T + 16, 2 * T), BF)], "corner", 300)
        b_corner, a_corner = swap(sizes, corner, 2, 0), swap(sizes, corner, 1, 0)
        a_edge, b_edge = call(edge_kernel, m, [b, a], [tile, tile], "edge", free=True)
        a_edge, b_edge = swap(sizes, a_edge, 0, 1), swap(sizes, b_edge, 0, 1)
        (acc,) = call(
            core_kernel, m, [o, x, p, q, b, a], [shaped(block, F32)], "core", free=True, scratch=[ext]
        )
        kernel = functools.partial(rim_kernel, last=len(more) > 0)
        return call(kernel, m, [o, a_edge, b_edge, b_corner, a_corner, acc, *more], outs, "rim", 2)

    first, p, q = apply_ham(v, p, q, [], outs)
    longer = shaped((3 * T // 2, 2 * T), BF)
    second, p, q = apply_ham(first, p, q, [v, h_p, h_q], [shaped(block, BF), longer, longer])

    right = shift(sizes, second, -1, 0)
    p, q = swap(sizes, p, 0, 1), swap(sizes, q, 0, 2)
    corr, turned, acc = call(
        corr_kernel, m, [o, second], [shaped(full, F32), shaped((2 * T, 4 * T), BF), shaped(block, F32)], "corr", 15
    )
    piece = shaped((members // 2, 1, 5 * T), F32)
    mine, theirs = call(
        gram_kernel, m, [o, turned, p, q, right, acc, corr], [piece, piece], "gram", 30
    )

    rows = members * second.shape[0] * second.shape[1]
    partial = mine + swap(sizes, theirs, 0, 1)
    (both,) = call(stack_kernel, m, [second, swap_col(sizes, second)], [shaped((2, *block), BF)], "stack", 200)
    total = exchange(sizes, partial, False)
    total, both = lax.optimization_barrier((total, both))
    total = total.sum(axis=0, keepdims=True) / rows
    mine = exchange(sizes, jnp.broadcast_to(total, (members, 1, 5 * T)), True)
    theirs = swap(sizes, mine, 0, 1)
    squared = pltpu.VMEM((2, *full), F32)
    return tuple(
        call(
            final_kernel, m, [mine, theirs, both],
            [shaped((2, 1, 4, T, T), BF), shaped((2, 2 * T, T), F32)], "final", 200,
            scratch=[squared, squared, squared],
        )
    )


def solution(mesh):
    return jax.shard_map(
        per_device,
        mesh=mesh,
        in_specs=(
            P(None, "gx", "gy", None, "col"),
            P(None, "gx", "gy", None, None, None),
            P("gx", "gy", None),
            P("gx", "gy"),
        ),
        out_specs=(P(None, "gx", "gy", None, "col"), P(None, None, "col")),
        check_vma=False,
    )
```
